32 devices in a mesh: tower: 2 (over core), rows: 8 (over z, x), mp: 2 (over y).
Axes of the slice: x: 2, y: 2, z: 4, core: 2. Of those that a mesh axis runs over, the one named last changes fastest.
Arguments:
- tokens: bfloat16 [2, 8, 512, 768], P('tower', 'rows'), may hold values from -24 to 24
- segment_ids: int32 [2, 8, 512], P('tower', 'rows'), may hold values from 0 to 7, never falling along the last dimension, each value on 1 to 160 neighbouring positions
- pair_ids: int32 [64], replicated, may hold values from 0 to 63, each once
- bucket_ids: int32 [1023], replicated, may hold values from 0 to 31
- attn_gain: float32 [768], replicated, may hold values from 0.5 to 1.5
- query_weight: bfloat16 [768, 768], P(None, 'mp'), may hold values from -0.109375 to 0.109375
- key_weight: bfloat16 [768, 768], P(None, 'mp'), may hold values from -0.109375 to 0.109375
- value_weight: bfloat16 [768, 768], P(None, 'mp'), may hold values from -0.21875 to 0.21875
- output_weight: bfloat16 [768, 768], P('mp'), may hold values from -1.25 to 1.25
- bias_table: float32 [32, 12], P(None, 'mp'), may hold values from -4 to 4
- ff_gain: float32 [768], replicated, may hold values from 0.5 to 1.5
- up_weight: bfloat16 [768, 3072], P(None, 'mp'), may hold values from -0.21875 to 0.21875
- down_weight: bfloat16 [3072, 768], P('mp'), may hold values from -0.109375 to 0.109375
- final_gain: float32 [768], replicated, may hold values from 0.5 to 1.5
- proj_weight: bfloat16 [768, 768], replicated, may hold values from -6 to 6
Outputs:
- loss: float32 [], replicated
- tokens_grad: float32 [2, 8, 512, 768], P('tower', 'rows')
- attn_gain_grad: float32 [768], P(('tower', 'rows'))
- query_grad: float32 [768, 768], P(('tower', 'rows'), 'mp')
- key_grad: float32 [768, 768], P(('tower', 'rows'), 'mp')
- value_grad: float32 [768, 768], P(('tower', 'rows'), 'mp')
- output_grad: float32 [768, 768], P('mp', ('tower', 'rows'))
- bias_grad: float32 [32, 12], P(None, 'mp')
- ff_gain_grad: float32 [768], P(('tower', 'rows'))
- up_grad: float32 [768, 3072], P(('tower', 'rows'), 'mp')
- down_grad: float32 [3072, 768], P('mp', ('tower', 'rows'))
- final_gain_grad: float32 [768], P(('tower', 'rows'))
- proj_grad: float32 [768, 768], P(('tower', 'rows'))
The draws below stay inside these ranges and needn't reach their ends.
Inputs may be any that keep to these rules, and one draw needn't show every extreme that they name: `segment_ids`: in each row the sentence numbers never fall and every one of the 8 sentences holds 1 to 160 slots, one exactly 160. A permutation; query sentence a of the query tower is paired with document sentence pair_ids[a].
All inputs are finite; a program needn't handle non-finite values.
Results may differ from the reference program's by a relative error of at most 0.022.
Values may be sent and summed in bfloat16 or wider, within the bound.
No kernel may reach another device: no remote copies, remote signals or barrier semaphores. Data moves between devices by JAX's collectives and lax.ppermute only.
A program may use at most 192 MiB of HBM per device.

```python
import math
from functools import partial
import jax
import jax.numpy as jnp
import numpy as np
from jax import lax

D = 768
HEADS = 12
HEAD_DIM = 64
FF = 3072
BUCKETS = 32
ROW_LEN = 512
SEGS_ROW = 8
SEG_MOST = 160
TOWERS = 2
ROWS = 8
NSEG = 64


def draw_tokens(key, part):
    key = jax.random.fold_in(key, 11)
    full_shape = (TOWERS, ROWS, ROW_LEN, D)
    values = jax.random.truncated_normal(key, -6.0, 6.0, full_shape, jnp.float32)
    return values.astype(jnp.bfloat16)


def draw_proj_weight(key, part):
    key = jax.random.fold_in(key, 23)
    values = jax.random.truncated_normal(key, -4.0, 4.0, (D, D), jnp.float32) / jnp.sqrt(jnp.float32(D))
    return values.astype(jnp.bfloat16)


def touch_ends(entries, key, low, largest):
    dims = entries.shape
    index_at = [jax.random.randint(jax.random.fold_in(key, axis), (), 0, dims[axis]) for axis in range(len(dims))]
    entries = entries.at[tuple(index_at)].set(low)
    longest = dims.index(max(dims))
    index_at[longest] = (index_at[longest] + 1) % dims[longest]
    return entries.at[tuple(index_at)].set(largest)


def levels(key, shape, pieces, least, high):
    level, own = 1.0, jax.random.fold_in(key, 6)
    for dim, blocks in pieces:
        draws = jnp.exp(jax.random.uniform(jax.random.fold_in(own, dim), (blocks,), jnp.float32, least / len(pieces), high / len(pieces)))
        level = level * jnp.repeat(draws, shape[dim] // blocks).reshape([-1 if axis == dim else 1 for axis in range(len(shape))])
    return level


def length_profile(count, total, limit, slope):
    weights = [(1 << 20) // math.isqrt(grade ** slope) + 1 for grade in range(2, count + 1)]
    surplus, holding = total - limit - (count - 1), [1] * (count - 1)
    while surplus > 0:
        free = [i for i in range(count - 1) if holding[i] < limit]
        whole, remaining = sum([weights[i] for i in free]), surplus
        for i in free:
            addition = min(limit - holding[i], max(1, remaining * weights[i] // whole), surplus)
            holding[i] = holding[i] + addition
            surplus = surplus - addition
    return np.array([limit] + holding)


def uneven_parts(key, count, total, reach, skew):
    if count == 2:
        one = jax.random.randint(key, (), max(1, total - reach), min(reach, total - 1) + 1)
        return jnp.stack([one, total - one])
    tallies = jnp.asarray(length_profile(count, total, reach, skew), jnp.int32)
    twos = (count - 1) // 2
    donor, sink = tallies[1:1 + 2 * twos:2], tallies[2:2 + 2 * twos:2]
    margin = jnp.minimum(donor - 1, reach - sink)
    moved = jax.random.randint(jax.random.fold_in(key, 1), (twos,), 0, 1 << 20) % (margin + 1)
    tallies = tallies.at[1:1 + 2 * twos:2].set(donor - moved).at[2:2 + 2 * twos:2].set(sink + moved)
    return tallies[jax.random.permutation(jax.random.fold_in(key, 2), count)]


def bell_draw(rng, dims, width, most, cuts=(), held_as=jnp.bfloat16):
    values = jax.random.normal(rng, dims, jnp.float32) * width
    if len(cuts) > 0:
        values = levels(rng, dims, cuts, -0.22, 0.18) * values
    return jnp.clip(values, min=-most, max=most).astype(held_as)


def setup_inputs(seed: int = 0) -> dict:
    seeds = jax.random.split(jax.random.key(seed), 16)
    return {
        "tokens": draw_tokens(jax.random.fold_in(seeds[15], 71), 0),
        "segment_ids": jax.vmap(lambda own: jnp.searchsorted(jnp.cumsum(uneven_parts(own, SEGS_ROW, ROW_LEN, SEG_MOST, 1)), jnp.arange(ROW_LEN), side="right"))(jax.random.split(seeds[1], TOWERS * ROWS)).reshape((TOWERS, ROWS, ROW_LEN)).astype(jnp.int32),
        "pair_ids": jax.random.permutation(seeds[2], NSEG).astype(jnp.int32),
        "bucket_ids": touch_ends(jax.random.randint(seeds[3], (2 * ROW_LEN - 1,), 0, BUCKETS), jax.random.fold_in(seeds[3], 1), 0, BUCKETS - 1).astype(jnp.int32),
        "attn_gain": jnp.clip(1.0 + 0.1 * jax.random.normal(seeds[4], (D,), jnp.float32), 0.5, 1.5),
        "query_weight": bell_draw(seeds[5], (D, HEADS * HEAD_DIM), (4 * D) ** -0.5, 0.109375, ((1, 2),)),
        "key_weight": bell_draw(seeds[6], (D, HEADS * HEAD_DIM), (4 * D) ** -0.5, 0.109375, ((1, 2),)),
        "value_weight": bell_draw(seeds[7], (D, HEADS * HEAD_DIM), D ** -0.5, 0.21875, ((1, 2),)),
        "output_weight": bell_draw(seeds[8], (HEADS * HEAD_DIM, D), (HEADS * HEAD_DIM // 32) ** -0.5, 1.25, ((0, 2),)),
        "bias_table": bell_draw(seeds[9], (BUCKETS, HEADS), 1.0, 4.0, ((1, 2),), jnp.float32),
        "ff_gain": jnp.clip(1.0 + 0.1 * jax.random.normal(seeds[10], (D,), jnp.float32), 0.5, 1.5),
        "up_weight": bell_draw(seeds[11], (D, FF), D ** -0.5, 0.21875, ((1, 2),)),
        "down_weight": bell_draw(seeds[12], (FF, D), FF ** -0.5, 0.109375, ((0, 2),)),
        "final_gain": jnp.clip(1.0 + 0.1 * jax.random.normal(seeds[13], (D,), jnp.float32), 0.5, 1.5),
        "proj_weight": draw_proj_weight(jax.random.fold_in(seeds[15], 71), 0),
    }


@jax.custom_vjp
def low(v):
    return lax.optimization_barrier(v.astype(jnp.bfloat16)).astype(jnp.float32)

@jax.custom_vjp
def low_back(v):
    return v

def low_keep(v):
    return (low(v), None)

def low_pass(kept, grad):
    return (grad,)

def back_keep(v):
    return (v, None)

def back_low(kept, grad):
    return (low(grad),)
low.defvjp(low_keep, low_pass)
low_back.defvjp(back_keep, back_low)
eps = 1e-06
logit_scale = 50.0
highest = lax.Precision.HIGHEST

def matmul(left_side, right_side):
    return jnp.dot(left_side, right_side, precision=highest)

def rms_norm(values, scale_gain):
    return values * lax.rsqrt(lax.optimization_barrier(jnp.mean(values * values, -1, keepdims=True)) + eps) * scale_gain

def attend_block(block_rows, begin_at, queries, key_heads, values, rel_bias, segments):
    length = key_heads.shape[0]
    query_block = lax.dynamic_slice_in_dim(queries, begin_at, block_rows, 0)
    seg_block = lax.dynamic_slice_in_dim(segments, begin_at, block_rows, 0)
    offsets = (lax.broadcasted_iota(jnp.int32, (block_rows, length), 1) - lax.broadcasted_iota(jnp.int32, (block_rows, length), 0) - begin_at + (length - 1)).astype(jnp.int32)
    bias_block = jnp.transpose(jnp.take(rel_bias, offsets, axis=0), (2, 0, 1))
    scores = jnp.einsum('ihd,jhd->hij', query_block, key_heads, precision=highest) + bias_block
    scores = low_back(scores)
    same_seg = seg_block[:, None] == segments[None, :]
    scores = jnp.where(same_seg[None], scores, -1e+30)
    log_norm = jax.nn.logsumexp(scores, -1, keepdims=True)
    attn_probs = low(jnp.exp(scores - log_norm))
    return jnp.einsum('hij,jhd->ihd', attn_probs, values, precision=highest)

def encode_row(row_tokens, segments, rel_bias, attn_gain, query_weight, key_weight, value_weight, output_weight, ff_gain, up_weight, down_weight, final_gain, proj_weight):
    normed = low(rms_norm(row_tokens, attn_gain))
    queries = low_back(low(matmul(normed, query_weight))).reshape(ROW_LEN, HEADS, HEAD_DIM)
    key_heads = low_back(low(matmul(normed, key_weight))).reshape(ROW_LEN, HEADS, HEAD_DIM)
    values = low_back(low(matmul(normed, value_weight))).reshape(ROW_LEN, HEADS, HEAD_DIM)
    block_rows = min(512, ROW_LEN)
    starts = (jnp.arange(ROW_LEN // block_rows) * block_rows).astype(jnp.int32)
    attend = jax.checkpoint(partial(attend_block, block_rows))
    mixes = lax.map(lambda begin_at: attend(begin_at, queries, key_heads, values, rel_bias, segments), starts)
    attn_mix = low_back(low(mixes.reshape(ROW_LEN, HEADS * HEAD_DIM)))
    hidden = row_tokens + low_back(matmul(attn_mix, output_weight))
    normed_two = low(rms_norm(hidden, ff_gain))
    active = low(jax.nn.gelu(low_back(matmul(normed_two, up_weight)), approximate=False))
    hidden = hidden + low_back(matmul(active, down_weight))
    final_out = rms_norm(hidden, final_gain)
    member = (segments[None, :] == jnp.arange(SEGS_ROW)[:, None]).astype(jnp.float32)
    pooled = matmul(member, final_out) / lax.optimization_barrier(jnp.sum(member, -1, keepdims=True))
    embedding = low_back(matmul(low(pooled), proj_weight))
    return low(embedding * lax.rsqrt(lax.optimization_barrier(jnp.sum(embedding * embedding, -1, keepdims=True)) + eps))

def forward(segment_ids, pair_ids, bucket_ids, tokens, attn_gain, query_weight, key_weight, value_weight, output_weight, bias_table, ff_gain, up_weight, down_weight, final_gain, proj_weight):
    bucket_hot = (bucket_ids[:, None] == jnp.arange(BUCKETS)[None, :]).astype(jnp.float32)
    rel_bias = matmul(bucket_hot, bias_table)
    encode = jax.checkpoint(encode_row)

    def encode_item(row_item):
        return encode(row_item[0], row_item[1], rel_bias, attn_gain, query_weight, key_weight, value_weight, output_weight, ff_gain, up_weight, down_weight, final_gain, proj_weight)
    flat_tokens = tokens.reshape(TOWERS * ROWS, ROW_LEN, D)
    flat_segments = segment_ids.reshape(TOWERS * ROWS, ROW_LEN)
    unit_rows = lax.map(encode_item, (flat_tokens, flat_segments))
    unit_rows = unit_rows.reshape(TOWERS, NSEG, D)
    query_side = unit_rows[0]
    doc_side = unit_rows[1]
    logits = low_back(logit_scale * matmul(query_side, doc_side.T))
    positive = (jnp.arange(NSEG)[None, :] == pair_ids[:, None]).astype(jnp.float32)
    row_terms = jax.nn.logsumexp(logits, 1) - lax.optimization_barrier(jnp.sum(logits * positive, 1))
    col_terms = jax.nn.logsumexp(logits, 0) - lax.optimization_barrier(jnp.sum(logits * positive, 0))
    return 0.5 * (jnp.mean(row_terms) + jnp.mean(col_terms))

def reference(tokens, segment_ids, pair_ids, bucket_ids, attn_gain, query_weight, key_weight, value_weight, output_weight, bias_table, ff_gain, up_weight, down_weight, final_gain, proj_weight):
    floats = (tokens.astype(jnp.float32), attn_gain.astype(jnp.float32), query_weight.astype(jnp.float32), key_weight.astype(jnp.float32), value_weight.astype(jnp.float32), output_weight.astype(jnp.float32), bias_table.astype(jnp.float32), ff_gain.astype(jnp.float32), up_weight.astype(jnp.float32), down_weight.astype(jnp.float32), final_gain.astype(jnp.float32), proj_weight.astype(jnp.float32))
    loss_value, pullback = jax.vjp(partial(forward, segment_ids, pair_ids, bucket_ids), *floats)
    gradients = pullback(jnp.ones((), jnp.float32))
    return (loss_value, gradients[0], gradients[1], gradients[2], gradients[3], gradients[4], gradients[5], gradients[6], gradients[7], gradients[8], gradients[9], gradients[10], gradients[11])
```

```python
import functools

import jax
import jax.numpy as jnp
from jax import lax
from jax.experimental import pallas as pl
from jax.experimental.pallas import tpu as pltpu
from jax.sharding import PartitionSpec as P

SEGS_ROW = 8
BLOCK = 128

eps = 1e-06
logit_scale = 50.0
highest = lax.Precision.HIGHEST
f32 = jnp.float32
bf16 = jnp.bfloat16


def inv_rms(values):
    return lax.rsqrt(jnp.mean(values * values, -1, keepdims=True) + eps)


def dot_nn(a, b):
    return lax.dot_general(a, b, (((1,), (0,)), ((), ())), preferred_element_type=f32)


def dot_nt(a, b):
    return lax.dot_general(a, b, (((1,), (1,)), ((), ())), preferred_element_type=f32)


def dot_tn(a, b):
    return lax.dot_general(a, b, (((0,), (0,)), ((), ())), preferred_element_type=f32)


def gelu_parts(values):
    size = jnp.abs(values)
    bell = jnp.exp(-0.5 * values * values)
    t = 1.0 / (1.0 + (0.3275911 * 0.7071067811865476) * size)
    poly = t * (
        0.127414796
        + t * (-0.142248368 + t * (0.7107068705 + t * (-0.7265760135 + t * 0.5307027145)))
    )
    tail = poly * bell
    return bell, jnp.where(values >= 0, 1.0 - tail, tail)


def key_range(block, blocks):
    return max(0, block - 2), min(blocks, block + 3)


def attend_kernel(
    tok_ref, gain_ref, wq_ref, wk_ref, wv_ref, table_ref, ids_ref, seg_ref,
    n1_ref, q_ref, k_ref, v_ref, probs_ref, mix_ref,
    rel_ref, mask_ref, skew_ref,
):
    length = tok_ref.shape[0]
    blocks = length // BLOCK
    buckets = table_ref.shape[0]
    pairs = q_ref.shape[1] // BLOCK
    span = rel_ref.shape[1]
    for b in range(blocks):
        rows = slice(b * BLOCK, (b + 1) * BLOCK)
        x = tok_ref[rows, :].astype(f32)
        n1_ref[rows, :] = (x * inv_rms(x) * gain_ref[...]).astype(bf16)
    n1 = n1_ref[...]
    q_ref[...] = dot_nn(n1, wq_ref[...]).astype(bf16)
    k_ref[...] = dot_nn(n1, wk_ref[...]).astype(bf16)
    v_ref[...] = dot_nn(n1, wv_ref[...]).astype(bf16)
    hot = (lax.broadcasted_iota(jnp.int32, (buckets, span), 0) == ids_ref[...]).astype(f32)
    rel_ref[0 : table_ref.shape[1], :] = lax.dot_general(
        table_ref[...], hot, (((0,), (0,)), ((), ())), precision=highest, preferred_element_type=f32
    )
    seg_row = seg_ref[...].astype(f32)
    for b in range(blocks):
        own = jnp.broadcast_to(seg_row[:, b * BLOCK : (b + 1) * BLOCK], (BLOCK, BLOCK)).T
        for c in range(blocks):
            other = jnp.broadcast_to(seg_row[:, c * BLOCK : (c + 1) * BLOCK], (BLOCK, BLOCK))
            mask_ref[b * BLOCK : (b + 1) * BLOCK, c * BLOCK : (c + 1) * BLOCK] = jnp.where(
                own == other, 0.0, -1e30
            )
    low_lanes = lax.broadcasted_iota(jnp.int32, (BLOCK, BLOCK), 1) < BLOCK // 2
    zero = jnp.zeros((BLOCK, BLOCK), bf16)

    @pl.loop(0, pairs)
    def _(pair):
        lanes = pl.ds(pl.multiple_of(pair * BLOCK, BLOCK), BLOCK)
        for h in range(2):
            row = jnp.broadcast_to(rel_ref[pl.ds(pair * 2 + h, 1), :], (BLOCK, span))
            skew_ref[h] = pltpu.roll(row, span - (BLOCK - 1), 1, stride=1, stride_axis=0)
        for b in range(blocks):
            first, last = key_range(b, blocks)
            rows = slice(b * BLOCK, (b + 1) * BLOCK)
            keys = slice(first * BLOCK, last * BLOCK)
            shift = length - BLOCK - b * BLOCK
            q_pair = q_ref[rows, lanes]
            k_pair = k_ref[keys, lanes]
            v_pair = v_ref[keys, lanes]
            mixes = []
            for h in range(2):
                q_one = jnp.where(low_lanes if h == 0 else ~low_lanes, q_pair, zero)
                scores = (
                    dot_nt(q_one, k_pair)
                    + skew_ref[h, :, shift + first * BLOCK : shift + last * BLOCK]
                    + mask_ref[rows, keys]
                )
                most = jnp.max(scores, -1, keepdims=True)
                raised = jnp.exp(scores - most)
                probs = (raised * (1.0 / jnp.sum(raised, -1, keepdims=True))).astype(bf16)
                if first > 0:
                    probs_ref[pair * 2 + h, rows, 0 : first * BLOCK] = jnp.zeros((BLOCK, first * BLOCK), bf16)
                if last < blocks:
                    probs_ref[pair * 2 + h, rows, last * BLOCK :] = jnp.zeros(
                        (BLOCK, length - last * BLOCK), bf16
                    )
                probs_ref[pair * 2 + h, rows, keys] = probs
                mixes.append(dot_nn(probs, v_pair))
            mix_ref[rows, lanes] = jnp.where(low_lanes, mixes[0], mixes[1]).astype(bf16)


def attend_back_kernel(
    q_ref, k_ref, v_ref, probs_ref, mixg_ref, ids_ref,
    dq_ref, dk_ref, dv_ref, biasg_ref,
    ds_ref, skew_ref, rel_ref,
):
    length = q_ref.shape[0]
    blocks = length // BLOCK
    pairs = q_ref.shape[1] // BLOCK
    span = rel_ref.shape[1]
    low_lanes = lax.broadcasted_iota(jnp.int32, (BLOCK, BLOCK), 1) < BLOCK // 2
    low_all = lax.broadcasted_iota(jnp.int32, (length, BLOCK), 1) < BLOCK // 2
    zero = jnp.zeros((BLOCK, BLOCK), bf16)
    rel_ref[...] = jnp.zeros_like(rel_ref)

    @pl.loop(0, pairs)
    def _(pair):
        lanes = pl.ds(pl.multiple_of(pair * BLOCK, BLOCK), BLOCK)
        skew_ref[...] = jnp.zeros_like(skew_ref)
        for b in range(blocks):
            first, last = key_range(b, blocks)
            rows = slice(b * BLOCK, (b + 1) * BLOCK)
            keys = slice(first * BLOCK, last * BLOCK)
            shift = length - BLOCK - b * BLOCK
            g_pair = mixg_ref[rows, lanes]
            k_pair = k_ref[keys, lanes]
            v_pair = v_ref[keys, lanes]
            parts = []
            for h in range(2):
                g_one = jnp.where(low_lanes if h == 0 else ~low_lanes, g_pair, zero)
                probs = probs_ref[pair * 2 + h, rows, keys].astype(f32)
                dp = dot_nt(g_one, v_pair)
                weighted = probs * dp
                ds = weighted - probs * jnp.sum(weighted, -1, keepdims=True)
                ds_low = ds.astype(bf16)
                if first > 0:
                    ds_ref[h, rows, 0 : first * BLOCK] = jnp.zeros((BLOCK, first * BLOCK), bf16)
                if last < blocks:
                    ds_ref[h, rows, last * BLOCK :] = jnp.zeros((BLOCK, length - last * BLOCK), bf16)
                ds_ref[h, rows, keys] = ds_low
                skew_ref[h, :, shift + first * BLOCK : shift + last * BLOCK] += ds
                parts.append(dot_nn(ds_low, k_pair))
            dq_ref[rows, lanes] = jnp.where(low_lanes, parts[0], parts[1]).astype(bf16)
        q_pair = q_ref[:, lanes]
        g_pair = mixg_ref[:, lanes]
        dk_ref[:, lanes] = jnp.where(
            low_all, dot_tn(ds_ref[0], q_pair), dot_tn(ds_ref[1], q_pair)
        ).astype(bf16)
        dv_ref[:, lanes] = jnp.where(
            low_all,
            dot_tn(probs_ref[pair * 2], g_pair),
            dot_tn(probs_ref[pair * 2 + 1], g_pair),
        ).astype(bf16)
        for h in range(2):
            tiles = skew_ref[h, BLOCK - 8 :, :]
            for r in range(0, BLOCK - 8, 8):
                tiles += pltpu.roll(skew_ref[h, r : r + 8, :], BLOCK - 8 - r, 1)
            line = tiles[7:8, :]
            for r in range(7):
                line += pltpu.roll(tiles[r : r + 1, :], 7 - r, 1)
            rel_ref[pl.ds(pair * 2 + h, 1), :] = line

    hot = (lax.broadcasted_iota(jnp.int32, (biasg_ref.shape[0], span), 0) == ids_ref[...]).astype(f32)
    total = lax.dot_general(
        hot, rel_ref[...], (((1,), (1,)), ((), ())), precision=highest, preferred_element_type=f32
    )
    biasg_ref[...] = total[:, : biasg_ref.shape[1]]


def whole(kernel, out_shapes, scratch, *args):
    return pl.pallas_call(
        kernel,
        out_shape=out_shapes,
        in_specs=[pl.BlockSpec(memory_space=pltpu.VMEM)] * len(args),
        out_specs=jax.tree.map(lambda _: pl.BlockSpec(memory_space=pltpu.VMEM), out_shapes),
        scratch_shapes=scratch,
        compiler_params=pltpu.CompilerParams(vmem_limit_bytes=56 * 1024 * 1024),
    )(*args)


def swap(values, axis, bit=1):
    count = lax.axis_size(axis)
    return lax.ppermute(values, axis, [(i, i ^ bit) for i in range(count)])


def mp_sum(part):
    own = lax.optimization_barrier(part.astype(bf16))
    return own.astype(f32) + swap(own, "mp").astype(f32)


def gather_all(values):
    rows_index = lax.axis_index("rows")
    out = values[None]
    bit = 1
    while bit < lax.axis_size("rows"):
        other = swap(out, "rows", bit)
        is_high = (rows_index & bit) > 0
        out = jnp.concatenate(
            [jnp.where(is_high, other, out), jnp.where(is_high, out, other)], 0
        )
        bit *= 2
    other = swap(out, "tower")
    is_high = lax.axis_index("tower") > 0
    return jnp.concatenate([jnp.where(is_high, other, out), jnp.where(is_high, out, other)], 0)


def rows_scatter(cur, shard):
    rows_index = lax.axis_index("rows")
    bit = 1
    while bit < lax.axis_size("rows"):
        columns = cur.shape[1]
        view = cur.reshape(-1, 2, shard, columns)
        own_bit = (rows_index & bit) // bit
        keep = lax.dynamic_index_in_dim(view, own_bit, 1, False).reshape(-1, columns)
        send = lax.dynamic_index_in_dim(view, 1 - own_bit, 1, False).reshape(-1, columns)
        cur = keep.astype(f32) + swap(send, "rows", bit).astype(f32)
        bit *= 2
        if bit < lax.axis_size("rows"):
            cur = lax.optimization_barrier(cur.astype(bf16))
    return cur


def weight_scatter(left, right):
    tower_index = lax.axis_index("tower")
    half = left.shape[1] // 2
    other_left = lax.dynamic_slice_in_dim(left, (1 - tower_index) * half, half, 1)
    own_left = lax.dynamic_slice_in_dim(left, tower_index * half, half, 1)
    received = swap(dot_tn(other_left, right).astype(bf16), "tower")
    total = (dot_tn(own_left, right) + received.astype(f32)).astype(bf16)
    return rows_scatter(total, half // lax.axis_size("rows"))


def per_device(
    tokens,
    segment_ids,
    pair_ids,
    bucket_ids,
    attn_gain,
    query_weight,
    key_weight,
    value_weight,
    output_weight,
    bias_table,
    ff_gain,
    up_weight,
    down_weight,
    final_gain,
    proj_weight,
):
    length = tokens.shape[2]
    width = tokens.shape[3]
    inner = query_weight.shape[1]
    head_count = bias_table.shape[1]
    bucket_count = bias_table.shape[0]
    total_segs = pair_ids.shape[0]
    span = 2 * length
    tower_index = lax.axis_index("tower")
    device_index = tower_index * lax.axis_size("rows") + lax.axis_index("rows")
    shard = width // (2 * lax.axis_size("rows"))

    token_row = tokens.reshape(length, width)
    residual = token_row.astype(f32)
    segments = segment_ids.reshape(1, length)
    ids_row = jnp.pad(bucket_ids, (0, 1), constant_values=-1).reshape(1, span)

    def struct(shape, dtype):
        return jax.ShapeDtypeStruct(shape, dtype)

    normed_one, query, key, value, probs, attn_mix = whole(
        attend_kernel,
        (
            struct((length, width), bf16),
            struct((length, inner), bf16),
            struct((length, inner), bf16),
            struct((length, inner), bf16),
            struct((head_count, length, length), bf16),
            struct((length, inner), bf16),
        ),
        [
            pltpu.VMEM((8, span), f32),
            pltpu.VMEM((length, length), f32),
            pltpu.VMEM((2, BLOCK, span), f32),
        ],
        token_row,
        attn_gain.reshape(1, width),
        query_weight,
        key_weight,
        value_weight,
        bias_table,
        ids_row,
        segments,
    )
    hidden_one = residual + mp_sum(dot_nn(attn_mix, output_weight))
    inv_two = inv_rms(hidden_one)
    normed_two = (hidden_one * inv_two * ff_gain).astype(bf16)
    up_out = dot_nn(normed_two, up_weight)
    bell, below = gelu_parts(up_out)
    active = (up_out * below).astype(bf16)
    slope = below + up_out * bell * 0.3989422804014327
    hidden_two = hidden_one + mp_sum(dot_nn(active, down_weight))
    inv_final = inv_rms(hidden_two)
    final_out = hidden_two * inv_final * final_gain
    member = (segments == lax.broadcasted_iota(jnp.int32, (SEGS_ROW, 1), 0)).astype(f32)
    counts = jnp.sum(member, -1, keepdims=True)
    pooled = jnp.dot(member, final_out, precision=highest) / counts
    all_pooled = gather_all(pooled.astype(bf16)).reshape(2 * total_segs, width)

    embedding = dot_nn(all_pooled, proj_weight)
    inv_unit = lax.rsqrt(jnp.sum(embedding * embedding, -1, keepdims=True) + eps)
    unit_vec = embedding * inv_unit
    unit_low = unit_vec.astype(bf16)
    query_unit, doc_unit = unit_low[:total_segs], unit_low[total_segs:]
    logits = logit_scale * dot_nt(query_unit, doc_unit)
    positive = (
        pair_ids[:, None] == lax.broadcasted_iota(jnp.int32, (1, total_segs), 1)
    ).astype(f32)
    row_norm = jax.nn.logsumexp(logits, 1, keepdims=True)
    col_norm = jax.nn.logsumexp(logits, 0, keepdims=True)
    half_share = 0.5 / total_segs
    loss_value = half_share * (
        jnp.sum(row_norm) + jnp.sum(col_norm) - 2.0 * jnp.sum(logits * positive)
    )
    logit_grad = (
        half_share * (jnp.exp(logits - row_norm) + jnp.exp(logits - col_norm) - 2.0 * positive)
    ).astype(bf16)
    unit_grad = logit_scale * jnp.concatenate(
        [dot_nn(logit_grad, doc_unit), dot_tn(logit_grad, query_unit)], 0
    )
    embed_grad = (
        (unit_grad - unit_vec * jnp.sum(unit_vec * unit_grad, -1, keepdims=True)) * inv_unit
    ).astype(bf16)
    own_embed = lax.dynamic_slice_in_dim(embed_grad, device_index * SEGS_ROW, SEGS_ROW, 0)
    proj_grad = lax.dynamic_slice_in_dim(
        dot_tn(all_pooled, embed_grad), device_index * shard, shard, 0
    )
    pooled_grad = dot_nt(own_embed, proj_weight) / counts
    final_grad = lax.dot_general(
        member, pooled_grad, (((0,), (0,)), ((), ())), precision=highest, preferred_element_type=f32
    )

    def norm_back(values, inv, gain, grad):
        scaled = grad * gain
        inner_mean = jnp.mean(values * scaled, -1, keepdims=True)
        return (
            inv * scaled - values * (inv * inv * inv * inner_mean),
            jnp.sum(values * inv * grad, 0),
        )

    hidden_two_grad, final_gain_grad = norm_back(hidden_two, inv_final, final_gain, final_grad)
    ff_grad = hidden_two_grad.astype(bf16)
    up_out_grad = (dot_nt(ff_grad, down_weight) * slope).astype(bf16)
    normed_two_grad = mp_sum(dot_nt(up_out_grad, up_weight))
    down_sum = weight_scatter(ff_grad, active).T
    up_sum = weight_scatter(normed_two, up_out_grad)
    part, ff_gain_grad = norm_back(hidden_one, inv_two, ff_gain, normed_two_grad)
    hidden_one_grad = hidden_two_grad + part
    attn_grad = hidden_one_grad.astype(bf16)
    output_sum = weight_scatter(attn_grad, attn_mix).T
    mix_grad = dot_nt(attn_grad, output_weight).astype(bf16)

    query_g, key_g, value_g, bias_g = whole(
        attend_back_kernel,
        (
            struct((length, inner), bf16),
            struct((length, inner), bf16),
            struct((length, inner), bf16),
            struct((bucket_count, head_count), f32),
        ),
        [
            pltpu.VMEM((2, length, length), bf16),
            pltpu.VMEM((2, BLOCK, span), f32),
            pltpu.VMEM((8, span), f32),
        ],
        query,
        key,
        value,
        probs,
        mix_grad,
        ids_row,
    )
    normed_one_grad = mp_sum(
        dot_nt(query_g, query_weight) + dot_nt(key_g, key_weight) + dot_nt(value_g, value_weight)
    )
    qkv_sum = weight_scatter(normed_one, jnp.concatenate([query_g, key_g, value_g], 1))
    part, attn_gain_grad = norm_back(residual, inv_rms(residual), attn_gain, normed_one_grad)
    tokens_grad = (hidden_one_grad + part).reshape(tokens.shape)

    gains = jnp.stack([attn_gain_grad, ff_gain_grad, final_gain_grad], 1)
    bias_columns = -(-bucket_count * head_count // shard)
    bias_flat = jnp.pad(bias_g.reshape(-1), (0, bias_columns * shard - bucket_count * head_count))
    bias_part = jnp.tile(bias_flat.reshape(shard, bias_columns), (width // shard, 1))
    small = lax.optimization_barrier(jnp.concatenate([gains, bias_part], 1))
    halves = small.reshape(2, width // 2, -1)
    small = lax.dynamic_index_in_dim(halves, tower_index, 0, False) + swap(
        lax.dynamic_index_in_dim(halves, 1 - tower_index, 0, False), "tower"
    )
    bit = 1
    while bit < lax.axis_size("rows"):
        view = small.reshape(-1, 2, shard, small.shape[-1])
        own_bit = (lax.axis_index("rows") & bit) // bit
        small = lax.dynamic_index_in_dim(view, own_bit, 1, False) + swap(
            lax.dynamic_index_in_dim(view, 1 - own_bit, 1, False), "rows", bit
        )
        bit *= 2
    small = small.reshape(shard, -1)
    bias_total = small[:, 3:].reshape(-1)[: bucket_count * head_count].reshape(
        bucket_count, head_count
    )
    return (
        loss_value,
        tokens_grad,
        small[:, 0],
        qkv_sum[:, :inner],
        qkv_sum[:, inner : 2 * inner],
        qkv_sum[:, 2 * inner :],
        output_sum,
        bias_total,
        small[:, 1],
        up_sum,
        down_sum,
        small[:, 2],
        proj_grad,
    )


def solution(mesh):
    in_specs = (
        P("tower", "rows", None, None),
        P("tower", "rows", None),
        P(),
        P(),
        P(),
        P(None, "mp"),
        P(None, "mp"),
        P(None, "mp"),
        P("mp", None),
        P(None, "mp"),
        P(),
        P(None, "mp"),
        P("mp", None),
        P(),
        P(),
    )
    out_specs = (
        P(),
        P("tower", "rows", None, None),
        P(("tower", "rows")),
        P(("tower", "rows"), "mp"),
        P(("tower", "rows"), "mp"),
        P(("tower", "rows"), "mp"),
        P("mp", ("tower", "rows")),
        P(None, "mp"),
        P(("tower", "rows")),
        P(("tower", "rows"), "mp"),
        P("mp", ("tower", "rows")),
        P(("tower", "rows")),
        P(("tower", "rows"), None),
    )
    return jax.shard_map(
        per_device, mesh=mesh, in_specs=in_specs, out_specs=out_specs, check_vma=False
    )
```

```python
import functools

import jax
import jax.numpy as jnp
from jax import lax
from jax.experimental import pallas as pl
from jax.experimental.pallas import tpu as pltpu
from jax.sharding import PartitionSpec as P

SEGS_ROW = 8
BLOCK = 128
STRIP = 32
PIECE = 384
LANES = 128
CHUNKS = 2

eps = 1e-06
logit_scale = 50.0
highest = lax.Precision.HIGHEST
f32 = jnp.float32
bf16 = jnp.bfloat16


def inv_rms(values):
    return lax.rsqrt(jnp.mean(values * values, -1, keepdims=True) + eps)


def dot_nn(a, b):
    return lax.dot_general(a, b, (((1,), (0,)), ((), ())), preferred_element_type=f32)


def dot_nt(a, b):
    return lax.dot_general(a, b, (((1,), (1,)), ((), ())), preferred_element_type=f32)


def dot_tn(a, b):
    return lax.dot_general(a, b, (((0,), (0,)), ((), ())), preferred_element_type=f32)


def gelu_parts(values):
    size = jnp.abs(values)
    bell = jnp.exp(-0.5 * values * values)
    t = 1.0 / (1.0 + (0.3275911 * 0.7071067811865476) * size)
    poly = t * (
        0.127414796
        + t * (-0.142248368 + t * (0.7107068705 + t * (-0.7265760135 + t * 0.5307027145)))
    )
    tail = poly * bell
    return bell, jnp.where(values >= 0, 1.0 - tail, tail)


def key_range(block, blocks):
    return max(0, block - 2), min(blocks, block + 3)


def split_low(values, parts):
    out = []
    for _ in range(parts):
        out.append(values.astype(bf16))
        values = values - out[-1].astype(f32)
    return out


def norm_back(values, inv, gain, grad):
    scaled = grad * gain
    inner_mean = jnp.mean(values * scaled, -1, keepdims=True)
    return inv * scaled - values * (inv * inv * inv * inner_mean)


def row_gain(gain_ref):
    return gain_ref[...].reshape(1, gain_ref.shape[0])


def attend_kernel(
    tok_hbm, wq_hbm, wk_hbm, wv_hbm, gain_hbm, table_hbm, ids_hbm, seg_hbm,
    n1_hbm, q_hbm, k_hbm, v_hbm, probs_hbm, mix_hbm, tok_ref, *rest,
):
    mix_refs = rest[:CHUNKS]
    (
        w_ref, gain_ref, table_ref, ids_ref, seg_ref, n1_ref, q_ref, k_ref, v_ref, probs_ref, mix_ref,
        rel_ref, mask_ref, skew_ref, score_ref, sems, out_sems,
    ) = rest[CHUNKS:]
    length, inner = q_ref.shape
    blocks = length // BLOCK
    heads, buckets = table_ref.shape
    pairs = inner // BLOCK
    span = rel_ref.shape[1]
    copies = start_copies(
        sems,
        (tok_hbm, tok_ref),
        (wq_hbm, w_ref.at[0]),
        (wk_hbm, w_ref.at[1]),
        (wv_hbm, w_ref.at[2]),
        (gain_hbm, gain_ref),
        (table_hbm, table_ref),
        (ids_hbm, ids_ref),
        (seg_hbm, seg_ref),
    )
    for copy in copies[4:]:
        copy.wait()
    hot = (
        lax.broadcasted_iota(jnp.int32, (buckets, span - 1), 0)
        == ids_ref[...].reshape(1, span - 1)
    ).astype(f32)
    rel_ref[...] = jnp.zeros_like(rel_ref)
    rel_ref[0:heads, 0 : span - 1] = lax.dot_general(
        table_ref[...], hot, (((1,), (0,)), ((), ())), precision=highest, preferred_element_type=f32
    )
    seg_row = seg_ref[...].astype(f32)
    for b in range(blocks):
        own = jnp.broadcast_to(seg_row[:, b * BLOCK : (b + 1) * BLOCK], (BLOCK, BLOCK)).T
        for c in range(blocks):
            other = jnp.broadcast_to(seg_row[:, c * BLOCK : (c + 1) * BLOCK], (BLOCK, BLOCK))
            mask_ref[b * BLOCK : (b + 1) * BLOCK, c * BLOCK : (c + 1) * BLOCK] = jnp.where(
                own == other, 0.0, -1e30
            )
    copies[0].wait()
    gain = row_gain(gain_ref)
    for at in range(0, length, STRIP):
        x = tok_ref[at : at + STRIP, :].astype(f32)
        n1_ref[at : at + STRIP, :] = (x * inv_rms(x) * gain).astype(bf16)
    n1 = n1_ref[...]
    for i, out_ref in enumerate((q_ref, k_ref, v_ref)):
        copies[1 + i].wait()
        out_ref[...] = dot_nn(n1, w_ref[i]).astype(bf16)
    outs = start_copies(out_sems, (n1_ref, n1_hbm), (q_ref, q_hbm), (k_ref, k_hbm), (v_ref, v_hbm))

    def probs_copy(pair):
        heads_of = pl.ds(2 * pair, 2)
        return pltpu.make_async_copy(probs_ref.at[heads_of], probs_hbm.at[heads_of], out_sems.at[4 + pair])

    low_lanes = lax.broadcasted_iota(jnp.int32, (BLOCK, BLOCK), 1) < BLOCK // 2
    zero = jnp.zeros((BLOCK, BLOCK), bf16)

    @pl.loop(0, pairs)
    def _(pair):
        lanes = pl.ds(pl.multiple_of(pair * BLOCK, BLOCK), BLOCK)
        for h in range(2):
            row = jnp.broadcast_to(rel_ref[pl.ds(pair * 2 + h, 1), :], (BLOCK, span))
            skew_ref[h] = pltpu.roll(row, span - (BLOCK - 1), 1, stride=1, stride_axis=0)
        for b in range(blocks):
            first, last = key_range(b, blocks)
            rows = slice(b * BLOCK, (b + 1) * BLOCK)
            keys = slice(first * BLOCK, last * BLOCK)
            shift = length - BLOCK - b * BLOCK
            q_pair = q_ref[rows, lanes]
            k_pair = k_ref[keys, lanes]
            v_pair = v_ref[keys, lanes]
            width = (last - first) * BLOCK
            for h in range(2):
                q_one = jnp.where(low_lanes if h == 0 else ~low_lanes, q_pair, zero)
                score_ref[h, :, :width] = dot_nt(q_one, k_pair)
            for at in range(0, BLOCK, STRIP):
                part = slice(b * BLOCK + at, b * BLOCK + at + STRIP)
                for h in range(2):
                    head = pair * 2 + h
                    scores = (
                        score_ref[h, at : at + STRIP, :width]
                        + skew_ref[h, at : at + STRIP, shift + first * BLOCK : shift + last * BLOCK]
                        + mask_ref[part, keys]
                    )
                    raised = jnp.exp(scores - jnp.max(scores, -1, keepdims=True))
                    scale = 1.0 / jnp.sum(raised, -1, keepdims=True)
                    probs_ref[head, part, keys] = (raised * scale).astype(bf16)
                    if first > 0:
                        probs_ref[head, part, 0 : first * BLOCK] = jnp.zeros((STRIP, first * BLOCK), bf16)
                    if last < blocks:
                        probs_ref[head, part, last * BLOCK :] = jnp.zeros(
                            (STRIP, length - last * BLOCK), bf16
                        )
            mix_ref[rows, lanes] = jnp.where(
                low_lanes,
                dot_nn(probs_ref[pair * 2, rows, keys], v_pair),
                dot_nn(probs_ref[pair * 2 + 1, rows, keys], v_pair),
            ).astype(bf16)
        probs_copy(pair).start()

    outs += start_copies(out_sems.at[4 + pairs :], (mix_ref, mix_hbm))
    for i, part in enumerate(mix_refs):
        part[...] = mix_ref[i * part.shape[0] : (i + 1) * part.shape[0], :]
    for copy in outs:
        copy.wait()
    for pair in range(pairs):
        probs_copy(pair).wait()


def load_kernel(
    wo_hbm, up_hbm, down_hbm, proj_hbm, fetched_hbm, fetched_too_hbm, wo_ref, up_ref, down_ref, proj_ref, sems
):
    me, tower_index = lax.axis_index("mp"), lax.axis_index("tower")
    inner = wo_hbm.shape[0]
    piece = inner // 2
    own_at = pl.multiple_of(me * inner, inner)
    other_at = (1 - me) * inner
    copies = start_copies(
        sems,
        (wo_hbm, wo_ref.at[pl.ds(own_at, inner), :]),
        (fetched_hbm, wo_ref.at[pl.ds(pl.multiple_of(other_at + tower_index * piece, piece), piece), :]),
        (fetched_too_hbm, wo_ref.at[pl.ds(pl.multiple_of(other_at + (1 - tower_index) * piece, piece), piece), :]),
        (up_hbm, up_ref),
        (down_hbm, down_ref),
        (proj_hbm, proj_ref),
    )
    for copy in copies:
        copy.wait()


def ff_kernel(
    chunk, tok_ref, wo_ref, up_ref, down_ref, mix_own, mix_other, gain_ref,
    h1_ref, n2_ref, a_ref, slope_ref, part_ref,
    mix_ref,
):
    size, width = h1_ref.shape
    inner = mix_own.shape[1]
    hidden = up_ref.shape[1]
    step = 256
    me = lax.axis_index("mp")
    mix_ref[:, pl.ds(pl.multiple_of(me * inner, inner), inner)] = mix_own[...]
    mix_ref[:, pl.ds(pl.multiple_of((1 - me) * inner, inner), inner)] = mix_other[...]
    h1_ref[...] = dot_nn(mix_ref[...], wo_ref[...])
    gain = row_gain(gain_ref)
    for at in range(0, size, STRIP):
        rows = slice(at, at + STRIP)
        h1 = tok_ref[chunk * size + at : chunk * size + at + STRIP, :].astype(f32) + h1_ref[rows, :]
        h1_ref[rows, :] = h1
        n2_ref[rows, :] = (h1 * inv_rms(h1) * gain).astype(bf16)
    n2 = n2_ref[...]
    for at in range(0, hidden, step):
        cols = slice(at, at + step)
        slope_ref[:, cols] = dot_nn(n2, up_ref[:, cols])
        for r in range(0, size, STRIP):
            rows = slice(r, r + STRIP)
            u = slope_ref[rows, cols]
            bell, below = gelu_parts(u)
            a_ref[rows, cols] = (u * below).astype(bf16)
            slope_ref[rows, cols] = below + u * bell * 0.3989422804014327
    part_ref[...] = dot_nn(a_ref[...], down_ref[...]).astype(bf16)


def pool_kernel(chunk, h1_ref, own_ref, rec_ref, gain_ref, seg_ref, *rest):
    total_ref = rest[0] if chunk > 0 else None
    h2_ref, out_ref = rest[-2:]
    size, width = h1_ref.shape
    gain = row_gain(gain_ref)
    number = lax.broadcasted_iota(jnp.int32, (SEGS_ROW, 1), 0)
    total = jnp.zeros((SEGS_ROW, width), f32)
    step = 128
    for at in range(0, size, step):
        rows = slice(at, at + step)
        h2 = h1_ref[rows, :] + (own_ref[rows, :].astype(f32) + rec_ref[rows, :].astype(f32))
        h2_ref[rows, :] = h2
        member = (seg_ref[:, chunk * size + at : chunk * size + at + step] == number).astype(f32).astype(bf16)
        for piece in split_low(h2 * inv_rms(h2) * gain, 2):
            total += dot_nn(member, piece)
    if chunk > 0:
        total += total_ref[...]
    if chunk == CHUNKS - 1:
        counts = jnp.sum((seg_ref[...] == number).astype(f32), -1, keepdims=True)
        total = total / counts
    out_ref[...] = total.astype(out_ref.dtype)


def contrast_kernel(
    total_segs, proj_ref, gathered_ref, pair_ref, loss_ref, dproj_ref, own_ref
):
    me = lax.axis_index("tower") * lax.axis_size("rows") + lax.axis_index("rows")
    count = gathered_ref.shape[0]
    row = lax.broadcasted_iota(jnp.int32, (count, count), 0)
    col = lax.broadcasted_iota(jnp.int32, (count, count), 1)
    order = (col == (row ^ (me * SEGS_ROW))).astype(f32).astype(bf16)
    pooled = dot_nn(order, gathered_ref[...]).astype(bf16)
    e = dot_nn(pooled, proj_ref[...])
    inv = lax.rsqrt(jnp.sum(e * e, -1, keepdims=True) + eps)
    unit = e * inv
    unit_low = unit.astype(bf16)
    zq, zd = unit_low[:total_segs], unit_low[total_segs:]
    logits = logit_scale * dot_nt(zd, zq)
    positive = (
        lax.broadcasted_iota(jnp.int32, (total_segs, total_segs), 0)
        == pair_ref[...].reshape(1, total_segs)
    ).astype(f32)
    norms, shares = [], []
    for axis in (0, 1):
        most = jnp.max(logits, axis, keepdims=True)
        raised = jnp.exp(logits - most)
        total = jnp.sum(raised, axis, keepdims=True)
        norms.append(jnp.log(total) + most)
        shares.append(raised / total)
    half_share = 0.5 / total_segs
    ends = jnp.sum(norms[0], 1, keepdims=True) + jnp.sum(norms[1], 0, keepdims=True)
    hits = jnp.sum(jnp.sum(logits * positive, 1, keepdims=True), 0, keepdims=True)
    loss_ref[...] = half_share * (ends - 2.0 * hits)
    grad = (half_share * (shares[0] + shares[1] - 2.0 * positive)).astype(bf16)
    dz = logit_scale * jnp.concatenate([dot_tn(grad, zd), dot_nn(grad, zq)], 0)
    de = ((dz - unit * jnp.sum(unit * dz, -1, keepdims=True)) * inv).astype(bf16)
    width, shard = proj_ref.shape[0], dproj_ref.shape[0]
    row = lax.broadcasted_iota(jnp.int32, (width, shard), 0)
    col = lax.broadcasted_iota(jnp.int32, (width, shard), 1)
    columns = (row == col + me * shard).astype(f32).astype(bf16)
    dproj_ref[...] = dot_tn(dot_nn(pooled, columns).astype(bf16), de)
    row = lax.broadcasted_iota(jnp.int32, (SEGS_ROW, count), 0)
    col = lax.broadcasted_iota(jnp.int32, (SEGS_ROW, count), 1)
    mine = (col == row + me * SEGS_ROW).astype(f32).astype(bf16)
    own_ref[...] = dot_nt(dot_nn(mine, de).astype(bf16), proj_ref[...])


def ff_back_kernel(
    chunk, down_ref, up_ref, h2_ref, slope_ref, *rest
):
    last = chunk == CHUNKS - 1
    count = 3 + (2 * CHUNKS - 1 if last else 0)
    given, outs = rest[:count], rest[count:]
    dpool_ref, seg_ref, gain_ref = given[-3:]
    part_ref, part_hbm, dh2_hbm, dgain_ref, du_ref = outs[:5]
    dh2_ref, sems = outs[-2:]
    df_ref = outs[-3] if last else outs[5]
    size, width = h2_ref.shape
    hidden = down_ref.shape[0]
    step = 256
    gain = row_gain(gain_ref)
    number = lax.broadcasted_iota(jnp.int32, (SEGS_ROW, 1), 0)
    counts = jnp.sum((seg_ref[...] == number).astype(f32), -1, keepdims=True)
    pieces = jnp.concatenate([p.astype(f32) for p in split_low(dpool_ref[...] / counts, 4)], 0).astype(bf16)
    member = (seg_ref[:, chunk * size : (chunk + 1) * size] == number).astype(f32)
    member = jnp.concatenate([member] * 4, 0).astype(bf16)
    dh2_ref[...] = dot_tn(member, pieces)
    dgain = jnp.zeros((1, width), f32)
    for at in range(0, size, STRIP):
        rows = slice(at, at + STRIP)
        h2 = h2_ref[rows, :]
        grad = dh2_ref[rows, :]
        inv = inv_rms(h2)
        dh2 = norm_back(h2, inv, gain, grad)
        dgain += jnp.sum(h2 * inv * grad, 0, keepdims=True)
        dh2_ref[rows, :] = dh2
        df_ref[rows, :] = dh2.astype(bf16)
    dgain_ref[...] = dgain
    df = df_ref[...]
    for at in range(0, hidden, step):
        cols = slice(at, at + step)
        du_ref[:, cols] = (dot_nt(df, down_ref[cols, :]) * slope_ref[:, cols]).astype(bf16)
    part_ref[...] = dot_nt(du_ref[...], up_ref[...]).astype(bf16)
    copies = start_copies(sems, (dh2_ref, dh2_hbm), (part_ref, part_hbm))
    if last:
        weight_products([*given[CHUNKS:-3], df_ref], given[:CHUNKS], outs[5:-4], outs[-4])
    for copy in copies:
        copy.wait()


def middle_back_kernel(chunk, *refs):
    first, last = chunk == 0, chunk == CHUNKS - 1
    refs = list(refs)

    def take(count):
        taken = refs[:count]
        del refs[:count]
        return taken

    own_hbm, dh2_hbm = take(2)
    ahead = take(4) if last else []
    wo_ref, h1_ref = take(2)
    lefts, rights = (take(CHUNKS), take(CHUNKS)) if first else ([], [])
    rec_ref, gain_ref = take(2)
    dh1_hbm, da_hbm, dmix_ref, dgain_ref = take(4)
    held = take(4) if last else []
    halves = take(len(refs) - 6) if first else []
    own_ref, dh2_ref, dh1_ref, da_ref, sems, out_sems = refs
    copies = start_copies(sems, (own_hbm, own_ref), (dh2_hbm, dh2_ref), *zip(ahead, held))
    if first:
        weight_products(lefts, rights, halves[:-1], halves[-1])
    for copy in copies[:2]:
        copy.wait()
    size, width = h1_ref.shape
    gain = row_gain(gain_ref)
    dgain = jnp.zeros((1, width), f32)
    for at in range(0, size, STRIP):
        rows = slice(at, at + STRIP)
        h1 = h1_ref[rows, :]
        grad = own_ref[rows, :].astype(f32) + rec_ref[rows, :].astype(f32)
        inv = inv_rms(h1)
        dh1 = dh2_ref[rows, :] + norm_back(h1, inv, gain, grad)
        dgain += jnp.sum(h1 * inv * grad, 0, keepdims=True)
        dh1_ref[rows, :] = dh1
        da_ref[rows, :] = dh1.astype(bf16)
    dgain_ref[...] = dgain
    outs = start_copies(out_sems, (dh1_ref, dh1_hbm), (da_ref, da_hbm))
    inner = dmix_ref.shape[1]
    own_at = pl.multiple_of(lax.axis_index("mp") * inner, inner)
    dmix_ref[...] = dot_nt(da_ref[...], wo_ref[pl.ds(own_at, inner), :]).astype(bf16)
    for copy in copies[2:] + outs:
        copy.wait()


def attend_back_kernel(wq_hbm, wk_hbm, wv_hbm, n1_hbm, q_ref, k_ref, v_ref, probs_ref, *rest):
    mixg_refs = rest[:CHUNKS]
    ids_ref, grads_ref, biasg_ref, w_ref, n1_ref, ds_ref, skew_ref, rel_ref, dp_ref, mixg_ref, sems = rest[CHUNKS:]
    length, inner = q_ref.shape
    blocks = length // BLOCK
    pairs = inner // BLOCK
    span = rel_ref.shape[1]
    later = start_copies(
        sems, (wq_hbm, w_ref.at[0]), (wk_hbm, w_ref.at[1]), (wv_hbm, w_ref.at[2]), (n1_hbm, n1_ref)
    )
    low_lanes = lax.broadcasted_iota(jnp.int32, (BLOCK, BLOCK), 1) < BLOCK // 2
    low_all = lax.broadcasted_iota(jnp.int32, (length, BLOCK), 1) < BLOCK // 2
    zero = jnp.zeros((BLOCK, BLOCK), bf16)
    rel_ref[...] = jnp.zeros_like(rel_ref)
    for i, part in enumerate(mixg_refs):
        mixg_ref[i * part.shape[0] : (i + 1) * part.shape[0], :] = part[...]

    @pl.loop(0, pairs)
    def _(pair):
        lanes = pl.ds(pl.multiple_of(pair * BLOCK, BLOCK), BLOCK)
        skew_ref[...] = jnp.zeros_like(skew_ref)
        for b in range(blocks):
            first, last = key_range(b, blocks)
            rows = slice(b * BLOCK, (b + 1) * BLOCK)
            keys = slice(first * BLOCK, last * BLOCK)
            shift = length - BLOCK - b * BLOCK
            g_pair = mixg_ref[rows, lanes]
            k_pair = k_ref[keys, lanes]
            v_pair = v_ref[keys, lanes]
            width = (last - first) * BLOCK
            for h in range(2):
                g_one = jnp.where(low_lanes if h == 0 else ~low_lanes, g_pair, zero)
                dp_ref[h, :, :width] = dot_nt(g_one, v_pair)
            for at in range(0, BLOCK, STRIP):
                part = slice(b * BLOCK + at, b * BLOCK + at + STRIP)
                for h in range(2):
                    probs = probs_ref[pair * 2 + h, part, keys].astype(f32)
                    weighted = probs * dp_ref[h, at : at + STRIP, :width]
                    ds = weighted - probs * jnp.sum(weighted, -1, keepdims=True)
                    ds_ref[h, part, keys] = ds.astype(bf16)
                    if first > 0:
                        ds_ref[h, part, 0 : first * BLOCK] = jnp.zeros((STRIP, first * BLOCK), bf16)
                    if last < blocks:
                        ds_ref[h, part, last * BLOCK :] = jnp.zeros((STRIP, length - last * BLOCK), bf16)
                    skew_ref[h, at : at + STRIP, shift + first * BLOCK : shift + last * BLOCK] += ds
            grads_ref[rows, lanes] = jnp.where(
                low_lanes,
                dot_nn(ds_ref[0, rows, keys], k_pair),
                dot_nn(ds_ref[1, rows, keys], k_pair),
            ).astype(bf16)
        q_pair = q_ref[:, lanes]
        g_pair = mixg_ref[:, lanes]
        k_lanes = pl.ds(pl.multiple_of(inner + pair * BLOCK, BLOCK), BLOCK)
        v_lanes = pl.ds(pl.multiple_of(2 * inner + pair * BLOCK, BLOCK), BLOCK)
        grads_ref[:, k_lanes] = jnp.where(
            low_all, dot_tn(ds_ref[0], q_pair), dot_tn(ds_ref[1], q_pair)
        ).astype(bf16)
        grads_ref[:, v_lanes] = jnp.where(
            low_all,
            dot_tn(probs_ref[pair * 2], g_pair),
            dot_tn(probs_ref[pair * 2 + 1], g_pair),
        ).astype(bf16)
        for h in range(2):
            tiles = skew_ref[h, BLOCK - 8 :, :]
            for r in range(0, BLOCK - 8, 8):
                tiles += pltpu.roll(skew_ref[h, r : r + 8, :], BLOCK - 8 - r, 1)
            line = tiles[7:8, :]
            for r in range(7):
                line += pltpu.roll(tiles[r : r + 1, :], 7 - r, 1)
            rel_ref[pl.ds(pair * 2 + h, 1), :] = line

    hot = (
        lax.broadcasted_iota(jnp.int32, (biasg_ref.shape[0], span - 1), 0)
        == ids_ref[...].reshape(1, span - 1)
    ).astype(f32)
    total = lax.dot_general(
        hot, rel_ref[:, : span - 1], (((1,), (1,)), ((), ())), precision=highest, preferred_element_type=f32
    )
    biasg_ref[...] = total[:, : biasg_ref.shape[1]]
    for copy in later:
        copy.wait()


def project_back_kernel(w_ref, tok_ref, grads_ref, *refs):
    part_refs, (part_hbm, dgain_ref, part_ref, sems) = refs[:CHUNKS], refs[CHUNKS:]
    length, width = part_ref.shape
    inner = w_ref.shape[2]
    size = length // CHUNKS
    for c in range(CHUNKS):
        rows = slice(c * size, (c + 1) * size)
        part = (
            dot_nt(grads_ref[rows, :inner], w_ref[0])
            + dot_nt(grads_ref[rows, inner : 2 * inner], w_ref[1])
            + dot_nt(grads_ref[rows, 2 * inner :], w_ref[2])
        ).astype(bf16)
        part_ref[rows, :] = part
        part_refs[c][...] = part
    (copy,) = start_copies(sems, (part_ref, part_hbm))
    dgain = jnp.zeros((1, width), f32)
    for at in range(0, length, STRIP):
        rows = slice(at, at + STRIP)
        x = tok_ref[rows, :].astype(f32)
        dgain += jnp.sum(x * inv_rms(x) * part_ref[rows, :].astype(f32), 0, keepdims=True)
    dgain_ref[...] = dgain
    copy.wait()


def last_kernel(own_hbm, *refs):
    stored_refs, (tok_ref, gain_ref), received = refs[:CHUNKS], refs[CHUNKS : CHUNKS + 2], refs[CHUNKS + 2 : 2 * CHUNKS + 2]
    out_ref, own_ref, dh1_ref, sems = refs[-4:]
    size = own_ref.shape[0] // CHUNKS
    copies = start_copies(
        sems, (own_hbm, own_ref), *[(stored_refs[c], dh1_ref.at[pl.ds(c * size, size), :]) for c in range(CHUNKS)]
    )
    gain = row_gain(gain_ref)
    for copy in copies:
        copy.wait()
    for at in range(0, CHUNKS * size, STRIP):
        rows = slice(at, at + STRIP)
        there = slice(at % size, at % size + STRIP)
        x = tok_ref[rows, :].astype(f32)
        grad = own_ref[rows, :].astype(f32) + received[at // size][there, :].astype(f32)
        out_ref[rows, :] = dh1_ref[rows, :] + norm_back(x, inv_rms(x), gain, grad)


def weight_products(lefts, rights, other_refs, own_ref, columns=0):
    tower_index = lax.axis_index("tower")
    half = lefts[0].shape[1] // 2
    for which in (1 - tower_index, tower_index):
        is_own = which is tower_index
        lanes = pl.ds(pl.multiple_of(which * half, half), half)
        turned = [left[:, lanes].T for left in lefts]
        for at in range(0, rights[0].shape[1], PIECE):
            total = None
            for left, right in zip(turned, rights):
                term = dot_nn(left, right[:, at : at + PIECE])
                total = term if total is None else total + term
            there = columns + at
            if is_own:
                own_ref[:, there : there + PIECE] = total.astype(bf16)
            else:
                other_refs[there // PIECE][...] = total.astype(bf16)


def query_key_kernel(shard, n1_ref, grads_ref, bias_ref, *refs):
    inner = grads_ref.shape[1] // 3
    count = 2 * inner // PIECE + 3
    parts, outs, all_ref = refs[:-count], refs[-count:-1], refs[-1]
    own_ref = outs[-1]
    tower_index = lax.axis_index("tower")
    width = all_ref.shape[0]
    half = width // 2
    buckets, heads = bias_ref.shape
    lane = lax.broadcasted_iota(jnp.int32, (1, LANES), 1)

    def low(values):
        return values.astype(f32).astype(bf16)

    row = lax.broadcasted_iota(jnp.int32, (width, buckets), 0) % shard
    col = lax.broadcasted_iota(jnp.int32, (width, buckets), 1)
    total = jnp.zeros((width, LANES), f32)
    for g in range(-(-buckets // shard)):
        place = lax.broadcasted_iota(jnp.int32, (heads, LANES), 0) + 3 + g * heads == lane
        total += dot_nn(low(col == row + g * shard), low(dot_nn(low(bias_ref[...]), low(place))))
    lines = [
        sum(part[...] for part in some) for some in (parts[:1], parts[1 : 1 + CHUNKS], parts[1 + CHUNKS :])
    ]
    place = lax.broadcasted_iota(jnp.int32, (3, LANES), 0) == lane
    all_ref[...] = total + dot_tn(low(jnp.concatenate(lines, 0)), low(place))
    outs[-2][...] = all_ref[pl.ds(pl.multiple_of((1 - tower_index) * half, half), half), :].astype(bf16)
    own_ref[:, 2 * inner :] = all_ref[pl.ds(pl.multiple_of(tower_index * half, half), half), :].astype(bf16)
    weight_products([n1_ref], [grads_ref.at[:, : 2 * inner]], outs[:-2], own_ref)


def value_output_kernel(*refs):
    stored_refs = refs[: CHUNKS + 1]
    n1_ref, grads_ref, *outs = refs[CHUNKS + 1 : -2 - CHUNKS]
    mix_ref, *da_refs = refs[-2 - CHUNKS : -1]
    copies = start_copies(refs[-1], *zip(stored_refs, (mix_ref, *da_refs)))
    inner = grads_ref.shape[1] // 3
    weight_products([n1_ref], [grads_ref.at[:, 2 * inner :]], outs[:-1], outs[-1])
    for copy in copies:
        copy.wait()
    size = da_refs[0].shape[0]
    pieces = [mix_ref.at[c * size : (c + 1) * size, :] for c in range(CHUNKS)]
    weight_products(da_refs, pieces, outs[:-1], outs[-1], inner)


def split_kernel(shard, bit, low, own_ref, *refs):
    rec_refs, (keep_ref, send_ref) = refs[:-2], refs[-2:]
    own_bit = lax.axis_index("rows") // bit % 2
    at = 0
    for rec_ref in rec_refs:
        cols = slice(at, at + rec_ref.shape[1])
        at = cols.stop
        for j in range(keep_ref.shape[0] // shard):
            for which, out_ref in ((own_bit, keep_ref), (1 - own_bit, send_ref)):
                start = ((j // low * 2 + which) * low + j % low) * shard
                rows = pl.ds(pl.multiple_of(start, shard), shard)
                out_ref[j * shard : (j + 1) * shard, cols] = (
                    own_ref[rows, cols].astype(f32) + rec_ref[rows, :].astype(f32)
                ).astype(bf16)


def fixed(shape, dtype):
    return pltpu.VMEM(shape, dtype)


def stored(shape, dtype):
    return pltpu.HBM(shape, dtype)


def whole(name, kernel, out_shapes, *args, scratch=(), in_hbm=0, in_vmem=0, mib=16):
    args = (
        [pltpu.with_memory_space_constraint(v, pltpu.HBM) for v in args[:in_hbm]]
        + [pltpu.with_memory_space_constraint(v, pltpu.VMEM) for v in args[in_hbm : in_hbm + in_vmem]]
        + list(args[in_hbm + in_vmem :])
    )
    vmem = pl.BlockSpec(memory_space=pltpu.VMEM)
    hbm = pl.BlockSpec(memory_space=pl.ANY)
    is_stored = lambda out: getattr(out, "memory_space", None) == pltpu.HBM
    with jax.named_scope(name):
        return pl.pallas_call(
            kernel,
            out_shape=out_shapes,
            in_specs=[hbm] * in_hbm + [vmem] * (len(args) - in_hbm),
            out_specs=jax.tree.map(lambda out: hbm if is_stored(out) else vmem, out_shapes),
            scratch_shapes=scratch,
            compiler_params=pltpu.CompilerParams(vmem_limit_bytes=mib * 1024 * 1024),
            cost_estimate=pl.CostEstimate(flops=1, bytes_accessed=1, transcendentals=0),
        )(*args)


def start_copies(sems, *pairs):
    copies = [pltpu.make_async_copy(src, dst, sems.at[i]) for i, (src, dst) in enumerate(pairs)]
    for copy in copies:
        copy.start()
    return copies


def swap(values, axis, bit=1):
    count = lax.axis_size(axis)
    return lax.ppermute(values, axis, [(i, i ^ bit) for i in range(count)])


def gather_all(values):
    bit = 1
    while bit < lax.axis_size("rows"):
        values = jnp.concatenate([values, swap(values, "rows", bit)], 0)
        bit *= 2
    return jnp.concatenate([values, swap(values, "tower")], 0)


def row_halves(cur, bit, low, shard):
    columns = cur.shape[-1]
    view = cur.reshape(-1, 2, low * shard, columns)
    own_bit = (lax.axis_index("rows") & bit) // bit
    keep = lax.dynamic_index_in_dim(view, own_bit, 1, False).reshape(-1, columns)
    send = lax.dynamic_index_in_dim(view, 1 - own_bit, 1, False).reshape(-1, columns)
    return keep, send


class RowsScatter:
    def __init__(self, name, shard, own, received, swapped=False):
        self.name, self.shard = name, shard
        self.own, self.received = own, received
        self.bits = [1 << i for i in range(lax.axis_size("rows").bit_length() - 1)]
        self.order = list(self.bits)
        if swapped and len(self.order) > 1:
            self.order[0], self.order[1] = self.order[1], self.order[0]

    def split(self):
        self.bit = self.order.pop(0)
        low = 1 << sorted(self.bits).index(self.bit)
        self.bits.remove(self.bit)
        columns = self.own.shape[1]
        if self.shard % 16 == 0:
            half = struct((self.own.shape[0] // 2, columns), bf16)
            self.own, self.send = whole(
                self.name, functools.partial(split_kernel, self.shard, self.bit, low), (half, half), self.own, *self.received
            )
        else:
            total = self.total().astype(bf16)
            self.own, self.send = row_halves(total, self.bit, low, self.shard)

    def exchange(self):
        self.received = [swap(self.send, "rows", self.bit)]

    def total(self):
        return self.own.astype(f32) + jnp.concatenate(self.received, 1).astype(f32)

    def step(self):
        self.split()
        self.exchange()

    def finish(self):
        while self.order:
            self.step()
        return self.total()


def tie(*values):
    return lax.optimization_barrier(values)


def struct(shape, dtype):
    return jax.ShapeDtypeStruct(shape, dtype)


def per_device(
    tokens,
    segment_ids,
    pair_ids,
    bucket_ids,
    attn_gain,
    query_weight,
    key_weight,
    value_weight,
    output_weight,
    bias_table,
    ff_gain,
    up_weight,
    down_weight,
    final_gain,
    proj_weight,
):
    length = tokens.shape[2]
    width = tokens.shape[3]
    inner = query_weight.shape[1]
    hidden = up_weight.shape[1]
    head_count = bias_table.shape[1]
    bucket_count = bias_table.shape[0]
    total_segs = pair_ids.shape[0]
    span = 2 * length
    size = length // CHUNKS
    chunks = range(CHUNKS)
    tower_index = lax.axis_index("tower")
    device_index = tower_index * lax.axis_size("rows") + lax.axis_index("rows")
    shard = width // (2 * lax.axis_size("rows"))

    token_row = tokens.reshape(length, width)
    segments = segment_ids.reshape(1, length)

    part_rows = inner // 2
    fetched = swap(
        lax.dynamic_slice_in_dim(output_weight, tower_index * part_rows, part_rows, 0), "mp"
    )

    normed_one, query, key, value, probs, mix_stored, tok, *mixes = whole(
        "attention",
        attend_kernel,
        (
            stored((length, width), bf16),
            stored((length, inner), bf16),
            stored((length, inner), bf16),
            stored((length, inner), bf16),
            stored((head_count, length, length), bf16),
            stored((length, inner), bf16),
            fixed((length, width), bf16),
        )
        + (fixed((size, inner), bf16),) * CHUNKS,
        token_row,
        query_weight,
        key_weight,
        value_weight,
        attn_gain,
        bias_table.T,
        bucket_ids,
        segments,
        scratch=[
            pltpu.VMEM((3, width, inner), bf16),
            pltpu.VMEM((width,), f32),
            pltpu.VMEM((head_count, bucket_count), f32),
            pltpu.VMEM((span - 1,), jnp.int32),
            pltpu.VMEM((1, length), jnp.int32),
            pltpu.VMEM((length, width), bf16),
            pltpu.VMEM((length, inner), bf16),
            pltpu.VMEM((length, inner), bf16),
            pltpu.VMEM((length, inner), bf16),
            pltpu.VMEM((head_count, length, length), bf16),
            pltpu.VMEM((length, inner), bf16),
            pltpu.VMEM((8, span), f32),
            pltpu.VMEM((length, length), f32),
            pltpu.VMEM((2, BLOCK, span), f32),
            pltpu.VMEM((2, BLOCK, length), f32),
            pltpu.SemaphoreType.DMA((8,)),
            pltpu.SemaphoreType.DMA((5 + inner // BLOCK,)),
        ],
        in_hbm=8,
        mib=24,
    )
    mix_received = [swap(mix, "mp") for mix in mixes]
    fetched, segments = tie(fetched, tie(segments, mixes[-1])[0])
    fetched_too = swap(fetched, "tower")
    output_whole, up_held, down_held, proj_held = whole(
        "load",
        load_kernel,
        (
            fixed((2 * inner, width), bf16),
            fixed((width, hidden), bf16),
            fixed((hidden, width), bf16),
            fixed((width, width), bf16),
        ),
        output_weight,
        up_weight,
        down_weight,
        proj_weight,
        fetched,
        fetched_too,
        scratch=[pltpu.SemaphoreType.DMA((6,))],
        in_hbm=4,
    )

    hidden_one, normed_two, active, slope, ff_part, ff_received = [], [], [], [], [], []
    for c in chunks:
        outs = whole(
            "feed_forward",
            functools.partial(ff_kernel, c),
            (
                fixed((size, width), f32),
                fixed((size, width), bf16),
                fixed((size, hidden), bf16),
                fixed((size, hidden), f32),
                fixed((size, width), bf16),
            ),
            tok,
            output_whole,
            up_held,
            down_held,
            mixes[c],
            mix_received[c],
            ff_gain,
            scratch=[pltpu.VMEM((size, 2 * inner), bf16)],
            in_vmem=5,
        )
        for kept, out in zip((hidden_one, normed_two, active, slope, ff_part), outs):
            kept.append(out)
        ff_received.append(swap(ff_part[c], "mp"))

    hidden_two, pooled = [], []
    for c in chunks:
        h2, total = whole(
            "pool",
            functools.partial(pool_kernel, c),
            (
                fixed((size, width), f32),
                struct((SEGS_ROW, width), bf16 if c == CHUNKS - 1 else f32),
            ),
            hidden_one[c],
            ff_part[c],
            ff_received[c],
            final_gain,
            segments,
            *pooled,
            in_vmem=2,
        )
        hidden_two.append(h2)
        pooled = [total]
    gathered = gather_all(pooled[0])
    loss, proj_grad, pooled_grad = whole(
        "contrast",
        functools.partial(contrast_kernel, total_segs),
        (
            struct((1, 1), f32),
            struct((shard, width), f32),
            struct((SEGS_ROW, width), f32),
        ),
        proj_held,
        gathered,
        pair_ids,
        in_vmem=1,
    )

    two_part, two_own, two_received, hidden_two_grad, final_gain_part = [], [], [], [], []
    ff_grad, up_out_grad = [], []
    half_shapes = (struct((width // 2, PIECE), bf16),) * (hidden // PIECE) + (struct((width // 2, hidden), bf16),)
    for c in chunks:
        last = c == CHUNKS - 1
        low_shape = ((size, width), bf16)
        outs = whole(
            "feed_forward_back",
            functools.partial(ff_back_kernel, c),
            (
                struct((size, width), bf16),
                stored((size, width), bf16),
                stored((size, width), f32),
                struct((1, width), f32),
                fixed((size, hidden), bf16),
            )
            + (half_shapes if last else (fixed(*low_shape),)),
            down_held,
            up_held,
            hidden_two[c],
            slope[c],
            *([*active, *ff_grad] if last else []),
            pooled_grad,
            segments,
            final_gain,
            scratch=([pltpu.VMEM(*low_shape)] if last else [])
            + [pltpu.VMEM((size, width), f32), pltpu.SemaphoreType.DMA((2,))],
            in_vmem=4 + (2 * CHUNKS - 1 if last else 0),
        )
        for kept, out in zip((two_part, two_own, hidden_two_grad, final_gain_part, up_out_grad), outs):
            kept.append(out)
        if not last:
            ff_grad.append(outs[5])
        two_received.append(swap(two_part[c], "mp"))
    down_scatter = RowsScatter("down_split", shard, outs[-1], [swap(v, "tower") for v in outs[5:-1]])

    hidden_one_grad, attn_grad, mix_grad, ff_gain_part = [], [], [], []
    for c in chunks:
        first, last = c == 0, c == CHUNKS - 1
        if last:
            down_scatter.split()
            up_scatter.split()
            two_received[c], down_scatter.send, up_scatter.send = tie(
                two_received[c], down_scatter.send, up_scatter.send
            )
            down_scatter.exchange()
            up_scatter.exchange()
        heads_shape = fixed((length, inner), bf16)
        outs = whole(
            "middle_back",
            functools.partial(middle_back_kernel, c),
            (
                stored((size, width), f32),
                stored((size, width), bf16),
                fixed((size, inner), bf16),
                struct((1, width), f32),
            )
            + ((heads_shape,) * 3 + (fixed((head_count, length, length), bf16),) if last else ())
            + (half_shapes if first else ()),
            two_own[c],
            hidden_two_grad[c],
            *([query, key, value, probs] if last else []),
            output_whole,
            hidden_one[c],
            *([*normed_two, *up_out_grad] if first else []),
            two_received[c],
            ff_gain,
            scratch=[
                pltpu.VMEM((size, width), bf16),
                pltpu.VMEM((size, width), f32),
                pltpu.VMEM((size, width), f32),
                pltpu.VMEM((size, width), bf16),
                pltpu.SemaphoreType.DMA((6,)),
                pltpu.SemaphoreType.DMA((2,)),
            ],
            in_hbm=6 if last else 2,
            in_vmem=2 + (2 * CHUNKS if first else 0),
        )
        for kept, out in zip((hidden_one_grad, attn_grad, mix_grad, ff_gain_part), outs):
            kept.append(out)
        if first:
            up_scatter = RowsScatter(
                "up_split", shard, outs[-1], [swap(v, "tower") for v in outs[4:-1]], swapped=True
            )
        if last:
            heads_held = outs[4:8]

    qkv_grads, bias_grad, qkv_weight, normed_held = whole(
        "attention_back",
        attend_back_kernel,
        (
            fixed((length, 3 * inner), bf16),
            struct((bucket_count, head_count), f32),
            fixed((3, width, inner), bf16),
            fixed((length, width), bf16),
        ),
        query_weight,
        key_weight,
        value_weight,
        normed_one,
        *heads_held,
        *mix_grad,
        bucket_ids,
        scratch=[
            pltpu.VMEM((2, length, length), bf16),
            pltpu.VMEM((2, BLOCK, span), f32),
            pltpu.VMEM((8, span), f32),
            pltpu.VMEM((2, BLOCK, length), f32),
            pltpu.VMEM((length, inner), bf16),
            pltpu.SemaphoreType.DMA((4,)),
        ],
        in_hbm=4,
        in_vmem=4 + CHUNKS,
    )
    *one_part, one_own, attn_gain_part = whole(
        "project_back",
        project_back_kernel,
        (struct((size, width), bf16),) * CHUNKS
        + (stored((length, width), bf16), struct((1, width), f32)),
        qkv_weight,
        tok,
        qkv_grads,
        scratch=[pltpu.VMEM((length, width), bf16), pltpu.SemaphoreType.DMA((1,))],
        in_vmem=3,
    )
    one_received = [swap(part, "mp") for part in one_part]

    piece = struct((width // 2, PIECE), bf16)
    *others, small_other, own = whole(
        "query_key_weight",
        functools.partial(query_key_kernel, shard),
        (piece,) * (2 * inner // PIECE)
        + (struct((width // 2, LANES), bf16), struct((width // 2, 2 * inner + LANES), bf16)),
        normed_held,
        qkv_grads,
        bias_grad,
        attn_gain_part,
        *ff_gain_part,
        *final_gain_part,
        scratch=[pltpu.VMEM((width, LANES), f32)],
        in_vmem=2,
    )
    first_scatter = RowsScatter("query_key_split", shard, own, [swap(v, "tower") for v in (*others, small_other)])
    *others, own = whole(
        "value_output_weight",
        value_output_kernel,
        (piece,) * (2 * inner // PIECE) + (struct((width // 2, 2 * inner), bf16),),
        mix_stored,
        *attn_grad,
        normed_held,
        qkv_grads,
        scratch=[pltpu.VMEM((length, inner), bf16)]
        + [pltpu.VMEM((size, width), bf16)] * CHUNKS
        + [pltpu.SemaphoreType.DMA((1 + CHUNKS,))],
        in_hbm=1 + CHUNKS,
        in_vmem=2,
    )
    second_scatter = RowsScatter(
        "value_output_split", shard, own, [swap(v, "tower") for v in others], swapped=True
    )
    first_scatter.split()
    second_scatter.split()
    down_scatter.split()
    up_scatter.split()
    one_received[0], first_scatter.send, second_scatter.send, down_scatter.send, up_scatter.send = tie(
        one_received[0], first_scatter.send, second_scatter.send, down_scatter.send, up_scatter.send
    )
    first_scatter.exchange()
    second_scatter.exchange()
    down_scatter.exchange()
    up_scatter.exchange()
    down_sum = down_scatter.finish()
    up_sum = up_scatter.finish()
    first_sum = first_scatter.finish()
    second_sum = second_scatter.finish()
    small = first_sum[:, 2 * inner :]
    attn_gain_sum = small[:, 0:1] + swap(small[:, 0:1], "mp")
    bias_rows = [
        small[:, 3 + g * head_count : 3 + (g + 1) * head_count]
        for g in range(-(-bucket_count // shard))
    ]
    bias_total = jnp.concatenate(bias_rows, 0)[:bucket_count]

    tokens_grad = whole(
        "last",
        last_kernel,
        struct((length, width), f32),
        one_own,
        *hidden_one_grad,
        tok,
        attn_gain,
        *one_received,
        scratch=[
            pltpu.VMEM((length, width), bf16),
            pltpu.VMEM((length, width), f32),
            pltpu.SemaphoreType.DMA((1 + CHUNKS,)),
        ],
        in_hbm=1 + CHUNKS,
        in_vmem=1,
    ).reshape(tokens.shape)
    return (
        loss[0, 0],
        tokens_grad,
        attn_gain_sum[:, 0],
        first_sum[:, :inner],
        first_sum[:, inner : 2 * inner],
        second_sum[:, :inner],
        second_sum[:, inner:].T,
        bias_total,
        small[:, 1],
        up_sum,
        down_sum.T,
        small[:, 2],
        proj_grad,
    )


def solution(mesh):
    in_specs = (
        P("tower", "rows", None, None),
        P("tower", "rows", None),
        P(),
        P(),
        P(),
        P(None, "mp"),
        P(None, "mp"),
        P(None, "mp"),
        P("mp", None),
        P(None, "mp"),
        P(),
        P(None, "mp"),
        P("mp", None),
        P(),
        P(),
    )
    out_specs = (
        P(),
        P("tower", "rows", None, None),
        P(("tower", "rows")),
        P(("tower", "rows"), "mp"),
        P(("tower", "rows"), "mp"),
        P(("tower", "rows"), "mp"),
        P("mp", ("tower", "rows")),
        P(None, "mp"),
        P(("tower", "rows")),
        P(("tower", "rows"), "mp"),
        P("mp", ("tower", "rows")),
        P(("tower", "rows")),
        P(("tower", "rows"), None),
    )
    return jax.shard_map(
        per_device, mesh=mesh, in_specs=in_specs, out_specs=out_specs, check_vma=False
    )
```

```python
import functools

import jax
import jax.numpy as jnp
from jax import lax
from jax.experimental import pallas as pl
from jax.experimental.pallas import tpu as pltpu
from jax.sharding import PartitionSpec as P

SEGS_ROW = 8
BLOCK = 128
STRIP = 32
STEP = 384
LANES = 128
FF_SENDS, QK_SENDS, VO_SENDS = 4, 2, 2
CHUNKS = 2

eps = 1e-06
logit_scale = 50.0
highest = lax.Precision.HIGHEST
f32 = jnp.float32
bf16 = jnp.bfloat16


def inv_rms(values):
    return lax.rsqrt(jnp.mean(values * values, -1, keepdims=True) + eps)


def dot_nn(a, b):
    return lax.dot_general(a, b, (((1,), (0,)), ((), ())), preferred_element_type=f32)


def dot_nt(a, b):
    return lax.dot_general(a, b, (((1,), (1,)), ((), ())), preferred_element_type=f32)


def dot_tn(a, b):
    return lax.dot_general(a, b, (((0,), (0,)), ((), ())), preferred_element_type=f32)


def gelu_parts(values):
    size = jnp.abs(values)
    bell = jnp.exp(-0.5 * values * values)
    t = 1.0 / (1.0 + (0.3275911 * 0.7071067811865476) * size)
    poly = t * (
        0.127414796
        + t * (-0.142248368 + t * (0.7107068705 + t * (-0.7265760135 + t * 0.5307027145)))
    )
    tail = poly * bell
    return bell, jnp.where(values >= 0, 1.0 - tail, tail)


def key_range(block, blocks):
    return max(0, block - 2), min(blocks, block + 3)


def split_low(values, parts):
    out = []
    for _ in range(parts):
        out.append(values.astype(bf16))
        values = values - out[-1].astype(f32)
    return out


def norm_back(values, inv, gain, grad):
    scaled = grad * gain
    inner_mean = jnp.mean(values * scaled, -1, keepdims=True)
    return inv * scaled - values * (inv * inv * inv * inner_mean)


def row_gain(gain_ref):
    return gain_ref[...].reshape(1, gain_ref.shape[0])


def attend_kernel(
    tok_hbm, wq_hbm, wk_hbm, wv_hbm, gain_hbm, table_hbm, ids_hbm, seg_hbm,
    n1_hbm, q_hbm, k_hbm, v_hbm, probs_hbm, mix_hbm, tok_ref, *rest,
):
    mix_refs = rest[:CHUNKS]
    (
        w_ref, gain_ref, table_ref, ids_ref, seg_ref, n1_ref, q_ref, k_ref, v_ref, probs_ref, mix_ref,
        rel_ref, mask_ref, skew_ref, score_ref, sems, out_sems,
    ) = rest[CHUNKS:]
    length, inner = q_ref.shape
    blocks = length // BLOCK
    heads, buckets = table_ref.shape
    pairs = inner // BLOCK
    span = rel_ref.shape[1]
    copies = start_copies(
        sems,
        (tok_hbm, tok_ref),
        (wq_hbm, w_ref.at[0]),
        (wk_hbm, w_ref.at[1]),
        (wv_hbm, w_ref.at[2]),
        (gain_hbm, gain_ref),
        (table_hbm, table_ref),
        (ids_hbm, ids_ref),
        (seg_hbm, seg_ref),
    )
    for copy in copies[4:]:
        copy.wait()
    hot = (
        lax.broadcasted_iota(jnp.int32, (buckets, span - 1), 0)
        == ids_ref[...].reshape(1, span - 1)
    ).astype(f32)
    rel_ref[...] = jnp.zeros_like(rel_ref)
    rel_ref[0:heads, 0 : span - 1] = lax.dot_general(
        table_ref[...], hot, (((1,), (0,)), ((), ())), precision=highest, preferred_element_type=f32
    )
    seg_row = seg_ref[...].astype(f32)
    for b in range(blocks):
        own = jnp.broadcast_to(seg_row[:, b * BLOCK : (b + 1) * BLOCK], (BLOCK, BLOCK)).T
        for c in range(blocks):
            other = jnp.broadcast_to(seg_row[:, c * BLOCK : (c + 1) * BLOCK], (BLOCK, BLOCK))
            mask_ref[b * BLOCK : (b + 1) * BLOCK, c * BLOCK : (c + 1) * BLOCK] = jnp.where(
                own == other, 0.0, -1e30
            )
    copies[0].wait()
    gain = row_gain(gain_ref)
    for at in range(0, length, STRIP):
        x = tok_ref[at : at + STRIP, :].astype(f32)
        n1_ref[at : at + STRIP, :] = (x * inv_rms(x) * gain).astype(bf16)
    n1 = n1_ref[...]
    for i, out_ref in enumerate((q_ref, k_ref, v_ref)):
        copies[1 + i].wait()
        out_ref[...] = dot_nn(n1, w_ref[i]).astype(bf16)
    outs = start_copies(out_sems, (n1_ref, n1_hbm), (q_ref, q_hbm), (k_ref, k_hbm), (v_ref, v_hbm))

    def probs_copy(pair):
        heads_of = pl.ds(2 * pair, 2)
        return pltpu.make_async_copy(probs_ref.at[heads_of], probs_hbm.at[heads_of], out_sems.at[4 + pair])

    low_lanes = lax.broadcasted_iota(jnp.int32, (BLOCK, BLOCK), 1) < BLOCK // 2
    zero = jnp.zeros((BLOCK, BLOCK), bf16)

    @pl.loop(0, pairs)
    def _(pair):
        lanes = pl.ds(pl.multiple_of(pair * BLOCK, BLOCK), BLOCK)
        for h in range(2):
            row = jnp.broadcast_to(rel_ref[pl.ds(pair * 2 + h, 1), :], (BLOCK, span))
            skew_ref[h] = pltpu.roll(row, span - (BLOCK - 1), 1, stride=1, stride_axis=0)
        for b in range(blocks):
            first, last = key_range(b, blocks)
            rows = slice(b * BLOCK, (b + 1) * BLOCK)
            keys = slice(first * BLOCK, last * BLOCK)
            shift = length - BLOCK - b * BLOCK
            q_pair = q_ref[rows, lanes]
            k_pair = k_ref[keys, lanes]
            v_pair = v_ref[keys, lanes]
            width = (last - first) * BLOCK
            for h in range(2):
                q_one = jnp.where(low_lanes if h == 0 else ~low_lanes, q_pair, zero)
                score_ref[h, :, :width] = dot_nt(q_one, k_pair)
            for at in range(0, BLOCK, STRIP):
                part = slice(b * BLOCK + at, b * BLOCK + at + STRIP)
                for h in range(2):
                    head = pair * 2 + h
                    scores = (
                        score_ref[h, at : at + STRIP, :width]
                        + skew_ref[h, at : at + STRIP, shift + first * BLOCK : shift + last * BLOCK]
                        + mask_ref[part, keys]
                    )
                    raised = jnp.exp(scores - jnp.max(scores, -1, keepdims=True))
                    scale = 1.0 / jnp.sum(raised, -1, keepdims=True)
                    probs_ref[head, part, keys] = (raised * scale).astype(bf16)
                    if first > 0:
                        probs_ref[head, part, 0 : first * BLOCK] = jnp.zeros((STRIP, first * BLOCK), bf16)
                    if last < blocks:
                        probs_ref[head, part, last * BLOCK :] = jnp.zeros(
                            (STRIP, length - last * BLOCK), bf16
                        )
            mix_ref[rows, lanes] = jnp.where(
                low_lanes,
                dot_nn(probs_ref[pair * 2, rows, keys], v_pair),
                dot_nn(probs_ref[pair * 2 + 1, rows, keys], v_pair),
            ).astype(bf16)
        probs_copy(pair).start()

    outs += start_copies(out_sems.at[4 + pairs :], (mix_ref, mix_hbm))
    for i, part in enumerate(mix_refs):
        part[...] = mix_ref[i * part.shape[0] : (i + 1) * part.shape[0], :]
    for copy in outs:
        copy.wait()
    for pair in range(pairs):
        probs_copy(pair).wait()


def load_kernel(
    wo_hbm, up_hbm, down_hbm, proj_hbm, fetched_hbm, fetched_too_hbm, wo_ref, up_ref, down_ref, proj_ref, sems
):
    me, tower_index = lax.axis_index("mp"), lax.axis_index("tower")
    inner = wo_hbm.shape[0]
    piece = inner // 2
    own_at = pl.multiple_of(me * inner, inner)
    other_at = (1 - me) * inner
    copies = start_copies(
        sems,
        (wo_hbm, wo_ref.at[pl.ds(own_at, inner), :]),
        (fetched_hbm, wo_ref.at[pl.ds(pl.multiple_of(other_at + tower_index * piece, piece), piece), :]),
        (fetched_too_hbm, wo_ref.at[pl.ds(pl.multiple_of(other_at + (1 - tower_index) * piece, piece), piece), :]),
        (up_hbm, up_ref),
        (down_hbm, down_ref),
        (proj_hbm, proj_ref),
    )
    for copy in copies:
        copy.wait()


def ff_kernel(
    chunk, tok_ref, wo_ref, up_ref, down_ref, mix_own, mix_other, gain_ref,
    h1_ref, n2_ref, a_ref, slope_ref, part_ref,
    mix_ref,
):
    size, width = h1_ref.shape
    inner = mix_own.shape[1]
    hidden = up_ref.shape[1]
    step = 256
    me = lax.axis_index("mp")
    mix_ref[:, pl.ds(pl.multiple_of(me * inner, inner), inner)] = mix_own[...]
    mix_ref[:, pl.ds(pl.multiple_of((1 - me) * inner, inner), inner)] = mix_other[...]
    h1_ref[...] = dot_nn(mix_ref[...], wo_ref[...])
    gain = row_gain(gain_ref)
    for at in range(0, size, STRIP):
        rows = slice(at, at + STRIP)
        h1 = tok_ref[chunk * size + at : chunk * size + at + STRIP, :].astype(f32) + h1_ref[rows, :]
        h1_ref[rows, :] = h1
        n2_ref[rows, :] = (h1 * inv_rms(h1) * gain).astype(bf16)
    n2 = n2_ref[...]
    for at in range(0, hidden, step):
        cols = slice(at, at + step)
        slope_ref[:, cols] = dot_nn(n2, up_ref[:, cols])
        for r in range(0, size, STRIP):
            rows = slice(r, r + STRIP)
            u = slope_ref[rows, cols]
            bell, below = gelu_parts(u)
            a_ref[rows, cols] = (u * below).astype(bf16)
            slope_ref[rows, cols] = below + u * bell * 0.3989422804014327
    part_ref[...] = dot_nn(a_ref[...], down_ref[...]).astype(bf16)


def pool_kernel(chunk, h1_ref, own_ref, rec_ref, gain_ref, seg_ref, *rest):
    total_ref = rest[0] if chunk > 0 else None
    h2_ref, out_ref = rest[-2:]
    size, width = h1_ref.shape
    gain = row_gain(gain_ref)
    number = lax.broadcasted_iota(jnp.int32, (SEGS_ROW, 1), 0)
    total = jnp.zeros((SEGS_ROW, width), f32)
    step = 128
    for at in range(0, size, step):
        rows = slice(at, at + step)
        h2 = h1_ref[rows, :] + (own_ref[rows, :].astype(f32) + rec_ref[rows, :].astype(f32))
        h2_ref[rows, :] = h2
        member = (seg_ref[:, chunk * size + at : chunk * size + at + step] == number).astype(f32).astype(bf16)
        for piece in split_low(h2 * inv_rms(h2) * gain, 2):
            total += dot_nn(member, piece)
    if chunk > 0:
        total += total_ref[...]
    if chunk == CHUNKS - 1:
        counts = jnp.sum((seg_ref[...] == number).astype(f32), -1, keepdims=True)
        total = total / counts
    out_ref[...] = total.astype(out_ref.dtype)


def contrast_kernel(
    total_segs, proj_ref, gathered_ref, pair_ref, loss_ref, dproj_ref, own_ref
):
    me = lax.axis_index("tower") * lax.axis_size("rows") + lax.axis_index("rows")
    count = gathered_ref.shape[0]
    row = lax.broadcasted_iota(jnp.int32, (count, count), 0)
    col = lax.broadcasted_iota(jnp.int32, (count, count), 1)
    order = (col == (row ^ (me * SEGS_ROW))).astype(f32).astype(bf16)
    pooled = dot_nn(order, gathered_ref[...]).astype(bf16)
    e = dot_nn(pooled, proj_ref[...])
    inv = lax.rsqrt(jnp.sum(e * e, -1, keepdims=True) + eps)
    unit = e * inv
    unit_low = unit.astype(bf16)
    zq, zd = unit_low[:total_segs], unit_low[total_segs:]
    logits = logit_scale * dot_nt(zd, zq)
    positive = (
        lax.broadcasted_iota(jnp.int32, (total_segs, total_segs), 0)
        == pair_ref[...].reshape(1, total_segs)
    ).astype(f32)
    norms, shares = [], []
    for axis in (0, 1):
        most = jnp.max(logits, axis, keepdims=True)
        raised = jnp.exp(logits - most)
        total = jnp.sum(raised, axis, keepdims=True)
        norms.append(jnp.log(total) + most)
        shares.append(raised / total)
    half_share = 0.5 / total_segs
    ends = jnp.sum(norms[0], 1, keepdims=True) + jnp.sum(norms[1], 0, keepdims=True)
    hits = jnp.sum(jnp.sum(logits * positive, 1, keepdims=True), 0, keepdims=True)
    loss_ref[...] = half_share * (ends - 2.0 * hits)
    grad = (half_share * (shares[0] + shares[1] - 2.0 * positive)).astype(bf16)
    dz = logit_scale * jnp.concatenate([dot_tn(grad, zd), dot_nn(grad, zq)], 0)
    de = ((dz - unit * jnp.sum(unit * dz, -1, keepdims=True)) * inv).astype(bf16)
    width, shard = proj_ref.shape[0], dproj_ref.shape[0]
    row = lax.broadcasted_iota(jnp.int32, (width, shard), 0)
    col = lax.broadcasted_iota(jnp.int32, (width, shard), 1)
    columns = (row == col + me * shard).astype(f32).astype(bf16)
    dproj_ref[...] = dot_tn(dot_nn(pooled, columns).astype(bf16), de)
    row = lax.broadcasted_iota(jnp.int32, (SEGS_ROW, count), 0)
    col = lax.broadcasted_iota(jnp.int32, (SEGS_ROW, count), 1)
    mine = (col == row + me * SEGS_ROW).astype(f32).astype(bf16)
    own_ref[...] = dot_nt(dot_nn(mine, de).astype(bf16), proj_ref[...])


def ff_back_kernel(down_ref, up_ref, *refs):
    h2_refs, slope_refs, refs = refs[:CHUNKS], refs[CHUNKS : 2 * CHUNKS], refs[2 * CHUNKS :]
    dpool_ref, seg_ref, gain_ref, part_ref, dh2_ref, df_ref, du_ref, dgain_ref = refs
    length, width = dh2_ref.shape
    size = length // CHUNKS
    hidden = down_ref.shape[0]
    step = 256
    gain = row_gain(gain_ref)
    number = lax.broadcasted_iota(jnp.int32, (SEGS_ROW, 1), 0)
    counts = jnp.sum((seg_ref[...] == number).astype(f32), -1, keepdims=True)
    pieces = jnp.concatenate([p.astype(f32) for p in split_low(dpool_ref[...] / counts, 4)], 0).astype(bf16)
    member = (seg_ref[...] == number).astype(f32)
    member = jnp.concatenate([member] * 4, 0).astype(bf16)
    dh2_ref[...] = dot_tn(member, pieces)
    dgain = jnp.zeros((1, width), f32)
    for at in range(0, length, STRIP):
        rows = slice(at, at + STRIP)
        h2 = h2_refs[at // size][at % size : at % size + STRIP, :]
        grad = dh2_ref[rows, :]
        inv = inv_rms(h2)
        dh2 = norm_back(h2, inv, gain, grad)
        dgain += jnp.sum(h2 * inv * grad, 0, keepdims=True)
        dh2_ref[rows, :] = dh2
        df_ref[rows, :] = dh2.astype(bf16)
    dgain_ref[...] = dgain
    df = df_ref[...]
    for at in range(0, hidden, step):
        cols = slice(at, at + step)
        da = dot_nt(df, down_ref[cols, :])
        for c in range(CHUNKS):
            rows = slice(c * size, (c + 1) * size)
            du_ref[rows, cols] = (da[rows, :] * slope_refs[c][:, cols]).astype(bf16)
    part_ref[...] = dot_nt(du_ref[...], up_ref[...]).astype(bf16)


def down_weight_kernel(df_ref, *refs):
    size = refs[0].shape[0]
    weight_products([df_ref.at[c * size : (c + 1) * size, :] for c in range(CHUNKS)], refs[:CHUNKS], refs[CHUNKS:-1], refs[-1])


def up_weight_kernel(du_ref, *refs):
    size = refs[0].shape[0]
    weight_products(refs[:CHUNKS], [du_ref.at[c * size : (c + 1) * size, :] for c in range(CHUNKS)], refs[CHUNKS:-1], refs[-1])


def middle_back_kernel(*refs):
    ahead, refs = refs[:4], refs[4:]
    wo_ref, own_ref, dh2_ref, *refs = refs
    h1_refs, refs = refs[:CHUNKS], refs[CHUNKS:]
    rec_ref, gain_ref, dh1_hbm, da_hbm, dmix_ref, dgain_ref, *refs = refs
    held, (dh1_ref, da_ref, sems, out_sems) = refs[:4], refs[4:]
    copies = start_copies(sems, *zip(ahead, held))
    length, width = dh1_ref.shape
    size = length // CHUNKS
    gain = row_gain(gain_ref)
    dgain = jnp.zeros((1, width), f32)
    for at in range(0, length, STRIP):
        rows = slice(at, at + STRIP)
        h1 = h1_refs[at // size][at % size : at % size + STRIP, :]
        grad = own_ref[rows, :].astype(f32) + rec_ref[rows, :].astype(f32)
        inv = inv_rms(h1)
        dh1 = dh2_ref[rows, :] + norm_back(h1, inv, gain, grad)
        dgain += jnp.sum(h1 * inv * grad, 0, keepdims=True)
        dh1_ref[rows, :] = dh1
        da_ref[rows, :] = dh1.astype(bf16)
    dgain_ref[...] = dgain
    copies += start_copies(out_sems, (dh1_ref, dh1_hbm), (da_ref, da_hbm))
    inner = dmix_ref.shape[1]
    own_at = pl.multiple_of(lax.axis_index("mp") * inner, inner)
    dmix_ref[...] = dot_nt(da_ref[...], wo_ref[pl.ds(own_at, inner), :]).astype(bf16)
    for copy in copies:
        copy.wait()


def attend_back_kernel(wq_hbm, wk_hbm, wv_hbm, n1_hbm, q_ref, k_ref, v_ref, probs_ref, *rest):
    mixg_ref, ids_ref, grads_ref, biasg_ref, n1_ref, w_ref, *halves = rest[:-5]
    ds_ref, skew_ref, rel_ref, dp_ref, sems = rest[-5:]
    length, inner = q_ref.shape
    blocks = length // BLOCK
    pairs = inner // BLOCK
    span = rel_ref.shape[1]
    later = start_copies(
        sems, (wq_hbm, w_ref.at[0]), (wk_hbm, w_ref.at[1]), (wv_hbm, w_ref.at[2]), (n1_hbm, n1_ref)
    )
    low_lanes = lax.broadcasted_iota(jnp.int32, (BLOCK, BLOCK), 1) < BLOCK // 2
    low_all = lax.broadcasted_iota(jnp.int32, (length, BLOCK), 1) < BLOCK // 2
    zero = jnp.zeros((BLOCK, BLOCK), bf16)
    rel_ref[...] = jnp.zeros_like(rel_ref)

    @pl.loop(0, pairs)
    def _(pair):
        lanes = pl.ds(pl.multiple_of(pair * BLOCK, BLOCK), BLOCK)
        skew_ref[...] = jnp.zeros_like(skew_ref)
        for b in range(blocks):
            first, last = key_range(b, blocks)
            rows = slice(b * BLOCK, (b + 1) * BLOCK)
            keys = slice(first * BLOCK, last * BLOCK)
            shift = length - BLOCK - b * BLOCK
            g_pair = mixg_ref[rows, lanes]
            k_pair = k_ref[keys, lanes]
            v_pair = v_ref[keys, lanes]
            width = (last - first) * BLOCK
            for h in range(2):
                g_one = jnp.where(low_lanes if h == 0 else ~low_lanes, g_pair, zero)
                dp_ref[h, :, :width] = dot_nt(g_one, v_pair)
            for at in range(0, BLOCK, STRIP):
                part = slice(b * BLOCK + at, b * BLOCK + at + STRIP)
                for h in range(2):
                    probs = probs_ref[pair * 2 + h, part, keys].astype(f32)
                    weighted = probs * dp_ref[h, at : at + STRIP, :width]
                    ds = weighted - probs * jnp.sum(weighted, -1, keepdims=True)
                    ds_ref[h, part, keys] = ds.astype(bf16)
                    if first > 0:
                        ds_ref[h, part, 0 : first * BLOCK] = jnp.zeros((STRIP, first * BLOCK), bf16)
                    if last < blocks:
                        ds_ref[h, part, last * BLOCK :] = jnp.zeros((STRIP, length - last * BLOCK), bf16)
                    skew_ref[h, at : at + STRIP, shift + first * BLOCK : shift + last * BLOCK] += ds
            grads_ref[rows, lanes] = jnp.where(
                low_lanes,
                dot_nn(ds_ref[0, rows, keys], k_pair),
                dot_nn(ds_ref[1, rows, keys], k_pair),
            ).astype(bf16)
        q_pair = q_ref[:, lanes]
        g_pair = mixg_ref[:, lanes]
        k_lanes = pl.ds(pl.multiple_of(inner + pair * BLOCK, BLOCK), BLOCK)
        v_lanes = pl.ds(pl.multiple_of(2 * inner + pair * BLOCK, BLOCK), BLOCK)
        grads_ref[:, k_lanes] = jnp.where(
            low_all, dot_tn(ds_ref[0], q_pair), dot_tn(ds_ref[1], q_pair)
        ).astype(bf16)
        grads_ref[:, v_lanes] = jnp.where(
            low_all,
            dot_tn(probs_ref[pair * 2], g_pair),
            dot_tn(probs_ref[pair * 2 + 1], g_pair),
        ).astype(bf16)
        for h in range(2):
            tiles = skew_ref[h, BLOCK - 8 :, :]
            for r in range(0, BLOCK - 8, 8):
                tiles += pltpu.roll(skew_ref[h, r : r + 8, :], BLOCK - 8 - r, 1)
            line = tiles[7:8, :]
            for r in range(7):
                line += pltpu.roll(tiles[r : r + 1, :], 7 - r, 1)
            rel_ref[pl.ds(pair * 2 + h, 1), :] = line

    hot = (
        lax.broadcasted_iota(jnp.int32, (biasg_ref.shape[0], span - 1), 0)
        == ids_ref[...].reshape(1, span - 1)
    ).astype(f32)
    total = lax.dot_general(
        hot, rel_ref[:, : span - 1], (((1,), (1,)), ((), ())), precision=highest, preferred_element_type=f32
    )
    biasg_ref[...] = total[:, : biasg_ref.shape[1]]
    for copy in later:
        copy.wait()
    weight_products([n1_ref], [grads_ref.at[:, : 2 * inner]], halves[:-1], halves[-1])


def project_back_kernel(shard, *refs):
    mix_hbm, da_hbm, w_ref, tok_ref, n1_ref, grads_ref, bias_ref, ff_gain, final_gain, part_ref, part_hbm, *refs = refs
    *others, small_ref, own_ref, all_ref, mix_ref, da_ref, sems = refs
    copies = start_copies(sems, (mix_hbm, mix_ref), (da_hbm, da_ref))
    length, width = part_ref.shape
    inner = w_ref.shape[2]
    part_ref[...] = (
        dot_nt(grads_ref[:, :inner], w_ref[0])
        + dot_nt(grads_ref[:, inner : 2 * inner], w_ref[1])
        + dot_nt(grads_ref[:, 2 * inner :], w_ref[2])
    ).astype(bf16)
    copies += start_copies(sems.at[2:], (part_ref, part_hbm))
    dgain = jnp.zeros((1, width), f32)
    for at in range(0, length, STRIP):
        rows = slice(at, at + STRIP)
        x = tok_ref[rows, :].astype(f32)
        dgain += jnp.sum(x * inv_rms(x) * part_ref[rows, :].astype(f32), 0, keepdims=True)
    weight_products([n1_ref], [grads_ref.at[:, 2 * inner :]], others, own_ref)
    small_columns(shard, bias_ref, [dgain, ff_gain[...], final_gain[...]], all_ref)
    tower_index = lax.axis_index("tower")
    half = small_ref.shape[0]
    small_ref[...] = all_ref[pl.ds(pl.multiple_of((1 - tower_index) * half, half), half), :].astype(bf16)
    own_ref[:, 2 * inner :] = all_ref[pl.ds(pl.multiple_of(tower_index * half, half), half), :].astype(bf16)
    for copy in copies:
        copy.wait()
    weight_products([da_ref], [mix_ref], others, own_ref, inner)


def last_kernel(own_hbm, dh1_hbm, tok_ref, gain_ref, rec_ref, out_ref, own_ref, dh1_ref, sems):
    copies = start_copies(sems, (own_hbm, own_ref), (dh1_hbm, dh1_ref))
    gain = row_gain(gain_ref)
    for copy in copies:
        copy.wait()
    for at in range(0, own_ref.shape[0], STRIP):
        rows = slice(at, at + STRIP)
        x = tok_ref[rows, :].astype(f32)
        grad = own_ref[rows, :].astype(f32) + rec_ref[rows, :].astype(f32)
        out_ref[rows, :] = dh1_ref[rows, :] + norm_back(x, inv_rms(x), gain, grad)


def weight_products(lefts, rights, other_refs, own_ref, columns=0):
    tower_index = lax.axis_index("tower")
    half = lefts[0].shape[1] // 2
    each = other_refs[0].shape[1]
    for which in (1 - tower_index, tower_index):
        lanes = pl.ds(pl.multiple_of(which * half, half), half)
        turned = [left[:, lanes].T for left in lefts]
        for at in range(0, rights[0].shape[1], STEP):
            total = None
            for left, right in zip(turned, rights):
                term = dot_nn(left, right[:, at : at + STEP])
                total = term if total is None else total + term
            total = total.astype(bf16)
            there = columns + at
            if which is tower_index:
                own_ref[:, there : there + STEP] = total
                continue
            for i, other_ref in enumerate(other_refs):
                begin, end = max(there, i * each), min(there + STEP, (i + 1) * each)
                if begin < end:
                    other_ref[:, begin - i * each : end - i * each] = total[:, begin - there : end - there]


def small_columns(shard, bias_ref, lines, all_ref):
    width = all_ref.shape[0]
    buckets, heads = bias_ref.shape
    lane = lax.broadcasted_iota(jnp.int32, (1, LANES), 1)

    def low(values):
        return values.astype(f32).astype(bf16)

    row = lax.broadcasted_iota(jnp.int32, (width, buckets), 0) % shard
    col = lax.broadcasted_iota(jnp.int32, (width, buckets), 1)
    total = jnp.zeros((width, LANES), f32)
    for g in range(-(-buckets // shard)):
        place = lax.broadcasted_iota(jnp.int32, (heads, LANES), 0) + 3 + g * heads == lane
        total += dot_nn(low(col == row + g * shard), low(dot_nn(low(bias_ref[...]), low(place))))
    place = lax.broadcasted_iota(jnp.int32, (3, LANES), 0) == lane
    all_ref[...] = total + dot_tn(low(jnp.concatenate(lines, 0)), low(place))


def finish_kernel(pieces, own_ref, *refs):
    rec_refs, out_refs = refs[:pieces], refs[pieces:]
    at = 0
    for out_ref, rec_ref in zip(out_refs, rec_refs if pieces > 1 else [rec_refs[0]] * len(out_refs)):
        cols = slice(at, at + out_ref.shape[1])
        at = cols.stop
        out_ref[...] = own_ref[:, cols].astype(f32) + rec_ref[:, cols].astype(f32)


def small_finish_kernel(own_ref, rec_ref, mp_own_ref, mp_rec_ref, *out_refs):
    finish_kernel(1, own_ref, rec_ref, *out_refs[:-4])
    *gain_refs, bias_ref = out_refs[-4:]
    at = own_ref.shape[1] - LANES
    values = own_ref[:, at:].astype(f32) + rec_ref[:, at:].astype(f32)
    others = mp_own_ref[...].astype(f32) + mp_rec_ref[...].astype(f32)
    lane = lax.broadcasted_iota(jnp.int32, (1, LANES), 1)
    values += jnp.where(lane == 0, others, 0.0)
    eye = (lax.broadcasted_iota(jnp.int32, (LANES, LANES), 0) == lane).astype(f32)
    turned = lax.dot_general(
        eye, values, (((1,), (1,)), ((), ())), precision=highest, preferred_element_type=f32
    )
    for i, gain_ref in enumerate(gain_refs):
        gain_ref[...] = turned[i, :]
    bias_ref[...] = turned[3 : 3 + bias_ref.shape[0], : bias_ref.shape[1]]


def split_kernel(shard, bit, low, sends, own_ref, *refs):
    rec_refs, keep_ref, send_refs = refs[: -1 - sends], refs[-1 - sends], refs[-sends:]
    own_bit = lax.axis_index("rows") // bit % 2
    each = send_refs[0].shape[1]
    at = 0
    for rec_ref in rec_refs:
        columns = rec_ref.shape[1]
        for j in range(keep_ref.shape[0] // shard):
            there = slice(j * shard, (j + 1) * shard)
            for which in (own_bit, 1 - own_bit):
                start = ((j // low * 2 + which) * low + j % low) * shard
                rows = pl.ds(pl.multiple_of(start, shard), shard)
                total = (
                    own_ref[rows, at : at + columns].astype(f32) + rec_ref[rows, :].astype(f32)
                ).astype(bf16)
                if which is own_bit:
                    keep_ref[there, at : at + columns] = total
                    continue
                for i, send_ref in enumerate(send_refs):
                    begin, end = max(at, i * each), min(at + columns, (i + 1) * each)
                    if begin < end:
                        send_ref[there, begin - i * each : end - i * each] = total[:, begin - at : end - at]
        at += columns


def fixed(shape, dtype):
    return pltpu.VMEM(shape, dtype)


def stored(shape, dtype):
    return pltpu.HBM(shape, dtype)


def whole(name, kernel, out_shapes, *args, scratch=(), in_hbm=0, in_vmem=0, mib=16):
    args = (
        [pltpu.with_memory_space_constraint(v, pltpu.HBM) for v in args[:in_hbm]]
        + [pltpu.with_memory_space_constraint(v, pltpu.VMEM) for v in args[in_hbm : in_hbm + in_vmem]]
        + list(args[in_hbm + in_vmem :])
    )
    vmem = pl.BlockSpec(memory_space=pltpu.VMEM)
    hbm = pl.BlockSpec(memory_space=pl.ANY)
    is_stored = lambda out: getattr(out, "memory_space", None) == pltpu.HBM
    with jax.named_scope(name):
        return pl.pallas_call(
            kernel,
            out_shape=out_shapes,
            in_specs=[hbm] * in_hbm + [vmem] * (len(args) - in_hbm),
            out_specs=jax.tree.map(lambda out: hbm if is_stored(out) else vmem, out_shapes),
            scratch_shapes=scratch,
            compiler_params=pltpu.CompilerParams(vmem_limit_bytes=mib * 1024 * 1024),
            cost_estimate=pl.CostEstimate(flops=1, bytes_accessed=1, transcendentals=0),
        )(*args)


def start_copies(sems, *pairs):
    copies = [pltpu.make_async_copy(src, dst, sems.at[i]) for i, (src, dst) in enumerate(pairs)]
    for copy in copies:
        copy.start()
    return copies


def swap(values, axis, bit=1):
    count = lax.axis_size(axis)
    return lax.ppermute(values, axis, [(i, i ^ bit) for i in range(count)])


def gather_all(values):
    bits = [1 << i for i in range(lax.axis_size("rows").bit_length() - 1)]
    steps = [bits[:1]] + [bits[i : i + 2] for i in range(1, len(bits), 2)]
    for step in steps:
        masks = step + ([step[0] | step[1]] if len(step) > 1 else [])
        values = jnp.concatenate([values] + [swap(values, "rows", mask) for mask in masks], 0)
    return jnp.concatenate([values, swap(values, "tower")], 0)


def row_halves(cur, bit, low, shard):
    columns = cur.shape[-1]
    view = cur.reshape(-1, 2, low * shard, columns)
    own_bit = (lax.axis_index("rows") & bit) // bit
    keep = lax.dynamic_index_in_dim(view, own_bit, 1, False).reshape(-1, columns)
    send = lax.dynamic_index_in_dim(view, 1 - own_bit, 1, False).reshape(-1, columns)
    return keep, send


class RowsScatter:
    def __init__(self, name, shard, own, received, swapped=False):
        self.name, self.shard = name, shard
        self.own, self.received = own, received
        self.bits = [1 << i for i in range(lax.axis_size("rows").bit_length() - 1)]
        self.order = list(self.bits)
        if swapped and len(self.order) > 1:
            self.order[0], self.order[1] = self.order[1], self.order[0]

    def split(self, sends=1):
        self.bit = self.order.pop(0)
        low = 1 << sorted(self.bits).index(self.bit)
        self.bits.remove(self.bit)
        rows, columns = self.own.shape[0] // 2, self.own.shape[1]
        if self.shard % 16 == 0:
            self.own, *self.send = whole(
                self.name,
                functools.partial(split_kernel, self.shard, self.bit, low, sends),
                (struct((rows, columns), bf16),) + (struct((rows, columns // sends), bf16),) * sends,
                self.own,
                *self.received,
            )
        else:
            self.own, send = row_halves(self.total().astype(bf16), self.bit, low, self.shard)
            self.send = jnp.split(send, sends, 1)

    def exchange(self):
        self.received = [swap(v, "rows", self.bit) for v in self.send]

    def step(self, sends=1):
        self.split(sends)
        self.exchange()

    def total(self):
        return self.own.astype(f32) + jnp.concatenate(self.received, 1).astype(f32)

    def finish(self, *columns):
        while self.order:
            self.step()
        outs = tuple(struct((self.own.shape[0], n), f32) for n in columns)
        kernel = functools.partial(finish_kernel, len(self.received))
        return whole(self.name + "_finish", kernel, outs, self.own, *self.received)

    def small_finish(self, bias_shape, *columns):
        while self.order:
            self.step()
        rows = self.own.shape[0]
        outs = tuple(struct((rows, n), f32) for n in columns)
        outs += (struct((rows,), f32),) * 3 + (struct(bias_shape, f32),)
        across = [(i, i ^ 1 ^ (2 * self.bit)) for i in range(2 * lax.axis_size("rows"))]
        return whole(
            self.name + "_finish",
            small_finish_kernel,
            outs,
            self.own,
            *self.received,
            swap(self.own[:, -LANES:], "mp"),
            lax.ppermute(self.send[0][:, -LANES:], ("rows", "mp"), across),
        )


def tie(*values):
    return list(lax.optimization_barrier(values))


def struct(shape, dtype):
    return jax.ShapeDtypeStruct(shape, dtype)


def per_device(
    tokens,
    segment_ids,
    pair_ids,
    bucket_ids,
    attn_gain,
    query_weight,
    key_weight,
    value_weight,
    output_weight,
    bias_table,
    ff_gain,
    up_weight,
    down_weight,
    final_gain,
    proj_weight,
):
    length = tokens.shape[2]
    width = tokens.shape[3]
    inner = query_weight.shape[1]
    hidden = up_weight.shape[1]
    head_count = bias_table.shape[1]
    bucket_count = bias_table.shape[0]
    total_segs = pair_ids.shape[0]
    span = 2 * length
    size = length // CHUNKS
    chunks = range(CHUNKS)
    tower_index = lax.axis_index("tower")
    device_index = tower_index * lax.axis_size("rows") + lax.axis_index("rows")
    shard = width // (2 * lax.axis_size("rows"))

    token_row = tokens.reshape(length, width)
    segments = segment_ids.reshape(1, length)

    part_rows = inner // 2
    fetched = swap(
        lax.dynamic_slice_in_dim(output_weight, tower_index * part_rows, part_rows, 0), "mp"
    )

    normed_one, query, key, value, probs, mix_stored, tok, *mixes = whole(
        "attention",
        attend_kernel,
        (
            stored((length, width), bf16),
            stored((length, inner), bf16),
            stored((length, inner), bf16),
            stored((length, inner), bf16),
            stored((head_count, length, length), bf16),
            stored((length, inner), bf16),
            fixed((length, width), bf16),
        )
        + (fixed((size, inner), bf16),) * CHUNKS,
        token_row,
        query_weight,
        key_weight,
        value_weight,
        attn_gain,
        bias_table.T,
        bucket_ids,
        segments,
        scratch=[
            pltpu.VMEM((3, width, inner), bf16),
            pltpu.VMEM((width,), f32),
            pltpu.VMEM((head_count, bucket_count), f32),
            pltpu.VMEM((span - 1,), jnp.int32),
            pltpu.VMEM((1, length), jnp.int32),
            pltpu.VMEM((length, width), bf16),
            pltpu.VMEM((length, inner), bf16),
            pltpu.VMEM((length, inner), bf16),
            pltpu.VMEM((length, inner), bf16),
            pltpu.VMEM((head_count, length, length), bf16),
            pltpu.VMEM((length, inner), bf16),
            pltpu.VMEM((8, span), f32),
            pltpu.VMEM((length, length), f32),
            pltpu.VMEM((2, BLOCK, span), f32),
            pltpu.VMEM((2, BLOCK, length), f32),
            pltpu.SemaphoreType.DMA((8,)),
            pltpu.SemaphoreType.DMA((5 + inner // BLOCK,)),
        ],
        in_hbm=8,
        mib=24,
    )
    mix_received = [swap(mix, "mp") for mix in mixes]
    fetched, segments = tie(fetched, tie(segments, mixes[-1])[0])
    fetched_too = swap(fetched, "tower")
    output_whole, up_held, down_held, proj_held = whole(
        "load",
        load_kernel,
        (
            fixed((2 * inner, width), bf16),
            fixed((width, hidden), bf16),
            fixed((hidden, width), bf16),
            fixed((width, width), bf16),
        ),
        output_weight,
        up_weight,
        down_weight,
        proj_weight,
        fetched,
        fetched_too,
        scratch=[pltpu.SemaphoreType.DMA((6,))],
        in_hbm=4,
    )

    hidden_one, normed_two, active, slope, ff_part, ff_received = [], [], [], [], [], []
    for c in chunks:
        outs = whole(
            "feed_forward",
            functools.partial(ff_kernel, c),
            (
                fixed((size, width), f32),
                fixed((size, width), bf16),
                fixed((size, hidden), bf16),
                fixed((size, hidden), f32),
                fixed((size, width), bf16),
            ),
            tok,
            output_whole,
            up_held,
            down_held,
            mixes[c],
            mix_received[c],
            ff_gain,
            scratch=[pltpu.VMEM((size, 2 * inner), bf16)],
            in_vmem=5,
        )
        for kept, out in zip((hidden_one, normed_two, active, slope, ff_part), outs):
            kept.append(out)
        ff_received.append(swap(ff_part[c], "mp"))

    hidden_two, pooled = [], []
    for c in chunks:
        h2, total = whole(
            "pool",
            functools.partial(pool_kernel, c),
            (
                fixed((size, width), f32),
                struct((SEGS_ROW, width), bf16 if c == CHUNKS - 1 else f32),
            ),
            hidden_one[c],
            ff_part[c],
            ff_received[c],
            final_gain,
            segments,
            *pooled,
            in_vmem=2,
        )
        hidden_two.append(h2)
        pooled = [total]
    gathered = gather_all(pooled[0])
    loss, proj_grad, pooled_grad = whole(
        "contrast",
        functools.partial(contrast_kernel, total_segs),
        (
            struct((1, 1), f32),
            struct((shard, width), f32),
            struct((SEGS_ROW, width), f32),
        ),
        proj_held,
        gathered,
        pair_ids,
        in_vmem=1,
    )

    two_part, hidden_two_grad, ff_grad, up_out_grad, final_gain_part = whole(
        "feed_forward_back",
        ff_back_kernel,
        (
            fixed((length, width), bf16),
            fixed((length, width), f32),
            fixed((length, width), bf16),
            fixed((length, hidden), bf16),
            struct((1, width), f32),
        ),
        down_held,
        up_held,
        *hidden_two,
        *slope,
        pooled_grad,
        segments,
        final_gain,
        in_vmem=2 + 2 * CHUNKS,
    )
    two_received = swap(two_part, "mp")
    half_shapes = (struct((width // 2, hidden // FF_SENDS), bf16),) * FF_SENDS + (struct((width // 2, hidden), bf16),)
    *halves, own = whole("down_weight", down_weight_kernel, half_shapes, ff_grad, *active, in_vmem=1 + CHUNKS)
    down_scatter = RowsScatter("down_split", shard, own, [swap(v, "tower") for v in halves])
    *halves, own = whole("up_weight", up_weight_kernel, half_shapes, up_out_grad, *normed_two, in_vmem=1 + CHUNKS)
    up_scatter = RowsScatter("up_split", shard, own, [swap(v, "tower") for v in halves], swapped=True)
    down_scatter.step()
    up_scatter.split()
    two_received, down_send, up_scatter.send = tie(
        two_received, down_scatter.send, up_scatter.send
    )
    up_scatter.exchange()
    hidden_one_grad, attn_grad, mix_grad, ff_gain_part, *heads_held = whole(
        "middle_back",
        middle_back_kernel,
        (
            stored((length, width), f32),
            stored((length, width), bf16),
            fixed((length, inner), bf16),
            struct((1, width), f32),
        )
        + (fixed((length, inner), bf16),) * 3
        + (fixed((head_count, length, length), bf16),),
        query,
        key,
        value,
        probs,
        output_whole,
        two_part,
        hidden_two_grad,
        *hidden_one,
        two_received,
        ff_gain,
        scratch=[
            pltpu.VMEM((length, width), f32),
            pltpu.VMEM((length, width), bf16),
            pltpu.SemaphoreType.DMA((4,)),
            pltpu.SemaphoreType.DMA((2,)),
        ],
        in_hbm=4,
        in_vmem=3 + CHUNKS,
    )

    qkv_grads, bias_grad, normed_held, qkv_weight, *halves = whole(
        "attention_back",
        attend_back_kernel,
        (
            fixed((length, 3 * inner), bf16),
            struct((bucket_count, head_count), f32),
            fixed((length, width), bf16),
            fixed((3, width, inner), bf16),
        )
        + (struct((width // 2, 2 * inner // QK_SENDS), bf16),) * QK_SENDS
        + (struct((width // 2, 2 * inner), bf16),),
        query_weight,
        key_weight,
        value_weight,
        normed_one,
        *heads_held,
        mix_grad,
        bucket_ids,
        scratch=[
            pltpu.VMEM((2, length, length), bf16),
            pltpu.VMEM((2, BLOCK, span), f32),
            pltpu.VMEM((8, span), f32),
            pltpu.VMEM((2, BLOCK, length), f32),
            pltpu.SemaphoreType.DMA((4,)),
        ],
        in_hbm=4,
        in_vmem=5,
    )
    first_scatter = RowsScatter("query_key_split", shard, halves[-1], [swap(v, "tower") for v in halves[:-1]])
    qkv_grads, down_scatter.received, up_scatter.received = tie(
        qkv_grads, down_scatter.received, up_scatter.received
    )
    down_scatter.split()
    up_scatter.split()
    first_scatter.split()
    qkv_grads = tie(qkv_grads, down_scatter.send, up_scatter.send, first_scatter.send)[0]
    down_scatter.exchange()
    up_scatter.exchange()
    first_scatter.exchange()
    one_part, one_own, *halves, own = whole(
        "project_back",
        functools.partial(project_back_kernel, shard),
        (struct((length, width), bf16), stored((length, width), bf16))
        + (struct((width // 2, 2 * inner // VO_SENDS), bf16),) * VO_SENDS
        + (struct((width // 2, LANES), bf16), struct((width // 2, 2 * inner + LANES), bf16)),
        mix_stored,
        attn_grad,
        qkv_weight,
        tok,
        normed_held,
        qkv_grads,
        bias_grad,
        ff_gain_part,
        final_gain_part,
        scratch=[
            pltpu.VMEM((width, LANES), f32),
            pltpu.VMEM((length, inner), bf16),
            pltpu.VMEM((length, width), bf16),
            pltpu.SemaphoreType.DMA((3,)),
        ],
        in_hbm=2,
        in_vmem=4,
    )
    one_received = swap(one_part, "mp")
    down_scatter.split()
    up_scatter.split()
    halves = tie(halves, down_scatter.send, up_scatter.send)[0]
    down_scatter.exchange()
    up_scatter.exchange()
    second_scatter = RowsScatter(
        "value_output_split", shard, own, [swap(v, "tower") for v in halves], swapped=True
    )
    second_scatter.step()
    first_scatter.received, second_scatter.received, down_scatter.received = tie(
        first_scatter.received, second_scatter.received, down_scatter.received
    )
    first_scatter.step()
    second_scatter.step()
    tokens_grad = whole(
        "last",
        last_kernel,
        struct((length, width), f32),
        one_own,
        hidden_one_grad,
        tok,
        attn_gain,
        one_received,
        scratch=[
            pltpu.VMEM((length, width), bf16),
            pltpu.VMEM((length, width), f32),
            pltpu.SemaphoreType.DMA((2,)),
        ],
        in_hbm=2,
        in_vmem=1,
    )
    first_scatter.received, second_scatter.received, down_scatter.received, up_scatter.received, tokens_grad = tie(
        first_scatter.received, second_scatter.received, down_scatter.received, up_scatter.received, tokens_grad
    )
    first_scatter.step()
    second_scatter.step()
    (down_sum,) = down_scatter.finish(hidden)
    (up_sum,) = up_scatter.finish(hidden)
    bias_pieces = -(-bucket_count // shard)
    value_sum, output_sum, attn_gain_sum, ff_gain_sum, final_gain_sum, turned = second_scatter.small_finish(
        (head_count * bias_pieces, min(shard, bucket_count)), inner, inner
    )
    query_sum, key_sum = first_scatter.finish(inner, inner)
    bias_rows = [turned[g * head_count : (g + 1) * head_count, :] for g in range(bias_pieces)]
    bias_total = jnp.concatenate(bias_rows, 1)[:, :bucket_count].T
    return (
        loss[0, 0],
        tokens_grad.reshape(tokens.shape),
        attn_gain_sum,
        query_sum,
        key_sum,
        value_sum,
        output_sum.T,
        bias_total,
        ff_gain_sum,
        up_sum,
        down_sum.T,
        final_gain_sum,
        proj_grad,
    )


def solution(mesh):
    in_specs = (
        P("tower", "rows", None, None),
        P("tower", "rows", None),
        P(),
        P(),
        P(),
        P(None, "mp"),
        P(None, "mp"),
        P(None, "mp"),
        P("mp", None),
        P(None, "mp"),
        P(),
        P(None, "mp"),
        P("mp", None),
        P(),
        P(),
    )
    out_specs = (
        P(),
        P("tower", "rows", None, None),
        P(("tower", "rows")),
        P(("tower", "rows"), "mp"),
        P(("tower", "rows"), "mp"),
        P(("tower", "rows"), "mp"),
        P("mp", ("tower", "rows")),
        P(None, "mp"),
        P(("tower", "rows")),
        P(("tower", "rows"), "mp"),
        P("mp", ("tower", "rows")),
        P(("tower", "rows")),
        P(("tower", "rows"), None),
    )
    return jax.shard_map(
        per_device, mesh=mesh, in_specs=in_specs, out_specs=out_specs, check_vma=False
    )
```

```python
import functools

import jax
import jax.numpy as jnp
from jax import lax
from jax.experimental import pallas as pl
from jax.experimental.pallas import tpu as pltpu
from jax.sharding import PartitionSpec as P

SEGS_ROW = 8
BLOCK = 128
STRIP = 32
STEP = 384
LANES = 128
DOWN_SENDS, UP_SENDS = 4, 8
CHUNKS = 2

eps = 1e-06
logit_scale = 50.0
highest = lax.Precision.HIGHEST
f32 = jnp.float32
bf16 = jnp.bfloat16


def inv_rms(values):
    return lax.rsqrt(jnp.mean(values * values, -1, keepdims=True) + eps)


def dot_nn(a, b):
    return lax.dot_general(a, b, (((1,), (0,)), ((), ())), preferred_element_type=f32)


def dot_nt(a, b):
    return lax.dot_general(a, b, (((1,), (1,)), ((), ())), preferred_element_type=f32)


def dot_tn(a, b):
    return lax.dot_general(a, b, (((0,), (0,)), ((), ())), preferred_element_type=f32)


def gelu_parts(values):
    size = jnp.abs(values)
    bell = jnp.exp(-0.5 * values * values)
    t = 1.0 / (1.0 + (0.3275911 * 0.7071067811865476) * size)
    poly = t * (
        0.127414796
        + t * (-0.142248368 + t * (0.7107068705 + t * (-0.7265760135 + t * 0.5307027145)))
    )
    tail = poly * bell
    return bell, jnp.where(values >= 0, 1.0 - tail, tail)


def key_range(block, blocks):
    return max(0, block - 2), min(blocks, block + 3)


def split_low(values, parts):
    out = []
    for _ in range(parts):
        out.append(values.astype(bf16))
        values = values - out[-1].astype(f32)
    return out


def norm_back(values, inv, gain, grad):
    scaled = grad * gain
    inner_mean = jnp.mean(values * scaled, -1, keepdims=True)
    return inv * scaled - values * (inv * inv * inv * inner_mean)


def row_gain(gain_ref):
    return gain_ref[...].reshape(1, gain_ref.shape[0])


def attend_kernel(
    tok_hbm, wq_hbm, wk_hbm, wv_hbm, gain_hbm, table_hbm, ids_hbm, seg_hbm,
    n1_hbm, q_hbm, k_hbm, v_hbm, probs_hbm, mix_hbm, tok_ref, *rest,
):
    mix_refs = rest[:CHUNKS]
    (
        w_ref, gain_ref, table_ref, ids_ref, seg_ref, n1_ref, q_ref, k_ref, v_ref, probs_ref, mix_ref,
        rel_ref, mask_ref, skew_ref, score_ref, sems, out_sems,
    ) = rest[CHUNKS:]
    length, inner = q_ref.shape
    blocks = length // BLOCK
    heads, buckets = table_ref.shape
    pairs = inner // BLOCK
    span = rel_ref.shape[1]
    copies = start_copies(
        sems,
        (tok_hbm, tok_ref),
        (wq_hbm, w_ref.at[0]),
        (wk_hbm, w_ref.at[1]),
        (wv_hbm, w_ref.at[2]),
        (gain_hbm, gain_ref),
        (table_hbm, table_ref),
        (ids_hbm, ids_ref),
        (seg_hbm, seg_ref),
    )
    for copy in copies[4:]:
        copy.wait()
    hot = (
        lax.broadcasted_iota(jnp.int32, (buckets, span - 1), 0)
        == ids_ref[...].reshape(1, span - 1)
    ).astype(f32)
    rel_ref[...] = jnp.zeros_like(rel_ref)
    rel_ref[0:heads, 0 : span - 1] = lax.dot_general(
        table_ref[...], hot, (((1,), (0,)), ((), ())), precision=highest, preferred_element_type=f32
    )
    seg_row = seg_ref[...].astype(f32)
    for b in range(blocks):
        own = jnp.broadcast_to(seg_row[:, b * BLOCK : (b + 1) * BLOCK], (BLOCK, BLOCK)).T
        for c in range(blocks):
            other = jnp.broadcast_to(seg_row[:, c * BLOCK : (c + 1) * BLOCK], (BLOCK, BLOCK))
            mask_ref[b * BLOCK : (b + 1) * BLOCK, c * BLOCK : (c + 1) * BLOCK] = jnp.where(
                own == other, 0.0, -1e30
            )
    copies[0].wait()
    gain = row_gain(gain_ref)
    for at in range(0, length, STRIP):
        x = tok_ref[at : at + STRIP, :].astype(f32)
        n1_ref[at : at + STRIP, :] = (x * inv_rms(x) * gain).astype(bf16)
    n1 = n1_ref[...]
    for i, out_ref in enumerate((q_ref, k_ref, v_ref)):
        copies[1 + i].wait()
        out_ref[...] = dot_nn(n1, w_ref[i]).astype(bf16)
    outs = start_copies(out_sems, (n1_ref, n1_hbm), (q_ref, q_hbm), (k_ref, k_hbm), (v_ref, v_hbm))

    def probs_copy(pair):
        heads_of = pl.ds(2 * pair, 2)
        return pltpu.make_async_copy(probs_ref.at[heads_of], probs_hbm.at[heads_of], out_sems.at[4 + pair])

    low_lanes = lax.broadcasted_iota(jnp.int32, (BLOCK, BLOCK), 1) < BLOCK // 2
    zero = jnp.zeros((BLOCK, BLOCK), bf16)

    @pl.loop(0, pairs)
    def _(pair):
        lanes = pl.ds(pl.multiple_of(pair * BLOCK, BLOCK), BLOCK)
        for h in range(2):
            row = jnp.broadcast_to(rel_ref[pl.ds(pair * 2 + h, 1), :], (BLOCK, span))
            skew_ref[h] = pltpu.roll(row, span - (BLOCK - 1), 1, stride=1, stride_axis=0)
        for b in range(blocks):
            first, last = key_range(b, blocks)
            rows = slice(b * BLOCK, (b + 1) * BLOCK)
            keys = slice(first * BLOCK, last * BLOCK)
            shift = length - BLOCK - b * BLOCK
            q_pair = q_ref[rows, lanes]
            k_pair = k_ref[keys, lanes]
            v_pair = v_ref[keys, lanes]
            width = (last - first) * BLOCK
            for h in range(2):
                q_one = jnp.where(low_lanes if h == 0 else ~low_lanes, q_pair, zero)
                score_ref[h, :, :width] = dot_nt(q_one, k_pair)
            for at in range(0, BLOCK, STRIP):
                part = slice(b * BLOCK + at, b * BLOCK + at + STRIP)
                for h in range(2):
                    head = pair * 2 + h
                    scores = (
                        score_ref[h, at : at + STRIP, :width]
                        + skew_ref[h, at : at + STRIP, shift + first * BLOCK : shift + last * BLOCK]
                        + mask_ref[part, keys]
                    )
                    raised = jnp.exp(scores - jnp.max(scores, -1, keepdims=True))
                    scale = 1.0 / jnp.sum(raised, -1, keepdims=True)
                    probs_ref[head, part, keys] = (raised * scale).astype(bf16)
                    if first > 0:
                        probs_ref[head, part, 0 : first * BLOCK] = jnp.zeros((STRIP, first * BLOCK), bf16)
                    if last < blocks:
                        probs_ref[head, part, last * BLOCK :] = jnp.zeros(
                            (STRIP, length - last * BLOCK), bf16
                        )
            mix_ref[rows, lanes] = jnp.where(
                low_lanes,
                dot_nn(probs_ref[pair * 2, rows, keys], v_pair),
                dot_nn(probs_ref[pair * 2 + 1, rows, keys], v_pair),
            ).astype(bf16)
        probs_copy(pair).start()

    outs += start_copies(out_sems.at[4 + pairs :], (mix_ref, mix_hbm))
    for i, part in enumerate(mix_refs):
        part[...] = mix_ref[i * part.shape[0] : (i + 1) * part.shape[0], :]
    for copy in outs:
        copy.wait()
    for pair in range(pairs):
        probs_copy(pair).wait()


def load_kernel(
    wo_hbm, up_hbm, down_hbm, proj_hbm, fetched_hbm, fetched_too_hbm, wo_ref, up_ref, down_ref, proj_ref, sems
):
    me, tower_index = lax.axis_index("mp"), lax.axis_index("tower")
    inner = wo_hbm.shape[0]
    piece = inner // 2
    own_at = pl.multiple_of(me * inner, inner)
    other_at = (1 - me) * inner
    copies = start_copies(
        sems,
        (wo_hbm, wo_ref.at[pl.ds(own_at, inner), :]),
        (fetched_hbm, wo_ref.at[pl.ds(pl.multiple_of(other_at + tower_index * piece, piece), piece), :]),
        (fetched_too_hbm, wo_ref.at[pl.ds(pl.multiple_of(other_at + (1 - tower_index) * piece, piece), piece), :]),
        (up_hbm, up_ref),
        (down_hbm, down_ref),
        (proj_hbm, proj_ref),
    )
    for copy in copies:
        copy.wait()


def ff_kernel(
    chunk, tok_ref, wo_ref, up_ref, down_ref, mix_own, mix_other, gain_ref,
    h1_ref, n2_ref, a_ref, slope_ref, part_ref,
    mix_ref,
):
    size, width = h1_ref.shape
    inner = mix_own.shape[1]
    hidden = up_ref.shape[1]
    step = 256
    me = lax.axis_index("mp")
    mix_ref[:, pl.ds(pl.multiple_of(me * inner, inner), inner)] = mix_own[...]
    mix_ref[:, pl.ds(pl.multiple_of((1 - me) * inner, inner), inner)] = mix_other[...]
    h1_ref[...] = dot_nn(mix_ref[...], wo_ref[...])
    gain = row_gain(gain_ref)
    for at in range(0, size, STRIP):
        rows = slice(at, at + STRIP)
        h1 = tok_ref[chunk * size + at : chunk * size + at + STRIP, :].astype(f32) + h1_ref[rows, :]
        h1_ref[rows, :] = h1
        n2_ref[rows, :] = (h1 * inv_rms(h1) * gain).astype(bf16)
    n2 = n2_ref[...]
    for at in range(0, hidden, step):
        cols = slice(at, at + step)
        slope_ref[:, cols] = dot_nn(n2, up_ref[:, cols])
        for r in range(0, size, STRIP):
            rows = slice(r, r + STRIP)
            u = slope_ref[rows, cols]
            bell, below = gelu_parts(u)
            a_ref[rows, cols] = (u * below).astype(bf16)
            slope_ref[rows, cols] = below + u * bell * 0.3989422804014327
    part_ref[...] = dot_nn(a_ref[...], down_ref[...]).astype(bf16)


def pool_kernel(chunk, h1_ref, own_ref, rec_ref, gain_ref, seg_ref, *rest):
    total_ref = rest[0] if chunk > 0 else None
    h2_ref, out_ref = rest[-2:]
    size, width = h1_ref.shape
    gain = row_gain(gain_ref)
    number = lax.broadcasted_iota(jnp.int32, (SEGS_ROW, 1), 0)
    total = jnp.zeros((SEGS_ROW, width), f32)
    step = 128
    for at in range(0, size, step):
        rows = slice(at, at + step)
        h2 = h1_ref[rows, :] + (own_ref[rows, :].astype(f32) + rec_ref[rows, :].astype(f32))
        h2_ref[rows, :] = h2
        member = (seg_ref[:, chunk * size + at : chunk * size + at + step] == number).astype(f32).astype(bf16)
        for piece in split_low(h2 * inv_rms(h2) * gain, 2):
            total += dot_nn(member, piece)
    if chunk > 0:
        total += total_ref[...]
    if chunk == CHUNKS - 1:
        counts = jnp.sum((seg_ref[...] == number).astype(f32), -1, keepdims=True)
        total = total / counts
    out_ref[...] = total.astype(out_ref.dtype)


def contrast_kernel(
    total_segs, proj_ref, gathered_ref, pair_ref, loss_ref, dproj_ref, own_ref
):
    me = lax.axis_index("tower") * lax.axis_size("rows") + lax.axis_index("rows")
    count = gathered_ref.shape[0]
    row = lax.broadcasted_iota(jnp.int32, (count, count), 0)
    col = lax.broadcasted_iota(jnp.int32, (count, count), 1)
    order = (col == (row ^ (me * SEGS_ROW))).astype(f32).astype(bf16)
    pooled = dot_nn(order, gathered_ref[...]).astype(bf16)
    e = dot_nn(pooled, proj_ref[...])
    inv = lax.rsqrt(jnp.sum(e * e, -1, keepdims=True) + eps)
    unit = e * inv
    unit_low = unit.astype(bf16)
    zq, zd = unit_low[:total_segs], unit_low[total_segs:]
    logits = logit_scale * dot_nt(zd, zq)
    positive = (
        lax.broadcasted_iota(jnp.int32, (total_segs, total_segs), 0)
        == pair_ref[...].reshape(1, total_segs)
    ).astype(f32)
    norms, shares = [], []
    for axis in (0, 1):
        most = jnp.max(logits, axis, keepdims=True)
        raised = jnp.exp(logits - most)
        total = jnp.sum(raised, axis, keepdims=True)
        norms.append(jnp.log(total) + most)
        shares.append(raised / total)
    half_share = 0.5 / total_segs
    ends = jnp.sum(norms[0], 1, keepdims=True) + jnp.sum(norms[1], 0, keepdims=True)
    hits = jnp.sum(jnp.sum(logits * positive, 1, keepdims=True), 0, keepdims=True)
    loss_ref[...] = half_share * (ends - 2.0 * hits)
    grad = (half_share * (shares[0] + shares[1] - 2.0 * positive)).astype(bf16)
    dz = logit_scale * jnp.concatenate([dot_tn(grad, zd), dot_nn(grad, zq)], 0)
    de = ((dz - unit * jnp.sum(unit * dz, -1, keepdims=True)) * inv).astype(bf16)
    width, shard = proj_ref.shape[0], dproj_ref.shape[0]
    row = lax.broadcasted_iota(jnp.int32, (width, shard), 0)
    col = lax.broadcasted_iota(jnp.int32, (width, shard), 1)
    columns = (row == col + me * shard).astype(f32).astype(bf16)
    dproj_ref[...] = dot_tn(dot_nn(pooled, columns).astype(bf16), de)
    row = lax.broadcasted_iota(jnp.int32, (SEGS_ROW, count), 0)
    col = lax.broadcasted_iota(jnp.int32, (SEGS_ROW, count), 1)
    mine = (col == row + me * SEGS_ROW).astype(f32).astype(bf16)
    own_ref[...] = dot_nt(dot_nn(mine, de).astype(bf16), proj_ref[...])


def ff_back_kernel(down_ref, up_ref, *refs):
    h2_refs, slope_refs, refs = refs[:CHUNKS], refs[CHUNKS : 2 * CHUNKS], refs[2 * CHUNKS :]
    dpool_ref, seg_ref, gain_ref, part_ref, dh2_ref, df_ref, du_ref, dgain_ref = refs
    length, width = dh2_ref.shape
    size = length // CHUNKS
    hidden = down_ref.shape[0]
    step = 256
    gain = row_gain(gain_ref)
    number = lax.broadcasted_iota(jnp.int32, (SEGS_ROW, 1), 0)
    counts = jnp.sum((seg_ref[...] == number).astype(f32), -1, keepdims=True)
    pieces = jnp.concatenate([p.astype(f32) for p in split_low(dpool_ref[...] / counts, 4)], 0).astype(bf16)
    member = (seg_ref[...] == number).astype(f32)
    member = jnp.concatenate([member] * 4, 0).astype(bf16)
    dh2_ref[...] = dot_tn(member, pieces)
    dgain = jnp.zeros((1, width), f32)
    for at in range(0, length, STRIP):
        rows = slice(at, at + STRIP)
        h2 = h2_refs[at // size][at % size : at % size + STRIP, :]
        grad = dh2_ref[rows, :]
        inv = inv_rms(h2)
        dh2 = norm_back(h2, inv, gain, grad)
        dgain += jnp.sum(h2 * inv * grad, 0, keepdims=True)
        dh2_ref[rows, :] = dh2
        df_ref[rows, :] = dh2.astype(bf16)
    dgain_ref[...] = dgain
    df = df_ref[...]
    for at in range(0, hidden, step):
        cols = slice(at, at + step)
        da = dot_nt(df, down_ref[cols, :])
        for c in range(CHUNKS):
            rows = slice(c * size, (c + 1) * size)
            du_ref[rows, cols] = (da[rows, :] * slope_refs[c][:, cols]).astype(bf16)
    part_ref[...] = dot_nt(du_ref[...], up_ref[...]).astype(bf16)


def down_weight_kernel(df_ref, *refs):
    size = refs[0].shape[0]
    weight_products([df_ref.at[c * size : (c + 1) * size, :] for c in range(CHUNKS)], refs[:CHUNKS], refs[CHUNKS:-1], refs[-1])


def up_weight_kernel(du_ref, *refs):
    size = refs[0].shape[0]
    weight_products(refs[:CHUNKS], [du_ref.at[c * size : (c + 1) * size, :] for c in range(CHUNKS)], refs[CHUNKS:-1], refs[-1])


def middle_back_kernel(*refs):
    ahead, refs = refs[:4], refs[4:]
    wo_ref, own_ref, dh2_ref, *refs = refs
    h1_refs, refs = refs[:CHUNKS], refs[CHUNKS:]
    rec_ref, gain_ref, dh1_ref, da_hbm, dmix_ref, dgain_ref, *refs = refs
    held, (da_ref, sems, out_sems) = refs[:4], refs[4:]
    copies = start_copies(sems, *zip(ahead, held))
    length, width = dh1_ref.shape
    size = length // CHUNKS
    gain = row_gain(gain_ref)
    dgain = jnp.zeros((1, width), f32)
    for at in range(0, length, STRIP):
        rows = slice(at, at + STRIP)
        h1 = h1_refs[at // size][at % size : at % size + STRIP, :]
        grad = own_ref[rows, :].astype(f32) + rec_ref[rows, :].astype(f32)
        inv = inv_rms(h1)
        dh1 = dh2_ref[rows, :] + norm_back(h1, inv, gain, grad)
        dgain += jnp.sum(h1 * inv * grad, 0, keepdims=True)
        dh1_ref[rows, :] = dh1
        da_ref[rows, :] = dh1.astype(bf16)
    dgain_ref[...] = dgain
    copies += start_copies(out_sems, (da_ref, da_hbm))
    inner = dmix_ref.shape[1]
    own_at = pl.multiple_of(lax.axis_index("mp") * inner, inner)
    dmix_ref[...] = dot_nt(da_ref[...], wo_ref[pl.ds(own_at, inner), :]).astype(bf16)
    for copy in copies:
        copy.wait()


def attend_back_kernel(
    shard, wq_hbm, wk_hbm, wv_hbm, n1_hbm, mix_hbm, da_hbm, q_ref, k_ref, v_ref, probs_ref, mixg_ref, tok_ref,
    ids_ref, ff_gain, final_gain,
    part_ref, qk_other, qk_own, vo_other, vo_own,
    grads_ref, n1_ref, w_ref, mix_ref, da_ref, all_ref, biasg_ref, ds_ref, skew_ref, rel_ref, dp_ref, sems,
):
    length, inner = q_ref.shape
    blocks = length // BLOCK
    pairs = inner // BLOCK
    span = rel_ref.shape[1]
    later = start_copies(
        sems,
        (wq_hbm, w_ref.at[0]),
        (wk_hbm, w_ref.at[1]),
        (wv_hbm, w_ref.at[2]),
        (n1_hbm, n1_ref),
        (mix_hbm, mix_ref),
        (da_hbm, da_ref),
    )
    low_lanes = lax.broadcasted_iota(jnp.int32, (BLOCK, BLOCK), 1) < BLOCK // 2
    low_all = lax.broadcasted_iota(jnp.int32, (length, BLOCK), 1) < BLOCK // 2
    zero = jnp.zeros((BLOCK, BLOCK), bf16)
    rel_ref[...] = jnp.zeros_like(rel_ref)

    @pl.loop(0, pairs)
    def _(pair):
        lanes = pl.ds(pl.multiple_of(pair * BLOCK, BLOCK), BLOCK)
        skew_ref[...] = jnp.zeros_like(skew_ref)
        for b in range(blocks):
            first, last = key_range(b, blocks)
            rows = slice(b * BLOCK, (b + 1) * BLOCK)
            keys = slice(first * BLOCK, last * BLOCK)
            shift = length - BLOCK - b * BLOCK
            g_pair = mixg_ref[rows, lanes]
            k_pair = k_ref[keys, lanes]
            v_pair = v_ref[keys, lanes]
            width = (last - first) * BLOCK
            for h in range(2):
                g_one = jnp.where(low_lanes if h == 0 else ~low_lanes, g_pair, zero)
                dp_ref[h, :, :width] = dot_nt(g_one, v_pair)
            for at in range(0, BLOCK, STRIP):
                part = slice(b * BLOCK + at, b * BLOCK + at + STRIP)
                for h in range(2):
                    probs = probs_ref[pair * 2 + h, part, keys].astype(f32)
                    weighted = probs * dp_ref[h, at : at + STRIP, :width]
                    ds = weighted - probs * jnp.sum(weighted, -1, keepdims=True)
                    ds_ref[h, part, keys] = ds.astype(bf16)
                    if first > 0:
                        ds_ref[h, part, 0 : first * BLOCK] = jnp.zeros((STRIP, first * BLOCK), bf16)
                    if last < blocks:
                        ds_ref[h, part, last * BLOCK :] = jnp.zeros((STRIP, length - last * BLOCK), bf16)
                    skew_ref[h, at : at + STRIP, shift + first * BLOCK : shift + last * BLOCK] += ds
            grads_ref[rows, lanes] = jnp.where(
                low_lanes,
                dot_nn(ds_ref[0, rows, keys], k_pair),
                dot_nn(ds_ref[1, rows, keys], k_pair),
            ).astype(bf16)
        q_pair = q_ref[:, lanes]
        g_pair = mixg_ref[:, lanes]
        k_lanes = pl.ds(pl.multiple_of(inner + pair * BLOCK, BLOCK), BLOCK)
        v_lanes = pl.ds(pl.multiple_of(2 * inner + pair * BLOCK, BLOCK), BLOCK)
        grads_ref[:, k_lanes] = jnp.where(
            low_all, dot_tn(ds_ref[0], q_pair), dot_tn(ds_ref[1], q_pair)
        ).astype(bf16)
        grads_ref[:, v_lanes] = jnp.where(
            low_all,
            dot_tn(probs_ref[pair * 2], g_pair),
            dot_tn(probs_ref[pair * 2 + 1], g_pair),
        ).astype(bf16)
        for h in range(2):
            tiles = skew_ref[h, BLOCK - 8 :, :]
            for r in range(0, BLOCK - 8, 8):
                tiles += pltpu.roll(skew_ref[h, r : r + 8, :], BLOCK - 8 - r, 1)
            line = tiles[7:8, :]
            for r in range(7):
                line += pltpu.roll(tiles[r : r + 1, :], 7 - r, 1)
            rel_ref[pl.ds(pair * 2 + h, 1), :] = line

    hot = (
        lax.broadcasted_iota(jnp.int32, (biasg_ref.shape[0], span - 1), 0)
        == ids_ref[...].reshape(1, span - 1)
    ).astype(f32)
    total = lax.dot_general(
        hot, rel_ref[:, : span - 1], (((1,), (1,)), ((), ())), precision=highest, preferred_element_type=f32
    )
    biasg_ref[...] = total[:, : biasg_ref.shape[1]]
    for copy in later:
        copy.wait()
    part_ref[...] = (
        dot_nt(grads_ref[:, :inner], w_ref[0])
        + dot_nt(grads_ref[:, inner : 2 * inner], w_ref[1])
        + dot_nt(grads_ref[:, 2 * inner :], w_ref[2])
    ).astype(bf16)
    weight_products([n1_ref], [grads_ref.at[:, : 2 * inner]], [qk_other], qk_own)
    width = n1_ref.shape[1]
    dgain = jnp.zeros((1, width), f32)
    for at in range(0, length, STRIP):
        rows = slice(at, at + STRIP)
        x = tok_ref[rows, :].astype(f32)
        dgain += jnp.sum(x * inv_rms(x) * part_ref[rows, :].astype(f32), 0, keepdims=True)
    weight_products([n1_ref], [grads_ref.at[:, 2 * inner :]], [vo_other], vo_own)
    weight_products([da_ref], [mix_ref], [vo_other], vo_own, inner)
    small_columns(shard, biasg_ref, [dgain, ff_gain[...], final_gain[...]], all_ref)
    tower_index = lax.axis_index("tower")
    half = width // 2
    for which, out_ref in ((1 - tower_index, qk_other), (tower_index, qk_own)):
        rows = pl.ds(pl.multiple_of(which * half, half), half)
        out_ref[:, 2 * inner :] = all_ref[rows, :].astype(bf16)


def last_kernel(tok_ref, own_ref, dh1_ref, gain_ref, rec_ref, out_hbm, out_ref, sems):
    gain = row_gain(gain_ref)
    length = own_ref.shape[0]
    copies = []
    for at in range(0, length, STRIP):
        rows = slice(at, at + STRIP)
        x = tok_ref[rows, :].astype(f32)
        grad = own_ref[rows, :].astype(f32) + rec_ref[rows, :].astype(f32)
        out_ref[rows, :] = dh1_ref[rows, :] + norm_back(x, inv_rms(x), gain, grad)
        if (at + STRIP) % BLOCK == 0:
            done = pl.ds(at + STRIP - BLOCK, BLOCK)
            copies += start_copies(sems.at[len(copies) :], (out_ref.at[done, :], out_hbm.at[done, :]))
    for copy in copies:
        copy.wait()


def weight_products(lefts, rights, other_refs, own_ref, columns=0):
    tower_index = lax.axis_index("tower")
    half = lefts[0].shape[1] // 2
    each = other_refs[0].shape[1]
    for which in (1 - tower_index, tower_index):
        lanes = pl.ds(pl.multiple_of(which * half, half), half)
        turned = [left[:, lanes].T for left in lefts]
        for at in range(0, rights[0].shape[1], STEP):
            total = None
            for left, right in zip(turned, rights):
                term = dot_nn(left, right[:, at : at + STEP])
                total = term if total is None else total + term
            total = total.astype(bf16)
            there = columns + at
            if which is tower_index:
                own_ref[:, there : there + STEP] = total
                continue
            for i, other_ref in enumerate(other_refs):
                begin, end = max(there, i * each), min(there + STEP, (i + 1) * each)
                if begin < end:
                    other_ref[:, begin - i * each : end - i * each] = total[:, begin - there : end - there]


def small_columns(shard, bias_ref, lines, all_ref):
    width = all_ref.shape[0]
    buckets, heads = bias_ref.shape
    lane = lax.broadcasted_iota(jnp.int32, (1, LANES), 1)

    def low(values):
        return values.astype(f32).astype(bf16)

    row = lax.broadcasted_iota(jnp.int32, (width, buckets), 0) % shard
    col = lax.broadcasted_iota(jnp.int32, (width, buckets), 1)
    total = jnp.zeros((width, LANES), f32)
    for g in range(-(-buckets // shard)):
        place = lax.broadcasted_iota(jnp.int32, (heads, LANES), 0) + 3 + g * heads == lane
        total += dot_nn(low(col == row + g * shard), low(dot_nn(low(bias_ref[...]), low(place))))
    place = lax.broadcasted_iota(jnp.int32, (3, LANES), 0) == lane
    all_ref[...] = total + dot_tn(low(jnp.concatenate(lines, 0)), low(place))


def finish_kernel(pieces, own_ref, *refs):
    rec_refs, out_refs = refs[:pieces], refs[pieces:]
    at = 0
    for out_ref, rec_ref in zip(out_refs, rec_refs if pieces > 1 else [rec_refs[0]] * len(out_refs)):
        cols = slice(at, at + out_ref.shape[1])
        at = cols.stop
        out_ref[...] = own_ref[:, cols].astype(f32) + rec_ref[:, cols].astype(f32)


def small_finish_kernel(own_ref, rec_ref, *out_refs):
    finish_kernel(1, own_ref, rec_ref, *out_refs[:-4])
    *gain_refs, bias_ref = out_refs[-4:]
    at = own_ref.shape[1] - LANES
    values = own_ref[:, at:].astype(f32) + rec_ref[:, at:].astype(f32)
    eye = (
        lax.broadcasted_iota(jnp.int32, (LANES, LANES), 0) == lax.broadcasted_iota(jnp.int32, (LANES, LANES), 1)
    ).astype(f32)
    turned = lax.dot_general(
        eye, values, (((1,), (1,)), ((), ())), precision=highest, preferred_element_type=f32
    )
    for i, gain_ref in enumerate(gain_refs):
        gain_ref[...] = turned[i, :]
    bias_ref[...] = turned[3 : 3 + bias_ref.shape[0], : bias_ref.shape[1]]


def gain_finish_kernel(own_ref, rec_ref, gain_own, gain_rec, *out_refs):
    finish_kernel(1, own_ref, rec_ref, *out_refs[:-1])
    out_refs[-1][...] = gain_own[...] + gain_rec[...]


def two_finish_kernel(own_ref, rec_ref, own_too, rec_too, out_ref, out_too):
    finish_kernel(1, own_ref, rec_ref, out_ref)
    finish_kernel(1, own_too, rec_too, out_too)


def split_kernel(shard, bit, low, sends, own_ref, *refs):
    rec_refs, keep_ref, send_refs = refs[: -1 - sends], refs[-1 - sends], refs[-sends:]
    own_bit = lax.axis_index("rows") // bit % 2
    each = send_refs[0].shape[1]
    at = 0
    for rec_ref in rec_refs:
        columns = rec_ref.shape[1]
        for j in range(keep_ref.shape[0] // shard):
            there = slice(j * shard, (j + 1) * shard)
            for which in (own_bit, 1 - own_bit):
                start = ((j // low * 2 + which) * low + j % low) * shard
                rows = pl.ds(pl.multiple_of(start, shard), shard)
                total = (
                    own_ref[rows, at : at + columns].astype(f32) + rec_ref[rows, :].astype(f32)
                ).astype(bf16)
                if which is own_bit:
                    keep_ref[there, at : at + columns] = total
                    continue
                for i, send_ref in enumerate(send_refs):
                    begin, end = max(at, i * each), min(at + columns, (i + 1) * each)
                    if begin < end:
                        send_ref[there, begin - i * each : end - i * each] = total[:, begin - at : end - at]
        at += columns


def fixed(shape, dtype):
    return pltpu.VMEM(shape, dtype)


def stored(shape, dtype):
    return pltpu.HBM(shape, dtype)


def whole(name, kernel, out_shapes, *args, scratch=(), in_hbm=0, in_vmem=0, mib=16):
    args = (
        [pltpu.with_memory_space_constraint(v, pltpu.HBM) for v in args[:in_hbm]]
        + [pltpu.with_memory_space_constraint(v, pltpu.VMEM) for v in args[in_hbm : in_hbm + in_vmem]]
        + list(args[in_hbm + in_vmem :])
    )
    vmem = pl.BlockSpec(memory_space=pltpu.VMEM)
    hbm = pl.BlockSpec(memory_space=pl.ANY)
    is_stored = lambda out: getattr(out, "memory_space", None) == pltpu.HBM
    with jax.named_scope(name):
        return pl.pallas_call(
            kernel,
            out_shape=out_shapes,
            in_specs=[hbm] * in_hbm + [vmem] * (len(args) - in_hbm),
            out_specs=jax.tree.map(lambda out: hbm if is_stored(out) else vmem, out_shapes),
            scratch_shapes=scratch,
            compiler_params=pltpu.CompilerParams(vmem_limit_bytes=mib * 1024 * 1024),
            cost_estimate=pl.CostEstimate(flops=1, bytes_accessed=1, transcendentals=0),
        )(*args)


def start_copies(sems, *pairs):
    copies = [pltpu.make_async_copy(src, dst, sems.at[i]) for i, (src, dst) in enumerate(pairs)]
    for copy in copies:
        copy.start()
    return copies


def swap(values, axis, bit=1):
    count = lax.axis_size(axis)
    return lax.ppermute(values, axis, [(i, i ^ bit) for i in range(count)])


def gather_all(values):
    bits = [1 << i for i in range(lax.axis_size("rows").bit_length() - 1)]
    steps = [bits[:1]] + [bits[i : i + 2] for i in range(1, len(bits), 2)]
    for step in steps:
        masks = step + ([step[0] | step[1]] if len(step) > 1 else [])
        values = jnp.concatenate([values] + [swap(values, "rows", mask) for mask in masks], 0)
    return jnp.concatenate([values, swap(values, "tower")], 0)


def row_halves(cur, bit, low, shard):
    columns = cur.shape[-1]
    view = cur.reshape(-1, 2, low * shard, columns)
    own_bit = (lax.axis_index("rows") & bit) // bit
    keep = lax.dynamic_index_in_dim(view, own_bit, 1, False).reshape(-1, columns)
    send = lax.dynamic_index_in_dim(view, 1 - own_bit, 1, False).reshape(-1, columns)
    return keep, send


class RowsScatter:
    def __init__(self, name, shard, own, received, swapped=False):
        self.name, self.shard = name, shard
        self.own, self.received = own, received
        self.bits = [1 << i for i in range(lax.axis_size("rows").bit_length() - 1)]
        self.order = list(self.bits)
        if swapped and len(self.order) > 1:
            self.order[0], self.order[1] = self.order[1], self.order[0]

    def split(self, sends=1):
        self.bit = self.order.pop(0)
        low = 1 << sorted(self.bits).index(self.bit)
        self.bits.remove(self.bit)
        rows, columns = self.own.shape[0] // 2, self.own.shape[1]
        if self.shard % 16 == 0:
            self.own, *self.send = whole(
                self.name,
                functools.partial(split_kernel, self.shard, self.bit, low, sends),
                (struct((rows, columns), bf16),) + (struct((rows, columns // sends), bf16),) * sends,
                self.own,
                *self.received,
            )
        else:
            self.own, send = row_halves(self.total().astype(bf16), self.bit, low, self.shard)
            self.send = jnp.split(send, sends, 1)

    def exchange(self):
        self.received = [swap(v, "rows", self.bit) for v in self.send]

    def step(self, sends=1):
        self.split(sends)
        self.exchange()

    def total(self):
        return self.own.astype(f32) + jnp.concatenate(self.received, 1).astype(f32)

    def finish(self, *columns):
        while self.order:
            self.step()
        outs = tuple(struct((self.own.shape[0], n), f32) for n in columns)
        kernel = functools.partial(finish_kernel, len(self.received))
        return whole(self.name + "_finish", kernel, outs, self.own, *self.received)

    def small_finish(self, bias_shape, *columns):
        while self.order:
            self.step()
        rows = self.own.shape[0]
        outs = tuple(struct((rows, n), f32) for n in columns)
        outs += (struct((rows,), f32),) * 3 + (struct(bias_shape, f32),)
        return whole(self.name + "_finish", small_finish_kernel, outs, self.own, *self.received)

    def gain_finish(self, gain, *columns):
        while self.order:
            self.step()
        outs = tuple(struct((self.own.shape[0], n), f32) for n in columns) + (struct(gain.shape, f32),)
        return whole(
            self.name + "_finish", gain_finish_kernel, outs, self.own, *self.received, gain, swap(gain, "mp")
        )


def finish_two(first, second):
    while first.order or second.order:
        for scatter in (first, second):
            if scatter.order:
                scatter.step()
    outs = tuple(struct(v.own.shape, f32) for v in (first, second))
    return whole("finish", two_finish_kernel, outs, first.own, *first.received, second.own, *second.received)


def tie(*values):
    return list(lax.optimization_barrier(values))


def struct(shape, dtype):
    return jax.ShapeDtypeStruct(shape, dtype)


def per_device(
    tokens,
    segment_ids,
    pair_ids,
    bucket_ids,
    attn_gain,
    query_weight,
    key_weight,
    value_weight,
    output_weight,
    bias_table,
    ff_gain,
    up_weight,
    down_weight,
    final_gain,
    proj_weight,
):
    length = tokens.shape[2]
    width = tokens.shape[3]
    inner = query_weight.shape[1]
    hidden = up_weight.shape[1]
    head_count = bias_table.shape[1]
    bucket_count = bias_table.shape[0]
    total_segs = pair_ids.shape[0]
    span = 2 * length
    size = length // CHUNKS
    chunks = range(CHUNKS)
    tower_index = lax.axis_index("tower")
    device_index = tower_index * lax.axis_size("rows") + lax.axis_index("rows")
    shard = width // (2 * lax.axis_size("rows"))

    token_row = tokens.reshape(length, width)
    segments = segment_ids.reshape(1, length)

    part_rows = inner // 2
    fetched = swap(
        lax.dynamic_slice_in_dim(output_weight, tower_index * part_rows, part_rows, 0), "mp"
    )

    normed_one, query, key, value, probs, mix_stored, tok, *mixes = whole(
        "attention",
        attend_kernel,
        (
            stored((length, width), bf16),
            stored((length, inner), bf16),
            stored((length, inner), bf16),
            stored((length, inner), bf16),
            stored((head_count, length, length), bf16),
            stored((length, inner), bf16),
            fixed((length, width), bf16),
        )
        + (fixed((size, inner), bf16),) * CHUNKS,
        token_row,
        query_weight,
        key_weight,
        value_weight,
        attn_gain,
        bias_table.T,
        bucket_ids,
        segments,
        scratch=[
            pltpu.VMEM((3, width, inner), bf16),
            pltpu.VMEM((width,), f32),
            pltpu.VMEM((head_count, bucket_count), f32),
            pltpu.VMEM((span - 1,), jnp.int32),
            pltpu.VMEM((1, length), jnp.int32),
            pltpu.VMEM((length, width), bf16),
            pltpu.VMEM((length, inner), bf16),
            pltpu.VMEM((length, inner), bf16),
            pltpu.VMEM((length, inner), bf16),
            pltpu.VMEM((head_count, length, length), bf16),
            pltpu.VMEM((length, inner), bf16),
            pltpu.VMEM((8, span), f32),
            pltpu.VMEM((length, length), f32),
            pltpu.VMEM((2, BLOCK, span), f32),
            pltpu.VMEM((2, BLOCK, length), f32),
            pltpu.SemaphoreType.DMA((8,)),
            pltpu.SemaphoreType.DMA((5 + inner // BLOCK,)),
        ],
        in_hbm=8,
        mib=24,
    )
    mix_received = [swap(mix, "mp") for mix in mixes]
    fetched, segments = tie(fetched, tie(segments, mixes[-1])[0])
    fetched_too = swap(fetched, "tower")
    output_whole, up_held, down_held, proj_held = whole(
        "load",
        load_kernel,
        (
            fixed((2 * inner, width), bf16),
            fixed((width, hidden), bf16),
            fixed((hidden, width), bf16),
            fixed((width, width), bf16),
        ),
        output_weight,
        up_weight,
        down_weight,
        proj_weight,
        fetched,
        fetched_too,
        scratch=[pltpu.SemaphoreType.DMA((6,))],
        in_hbm=4,
    )

    hidden_one, normed_two, active, slope, ff_part, ff_received = [], [], [], [], [], []
    for c in chunks:
        outs = whole(
            "feed_forward",
            functools.partial(ff_kernel, c),
            (
                fixed((size, width), f32),
                fixed((size, width), bf16),
                fixed((size, hidden), bf16),
                fixed((size, hidden), f32),
                fixed((size, width), bf16),
            ),
            tok,
            output_whole,
            up_held,
            down_held,
            mixes[c],
            mix_received[c],
            ff_gain,
            scratch=[pltpu.VMEM((size, 2 * inner), bf16)],
            in_vmem=5,
        )
        for kept, out in zip((hidden_one, normed_two, active, slope, ff_part), outs):
            kept.append(out)
        ff_received.append(swap(ff_part[c], "mp"))

    hidden_two, pooled = [], []
    for c in chunks:
        h2, total = whole(
            "pool",
            functools.partial(pool_kernel, c),
            (
                fixed((size, width), f32),
                struct((SEGS_ROW, width), bf16 if c == CHUNKS - 1 else f32),
            ),
            hidden_one[c],
            ff_part[c],
            ff_received[c],
            final_gain,
            segments,
            *pooled,
            in_vmem=2,
        )
        hidden_two.append(h2)
        pooled = [total]
    gathered = gather_all(pooled[0])
    loss, proj_grad, pooled_grad = whole(
        "contrast",
        functools.partial(contrast_kernel, total_segs),
        (
            struct((1, 1), f32),
            struct((shard, width), f32),
            struct((SEGS_ROW, width), f32),
        ),
        proj_held,
        gathered,
        pair_ids,
        in_vmem=1,
    )

    two_part, hidden_two_grad, ff_grad, up_out_grad, final_gain_part = whole(
        "feed_forward_back",
        ff_back_kernel,
        (
            fixed((length, width), bf16),
            fixed((length, width), f32),
            fixed((length, width), bf16),
            fixed((length, hidden), bf16),
            struct((1, width), f32),
        ),
        down_held,
        up_held,
        *hidden_two,
        *slope,
        pooled_grad,
        segments,
        final_gain,
        in_vmem=2 + 2 * CHUNKS,
    )
    two_received = swap(two_part, "mp")

    def half_shapes(sends):
        half = struct((width // 2, hidden), bf16)
        return (struct((width // 2, hidden // sends), bf16),) * sends + (half,)

    *halves, own = whole("down_weight", down_weight_kernel, half_shapes(DOWN_SENDS), ff_grad, *active, in_vmem=1 + CHUNKS)
    down_scatter = RowsScatter("down_split", shard, own, [swap(v, "tower") for v in halves])
    *halves, own = whole("up_weight", up_weight_kernel, half_shapes(UP_SENDS), up_out_grad, *normed_two, in_vmem=1 + CHUNKS)
    up_scatter = RowsScatter("up_split", shard, own, [swap(v, "tower") for v in halves])
    down_scatter.step()
    up_scatter.split()
    two_received, down_send, up_scatter.send = tie(
        two_received, down_scatter.send, up_scatter.send
    )
    up_scatter.exchange()
    hidden_one_grad, attn_grad, mix_grad, ff_gain_part, *heads_held = whole(
        "middle_back",
        middle_back_kernel,
        (
            fixed((length, width), f32),
            stored((length, width), bf16),
            fixed((length, inner), bf16),
            struct((1, width), f32),
        )
        + (fixed((length, inner), bf16),) * 3
        + (fixed((head_count, length, length), bf16),),
        query,
        key,
        value,
        probs,
        output_whole,
        two_part,
        hidden_two_grad,
        *hidden_one,
        two_received,
        ff_gain,
        scratch=[
            pltpu.VMEM((length, width), bf16),
            pltpu.SemaphoreType.DMA((4,)),
            pltpu.SemaphoreType.DMA((1,)),
        ],
        in_hbm=4,
        in_vmem=3 + CHUNKS,
    )

    down_scatter.received, mix_grad = tie(down_scatter.received, mix_grad)
    down_scatter.split()
    mix_grad = tie(mix_grad, down_scatter.send)[0]
    down_scatter.exchange()

    pair_shape = struct((width // 2, 2 * inner), bf16)
    more_shape = struct((width // 2, 2 * inner + LANES), bf16)
    one_part, first_other, first_own, second_other, second_own = whole(
        "attention_back",
        functools.partial(attend_back_kernel, shard),
        (
            fixed((length, width), bf16),
            more_shape,
            more_shape,
            pair_shape,
            pair_shape,
        ),
        query_weight,
        key_weight,
        value_weight,
        normed_one,
        mix_stored,
        attn_grad,
        *heads_held,
        mix_grad,
        tok,
        bucket_ids,
        ff_gain_part,
        final_gain_part,
        scratch=[
            pltpu.VMEM((length, 3 * inner), bf16),
            pltpu.VMEM((length, width), bf16),
            pltpu.VMEM((3, width, inner), bf16),
            pltpu.VMEM((length, inner), bf16),
            pltpu.VMEM((length, width), bf16),
            pltpu.VMEM((width, LANES), f32),
            pltpu.VMEM((bucket_count, head_count), f32),
            pltpu.VMEM((2, length, length), bf16),
            pltpu.VMEM((2, BLOCK, span), f32),
            pltpu.VMEM((8, span), f32),
            pltpu.VMEM((2, BLOCK, length), f32),
            pltpu.SemaphoreType.DMA((6,)),
        ],
        in_hbm=6,
        in_vmem=6,
        mib=24,
    )
    one_received = swap(one_part, "mp")
    first_other, second_other, down_scatter.received, up_scatter.received = tie(
        first_other, second_other, down_scatter.received, up_scatter.received
    )
    first_scatter = RowsScatter("query_key_split", shard, first_own, [swap(first_other, "tower")])
    second_scatter = RowsScatter("value_output_split", shard, second_own, [swap(second_other, "tower")])
    up_scatter.step()
    down_scatter.step()
    first_scatter.received = tie(first_scatter.received, up_scatter.send, down_scatter.send)[0]
    first_scatter.step()
    second_scatter.step()
    first_scatter.received, up_scatter.received, down_scatter.received = tie(
        first_scatter.received, up_scatter.received, down_scatter.received
    )
    first_scatter.step()
    up_scatter.step()
    first_scatter.received, second_scatter.received, down_scatter.received = tie(
        first_scatter.received, second_scatter.received, down_scatter.received
    )
    second_scatter.step()
    first_scatter.step()
    down_sum, up_sum = finish_two(down_scatter, up_scatter)
    tokens_grad = whole(
        "last",
        last_kernel,
        stored((length, width), f32),
        tok,
        one_part,
        hidden_one_grad,
        attn_gain,
        one_received,
        scratch=[pltpu.VMEM((length, width), f32), pltpu.SemaphoreType.DMA((length // BLOCK,))],
        in_vmem=3,
    )
    second_scatter.received, first_scatter.received, tokens_grad, down_sum, up_sum = tie(
        second_scatter.received, first_scatter.received, tokens_grad, down_sum, up_sum
    )
    second_scatter.step()
    bias_pieces = -(-bucket_count // shard)
    query_sum, key_sum, attn_gain_sum, ff_gain_sum, final_gain_sum, turned = first_scatter.small_finish(
        (head_count * bias_pieces, min(shard, bucket_count)), inner, inner
    )
    value_sum, output_sum, attn_gain_sum = second_scatter.gain_finish(attn_gain_sum, inner, inner)
    bias_rows = [turned[g * head_count : (g + 1) * head_count, :] for g in range(bias_pieces)]
    bias_total = jnp.concatenate(bias_rows, 1)[:, :bucket_count].T
    return (
        loss[0, 0],
        tokens_grad.reshape(tokens.shape),
        attn_gain_sum,
        query_sum,
        key_sum,
        value_sum,
        output_sum.T,
        bias_total,
        ff_gain_sum,
        up_sum,
        down_sum.T,
        final_gain_sum,
        proj_grad,
    )


def solution(mesh):
    in_specs = (
        P("tower", "rows", None, None),
        P("tower", "rows", None),
        P(),
        P(),
        P(),
        P(None, "mp"),
        P(None, "mp"),
        P(None, "mp"),
        P("mp", None),
        P(None, "mp"),
        P(),
        P(None, "mp"),
        P("mp", None),
        P(),
        P(),
    )
    out_specs = (
        P(),
        P("tower", "rows", None, None),
        P(("tower", "rows")),
        P(("tower", "rows"), "mp"),
        P(("tower", "rows"), "mp"),
        P(("tower", "rows"), "mp"),
        P("mp", ("tower", "rows")),
        P(None, "mp"),
        P(("tower", "rows")),
        P(("tower", "rows"), "mp"),
        P("mp", ("tower", "rows")),
        P(("tower", "rows")),
        P(("tower", "rows"), None),
    )
    return jax.shard_map(
        per_device, mesh=mesh, in_specs=in_specs, out_specs=out_specs, check_vma=False
    )
```

```python
import functools

import jax
import jax.numpy as jnp
from jax import lax
from jax.experimental import pallas as pl
from jax.experimental.pallas import tpu as pltpu
from jax.sharding import PartitionSpec as P

SEGS_ROW = 8
BLOCK = 128
STRIP = 32
STEP = 384
LANES = 128
DOWN_SENDS, UP_SENDS = 4, 8
CHUNKS = 2

eps = 1e-06
logit_scale = 50.0
highest = lax.Precision.HIGHEST
f32 = jnp.float32
bf16 = jnp.bfloat16


def inv_rms(values):
    return lax.rsqrt(jnp.mean(values * values, -1, keepdims=True) + eps)


def dot_nn(a, b):
    return lax.dot_general(a, b, (((1,), (0,)), ((), ())), preferred_element_type=f32)


def dot_nt(a, b):
    return lax.dot_general(a, b, (((1,), (1,)), ((), ())), preferred_element_type=f32)


def dot_tn(a, b):
    return lax.dot_general(a, b, (((0,), (0,)), ((), ())), preferred_element_type=f32)


def gelu_parts(values):
    size = jnp.abs(values)
    bell = jnp.exp(-0.5 * values * values)
    t = 1.0 / (1.0 + (0.3275911 * 0.7071067811865476) * size)
    poly = t * (
        0.127414796
        + t * (-0.142248368 + t * (0.7107068705 + t * (-0.7265760135 + t * 0.5307027145)))
    )
    tail = poly * bell
    return bell, jnp.where(values >= 0, 1.0 - tail, tail)


def key_range(block, blocks):
    return max(0, block - 2), min(blocks, block + 3)


def split_low(values, parts):
    out = []
    for _ in range(parts):
        out.append(values.astype(bf16))
        values = values - out[-1].astype(f32)
    return out


def norm_back(values, inv, gain, grad):
    scaled = grad * gain
    inner_mean = jnp.mean(values * scaled, -1, keepdims=True)
    return inv * scaled - values * (inv * inv * inv * inner_mean)


def row_gain(gain_ref):
    return gain_ref[...].reshape(1, gain_ref.shape[0])


def attend_kernel(
    tok_hbm, wq_hbm, wk_hbm, wv_hbm, gain_hbm, table_hbm, ids_hbm, seg_hbm,
    n1_hbm, q_hbm, k_hbm, v_hbm, probs_hbm, mix_hbm, tok_ref, *rest,
):
    mix_refs = rest[:CHUNKS]
    (
        w_ref, gain_ref, table_ref, ids_ref, seg_ref, n1_ref, q_ref, k_ref, v_ref, probs_ref, mix_ref,
        rel_ref, mask_ref, skew_ref, score_ref, sems, out_sems,
    ) = rest[CHUNKS:]
    length, inner = q_ref.shape
    blocks = length // BLOCK
    heads, buckets = table_ref.shape
    pairs = inner // BLOCK
    span = rel_ref.shape[1]
    copies = start_copies(
        sems,
        (tok_hbm, tok_ref),
        (wq_hbm, w_ref.at[0]),
        (wk_hbm, w_ref.at[1]),
        (wv_hbm, w_ref.at[2]),
        (gain_hbm, gain_ref),
        (table_hbm, table_ref),
        (ids_hbm, ids_ref),
        (seg_hbm, seg_ref),
    )
    for copy in copies[4:]:
        copy.wait()
    hot = (
        lax.broadcasted_iota(jnp.int32, (buckets, span - 1), 0)
        == ids_ref[...].reshape(1, span - 1)
    ).astype(f32)
    rel_ref[...] = jnp.zeros_like(rel_ref)
    rel_ref[0:heads, 0 : span - 1] = lax.dot_general(
        table_ref[...], hot, (((1,), (0,)), ((), ())), precision=highest, preferred_element_type=f32
    )
    seg_row = seg_ref[...].astype(f32)
    for b in range(blocks):
        own = jnp.broadcast_to(seg_row[:, b * BLOCK : (b + 1) * BLOCK], (BLOCK, BLOCK)).T
        for c in range(blocks):
            other = jnp.broadcast_to(seg_row[:, c * BLOCK : (c + 1) * BLOCK], (BLOCK, BLOCK))
            mask_ref[b * BLOCK : (b + 1) * BLOCK, c * BLOCK : (c + 1) * BLOCK] = jnp.where(
                own == other, 0.0, -1e30
            )
    copies[0].wait()
    gain = row_gain(gain_ref)
    for at in range(0, length, STRIP):
        x = tok_ref[at : at + STRIP, :].astype(f32)
        n1_ref[at : at + STRIP, :] = (x * inv_rms(x) * gain).astype(bf16)
    n1 = n1_ref[...]
    for i, out_ref in enumerate((q_ref, k_ref, v_ref)):
        copies[1 + i].wait()
        out_ref[...] = dot_nn(n1, w_ref[i]).astype(bf16)
    outs = start_copies(out_sems, (n1_ref, n1_hbm), (q_ref, q_hbm), (k_ref, k_hbm), (v_ref, v_hbm))

    def probs_copy(pair):
        heads_of = pl.ds(2 * pair, 2)
        return pltpu.make_async_copy(probs_ref.at[heads_of], probs_hbm.at[heads_of], out_sems.at[4 + pair])

    low_lanes = lax.broadcasted_iota(jnp.int32, (BLOCK, BLOCK), 1) < BLOCK // 2
    zero = jnp.zeros((BLOCK, BLOCK), bf16)

    @pl.loop(0, pairs, unroll=True)
    def _(pair):
        lanes = pl.ds(pl.multiple_of(pair * BLOCK, BLOCK), BLOCK)
        for h in range(2):
            row = jnp.broadcast_to(rel_ref[pl.ds(pair * 2 + h, 1), :], (BLOCK, span))
            skew_ref[h] = pltpu.roll(row, span - (BLOCK - 1), 1, stride=1, stride_axis=0)
        for b in range(blocks):
            first, last = key_range(b, blocks)
            rows = slice(b * BLOCK, (b + 1) * BLOCK)
            keys = slice(first * BLOCK, last * BLOCK)
            shift = length - BLOCK - b * BLOCK
            q_pair = q_ref[rows, lanes]
            k_pair = k_ref[keys, lanes]
            v_pair = v_ref[keys, lanes]
            width = (last - first) * BLOCK
            for h in range(2):
                q_one = jnp.where(low_lanes if h == 0 else ~low_lanes, q_pair, zero)
                score_ref[h, :, :width] = dot_nt(q_one, k_pair)
            for at in range(0, BLOCK, STRIP):
                part = slice(b * BLOCK + at, b * BLOCK + at + STRIP)
                for h in range(2):
                    head = pair * 2 + h
                    scores = (
                        score_ref[h, at : at + STRIP, :width]
                        + skew_ref[h, at : at + STRIP, shift + first * BLOCK : shift + last * BLOCK]
                        + mask_ref[part, keys]
                    )
                    raised = jnp.exp(scores - jnp.max(scores, -1, keepdims=True))
                    scale = 1.0 / jnp.sum(raised, -1, keepdims=True)
                    probs_ref[head, part, keys] = (raised * scale).astype(bf16)
                    if first > 0:
                        probs_ref[head, part, 0 : first * BLOCK] = jnp.zeros((STRIP, first * BLOCK), bf16)
                    if last < blocks:
                        probs_ref[head, part, last * BLOCK :] = jnp.zeros(
                            (STRIP, length - last * BLOCK), bf16
                        )
            mix_ref[rows, lanes] = jnp.where(
                low_lanes,
                dot_nn(probs_ref[pair * 2, rows, keys], v_pair),
                dot_nn(probs_ref[pair * 2 + 1, rows, keys], v_pair),
            ).astype(bf16)
        probs_copy(pair).start()

    outs += start_copies(out_sems.at[4 + pairs :], (mix_ref, mix_hbm))
    for i, part in enumerate(mix_refs):
        part[...] = mix_ref[i * part.shape[0] : (i + 1) * part.shape[0], :]
    for copy in outs:
        copy.wait()
    for pair in range(pairs):
        probs_copy(pair).wait()


def load_kernel(
    wo_hbm, up_hbm, down_hbm, proj_hbm, fetched_hbm, fetched_too_hbm, wo_ref, up_ref, down_ref, proj_ref, sems
):
    me, tower_index = lax.axis_index("mp"), lax.axis_index("tower")
    inner = wo_hbm.shape[0]
    piece = inner // 2
    own_at = pl.multiple_of(me * inner, inner)
    other_at = (1 - me) * inner
    copies = start_copies(
        sems,
        (wo_hbm, wo_ref.at[pl.ds(own_at, inner), :]),
        (fetched_hbm, wo_ref.at[pl.ds(pl.multiple_of(other_at + tower_index * piece, piece), piece), :]),
        (fetched_too_hbm, wo_ref.at[pl.ds(pl.multiple_of(other_at + (1 - tower_index) * piece, piece), piece), :]),
        (up_hbm, up_ref),
        (down_hbm, down_ref),
        (proj_hbm, proj_ref),
    )
    for copy in copies:
        copy.wait()


def ff_kernel(
    chunk, tok_ref, wo_ref, up_ref, down_ref, mix_own, mix_other, gain_ref,
    h1_ref, n2_ref, a_ref, slope_ref, part_ref,
    mix_ref,
):
    size, width = h1_ref.shape
    inner = mix_own.shape[1]
    hidden = up_ref.shape[1]
    step = 256
    me = lax.axis_index("mp")
    mix_ref[:, pl.ds(pl.multiple_of(me * inner, inner), inner)] = mix_own[...]
    mix_ref[:, pl.ds(pl.multiple_of((1 - me) * inner, inner), inner)] = mix_other[...]
    h1_ref[...] = dot_nn(mix_ref[...], wo_ref[...])
    gain = row_gain(gain_ref)
    for at in range(0, size, STRIP):
        rows = slice(at, at + STRIP)
        h1 = tok_ref[chunk * size + at : chunk * size + at + STRIP, :].astype(f32) + h1_ref[rows, :]
        h1_ref[rows, :] = h1
        n2_ref[rows, :] = (h1 * inv_rms(h1) * gain).astype(bf16)
    n2 = n2_ref[...]
    for at in range(0, hidden, step):
        cols = slice(at, at + step)
        slope_ref[:, cols] = dot_nn(n2, up_ref[:, cols])
        for r in range(0, size, STRIP):
            rows = slice(r, r + STRIP)
            u = slope_ref[rows, cols]
            bell, below = gelu_parts(u)
            a_ref[rows, cols] = (u * below).astype(bf16)
            slope_ref[rows, cols] = below + u * bell * 0.3989422804014327
    part_ref[...] = dot_nn(a_ref[...], down_ref[...]).astype(bf16)


def pool_kernel(chunk, h1_ref, own_ref, rec_ref, gain_ref, seg_ref, *rest):
    total_ref = rest[0] if chunk > 0 else None
    h2_ref, out_ref = rest[-2:]
    size, width = h1_ref.shape
    gain = row_gain(gain_ref)
    number = lax.broadcasted_iota(jnp.int32, (SEGS_ROW, 1), 0)
    total = jnp.zeros((SEGS_ROW, width), f32)
    step = 128
    for at in range(0, size, step):
        rows = slice(at, at + step)
        h2 = h1_ref[rows, :] + (own_ref[rows, :].astype(f32) + rec_ref[rows, :].astype(f32))
        h2_ref[rows, :] = h2
        member = (seg_ref[:, chunk * size + at : chunk * size + at + step] == number).astype(f32).astype(bf16)
        for piece in split_low(h2 * inv_rms(h2) * gain, 2):
            total += dot_nn(member, piece)
    if chunk > 0:
        total += total_ref[...]
    if chunk == CHUNKS - 1:
        counts = jnp.sum((seg_ref[...] == number).astype(f32), -1, keepdims=True)
        total = total / counts
    out_ref[...] = total.astype(out_ref.dtype)


def contrast_kernel(
    total_segs, proj_ref, gathered_ref, pair_ref, loss_ref, dproj_ref, own_ref
):
    me = lax.axis_index("tower") * lax.axis_size("rows") + lax.axis_index("rows")
    count = gathered_ref.shape[0]
    row = lax.broadcasted_iota(jnp.int32, (count, count), 0)
    col = lax.broadcasted_iota(jnp.int32, (count, count), 1)
    order = (col == (row ^ (me * SEGS_ROW))).astype(f32).astype(bf16)
    pooled = dot_nn(order, gathered_ref[...]).astype(bf16)
    e = dot_nn(pooled, proj_ref[...])
    inv = lax.rsqrt(jnp.sum(e * e, -1, keepdims=True) + eps)
    unit = e * inv
    unit_low = unit.astype(bf16)
    zq, zd = unit_low[:total_segs], unit_low[total_segs:]
    logits = logit_scale * dot_nt(zd, zq)
    positive = (
        lax.broadcasted_iota(jnp.int32, (total_segs, total_segs), 0)
        == pair_ref[...].reshape(1, total_segs)
    ).astype(f32)
    norms, shares = [], []
    for axis in (0, 1):
        most = jnp.max(logits, axis, keepdims=True)
        raised = jnp.exp(logits - most)
        total = jnp.sum(raised, axis, keepdims=True)
        norms.append(jnp.log(total) + most)
        shares.append(raised / total)
    half_share = 0.5 / total_segs
    ends = jnp.sum(norms[0], 1, keepdims=True) + jnp.sum(norms[1], 0, keepdims=True)
    hits = jnp.sum(jnp.sum(logits * positive, 1, keepdims=True), 0, keepdims=True)
    loss_ref[...] = half_share * (ends - 2.0 * hits)
    grad = (half_share * (shares[0] + shares[1] - 2.0 * positive)).astype(bf16)
    dz = logit_scale * jnp.concatenate([dot_tn(grad, zd), dot_nn(grad, zq)], 0)
    de = ((dz - unit * jnp.sum(unit * dz, -1, keepdims=True)) * inv).astype(bf16)
    width, shard = proj_ref.shape[0], dproj_ref.shape[0]
    row = lax.broadcasted_iota(jnp.int32, (width, shard), 0)
    col = lax.broadcasted_iota(jnp.int32, (width, shard), 1)
    columns = (row == col + me * shard).astype(f32).astype(bf16)
    dproj_ref[...] = dot_tn(dot_nn(pooled, columns).astype(bf16), de)
    row = lax.broadcasted_iota(jnp.int32, (SEGS_ROW, count), 0)
    col = lax.broadcasted_iota(jnp.int32, (SEGS_ROW, count), 1)
    mine = (col == row + me * SEGS_ROW).astype(f32).astype(bf16)
    own_ref[...] = dot_nt(dot_nn(mine, de).astype(bf16), proj_ref[...])


def ff_back_kernel(down_ref, up_ref, *refs):
    h2_refs, slope_refs, refs = refs[:CHUNKS], refs[CHUNKS : 2 * CHUNKS], refs[2 * CHUNKS :]
    dpool_ref, seg_ref, gain_ref, part_ref, dh2_ref, df_ref, du_ref, dgain_ref = refs
    length, width = dh2_ref.shape
    size = length // CHUNKS
    hidden = down_ref.shape[0]
    step = 256
    gain = row_gain(gain_ref)
    number = lax.broadcasted_iota(jnp.int32, (SEGS_ROW, 1), 0)
    counts = jnp.sum((seg_ref[...] == number).astype(f32), -1, keepdims=True)
    pieces = jnp.concatenate([p.astype(f32) for p in split_low(dpool_ref[...] / counts, 4)], 0).astype(bf16)
    member = (seg_ref[...] == number).astype(f32)
    member = jnp.concatenate([member] * 4, 0).astype(bf16)
    dh2_ref[...] = dot_tn(member, pieces)
    dgain = jnp.zeros((1, width), f32)
    for at in range(0, length, STRIP):
        rows = slice(at, at + STRIP)
        h2 = h2_refs[at // size][at % size : at % size + STRIP, :]
        grad = dh2_ref[rows, :]
        inv = inv_rms(h2)
        dh2 = norm_back(h2, inv, gain, grad)
        dgain += jnp.sum(h2 * inv * grad, 0, keepdims=True)
        dh2_ref[rows, :] = dh2
        df_ref[rows, :] = dh2.astype(bf16)
    dgain_ref[...] = dgain
    df = df_ref[...]
    for at in range(0, hidden, step):
        cols = slice(at, at + step)
        da = dot_nt(df, down_ref[cols, :])
        for c in range(CHUNKS):
            rows = slice(c * size, (c + 1) * size)
            du_ref[rows, cols] = (da[rows, :] * slope_refs[c][:, cols]).astype(bf16)
    part_ref[...] = dot_nt(du_ref[...], up_ref[...]).astype(bf16)


def down_weight_kernel(df_ref, *refs):
    size = refs[0].shape[0]
    weight_products([df_ref.at[c * size : (c + 1) * size, :] for c in range(CHUNKS)], refs[:CHUNKS], refs[CHUNKS:-1], refs[-1])


def up_weight_kernel(du_ref, *refs):
    size = refs[0].shape[0]
    weight_products(refs[:CHUNKS], [du_ref.at[c * size : (c + 1) * size, :] for c in range(CHUNKS)], refs[CHUNKS:-1], refs[-1])


def middle_back_kernel(*refs):
    ahead, refs = refs[:4], refs[4:]
    wo_ref, own_ref, dh2_ref, *refs = refs
    h1_refs, refs = refs[:CHUNKS], refs[CHUNKS:]
    rec_ref, gain_ref, dh1_ref, da_hbm, dmix_ref, dgain_ref, *refs = refs
    held, (da_ref, sems, out_sems) = refs[:4], refs[4:]
    copies = start_copies(sems, *zip(ahead, held))
    length, width = dh1_ref.shape
    size = length // CHUNKS
    gain = row_gain(gain_ref)
    dgain = jnp.zeros((1, width), f32)
    for at in range(0, length, STRIP):
        rows = slice(at, at + STRIP)
        h1 = h1_refs[at // size][at % size : at % size + STRIP, :]
        grad = own_ref[rows, :].astype(f32) + rec_ref[rows, :].astype(f32)
        inv = inv_rms(h1)
        dh1 = dh2_ref[rows, :] + norm_back(h1, inv, gain, grad)
        dgain += jnp.sum(h1 * inv * grad, 0, keepdims=True)
        dh1_ref[rows, :] = dh1
        da_ref[rows, :] = dh1.astype(bf16)
    dgain_ref[...] = dgain
    copies += start_copies(out_sems, (da_ref, da_hbm))
    inner = dmix_ref.shape[1]
    own_at = pl.multiple_of(lax.axis_index("mp") * inner, inner)
    dmix_ref[...] = dot_nt(da_ref[...], wo_ref[pl.ds(own_at, inner), :]).astype(bf16)
    for copy in copies:
        copy.wait()


def attend_back_kernel(
    shard, wq_hbm, wk_hbm, wv_hbm, n1_hbm, mix_hbm, da_hbm, q_ref, k_ref, v_ref, probs_ref, mixg_ref, tok_ref,
    ids_ref, ff_gain, final_gain,
    part_ref, qk_other, qk_own, vo_other, vo_own,
    grads_ref, n1_ref, w_ref, mix_ref, da_ref, all_ref, biasg_ref, ds_ref, skew_ref, rel_ref, dp_ref, sems,
):
    length, inner = q_ref.shape
    blocks = length // BLOCK
    pairs = inner // BLOCK
    span = rel_ref.shape[1]
    later = start_copies(
        sems,
        (wq_hbm, w_ref.at[0]),
        (wk_hbm, w_ref.at[1]),
        (wv_hbm, w_ref.at[2]),
        (n1_hbm, n1_ref),
        (mix_hbm, mix_ref),
        (da_hbm, da_ref),
    )
    low_lanes = lax.broadcasted_iota(jnp.int32, (BLOCK, BLOCK), 1) < BLOCK // 2
    low_all = lax.broadcasted_iota(jnp.int32, (length, BLOCK), 1) < BLOCK // 2
    zero = jnp.zeros((BLOCK, BLOCK), bf16)
    rel_ref[...] = jnp.zeros_like(rel_ref)

    @pl.loop(0, pairs)
    def _(pair):
        lanes = pl.ds(pl.multiple_of(pair * BLOCK, BLOCK), BLOCK)
        skew_ref[...] = jnp.zeros_like(skew_ref)
        for b in range(blocks):
            first, last = key_range(b, blocks)
            rows = slice(b * BLOCK, (b + 1) * BLOCK)
            keys = slice(first * BLOCK, last * BLOCK)
            shift = length - BLOCK - b * BLOCK
            g_pair = mixg_ref[rows, lanes]
            k_pair = k_ref[keys, lanes]
            v_pair = v_ref[keys, lanes]
            width = (last - first) * BLOCK
            for h in range(2):
                g_one = jnp.where(low_lanes if h == 0 else ~low_lanes, g_pair, zero)
                dp_ref[h, :, :width] = dot_nt(g_one, v_pair)
            for at in range(0, BLOCK, STRIP):
                part = slice(b * BLOCK + at, b * BLOCK + at + STRIP)
                for h in range(2):
                    probs = probs_ref[pair * 2 + h, part, keys].astype(f32)
                    weighted = probs * dp_ref[h, at : at + STRIP, :width]
                    ds = weighted - probs * jnp.sum(weighted, -1, keepdims=True)
                    ds_ref[h, part, keys] = ds.astype(bf16)
                    if first > 0:
                        ds_ref[h, part, 0 : first * BLOCK] = jnp.zeros((STRIP, first * BLOCK), bf16)
                    if last < blocks:
                        ds_ref[h, part, last * BLOCK :] = jnp.zeros((STRIP, length - last * BLOCK), bf16)
                    skew_ref[h, at : at + STRIP, shift + first * BLOCK : shift + last * BLOCK] += ds
            grads_ref[rows, lanes] = jnp.where(
                low_lanes,
                dot_nn(ds_ref[0, rows, keys], k_pair),
                dot_nn(ds_ref[1, rows, keys], k_pair),
            ).astype(bf16)
        q_pair = q_ref[:, lanes]
        g_pair = mixg_ref[:, lanes]
        k_lanes = pl.ds(pl.multiple_of(inner + pair * BLOCK, BLOCK), BLOCK)
        v_lanes = pl.ds(pl.multiple_of(2 * inner + pair * BLOCK, BLOCK), BLOCK)
        grads_ref[:, k_lanes] = jnp.where(
            low_all, dot_tn(ds_ref[0], q_pair), dot_tn(ds_ref[1], q_pair)
        ).astype(bf16)
        grads_ref[:, v_lanes] = jnp.where(
            low_all,
            dot_tn(probs_ref[pair * 2], g_pair),
            dot_tn(probs_ref[pair * 2 + 1], g_pair),
        ).astype(bf16)
        for h in range(2):
            tiles = skew_ref[h, BLOCK - 8 :, :]
            for r in range(0, BLOCK - 8, 8):
                tiles += pltpu.roll(skew_ref[h, r : r + 8, :], BLOCK - 8 - r, 1)
            line = tiles[7:8, :]
            for r in range(7):
                line += pltpu.roll(tiles[r : r + 1, :], 7 - r, 1)
            rel_ref[pl.ds(pair * 2 + h, 1), :] = line

    hot = (
        lax.broadcasted_iota(jnp.int32, (biasg_ref.shape[0], span - 1), 0)
        == ids_ref[...].reshape(1, span - 1)
    ).astype(f32)
    total = lax.dot_general(
        hot, rel_ref[:, : span - 1], (((1,), (1,)), ((), ())), precision=highest, preferred_element_type=f32
    )
    biasg_ref[...] = total[:, : biasg_ref.shape[1]]
    for copy in later:
        copy.wait()
    part_ref[...] = (
        dot_nt(grads_ref[:, :inner], w_ref[0])
        + dot_nt(grads_ref[:, inner : 2 * inner], w_ref[1])
        + dot_nt(grads_ref[:, 2 * inner :], w_ref[2])
    ).astype(bf16)
    weight_products([n1_ref], [grads_ref.at[:, : 2 * inner]], [qk_other], qk_own)
    width = n1_ref.shape[1]
    dgain = jnp.zeros((1, width), f32)
    for at in range(0, length, STRIP):
        rows = slice(at, at + STRIP)
        x = tok_ref[rows, :].astype(f32)
        dgain += jnp.sum(x * inv_rms(x) * part_ref[rows, :].astype(f32), 0, keepdims=True)
    weight_products([n1_ref], [grads_ref.at[:, 2 * inner :]], [vo_other], vo_own)
    weight_products([da_ref], [mix_ref], [vo_other], vo_own, inner)
    small_columns(shard, biasg_ref, [dgain, ff_gain[...], final_gain[...]], all_ref)
    tower_index = lax.axis_index("tower")
    half = width // 2
    for which, out_ref in ((1 - tower_index, qk_other), (tower_index, qk_own)):
        rows = pl.ds(pl.multiple_of(which * half, half), half)
        out_ref[:, 2 * inner :] = all_ref[rows, :].astype(bf16)


def last_kernel(tok_ref, own_ref, dh1_ref, gain_ref, rec_ref, out_hbm, out_ref, sems):
    gain = row_gain(gain_ref)
    length = own_ref.shape[0]
    copies = []
    for at in range(0, length, STRIP):
        rows = slice(at, at + STRIP)
        x = tok_ref[rows, :].astype(f32)
        grad = own_ref[rows, :].astype(f32) + rec_ref[rows, :].astype(f32)
        out_ref[rows, :] = dh1_ref[rows, :] + norm_back(x, inv_rms(x), gain, grad)
        if (at + STRIP) % BLOCK == 0:
            done = pl.ds(at + STRIP - BLOCK, BLOCK)
            copies += start_copies(sems.at[len(copies) :], (out_ref.at[done, :], out_hbm.at[done, :]))
    for copy in copies:
        copy.wait()


def weight_products(lefts, rights, other_refs, own_ref, columns=0):
    tower_index = lax.axis_index("tower")
    half = lefts[0].shape[1] // 2
    each = other_refs[0].shape[1]
    for which in (1 - tower_index, tower_index):
        lanes = pl.ds(pl.multiple_of(which * half, half), half)
        turned = [left[:, lanes].T for left in lefts]
        for at in range(0, rights[0].shape[1], STEP):
            total = None
            for left, right in zip(turned, rights):
                term = dot_nn(left, right[:, at : at + STEP])
                total = term if total is None else total + term
            total = total.astype(bf16)
            there = columns + at
            if which is tower_index:
                own_ref[:, there : there + STEP] = total
                continue
            for i, other_ref in enumerate(other_refs):
                begin, end = max(there, i * each), min(there + STEP, (i + 1) * each)
                if begin < end:
                    other_ref[:, begin - i * each : end - i * each] = total[:, begin - there : end - there]


def small_columns(shard, bias_ref, lines, all_ref):
    width = all_ref.shape[0]
    buckets, heads = bias_ref.shape
    lane = lax.broadcasted_iota(jnp.int32, (1, LANES), 1)

    def low(values):
        return values.astype(f32).astype(bf16)

    row = lax.broadcasted_iota(jnp.int32, (width, buckets), 0) % shard
    col = lax.broadcasted_iota(jnp.int32, (width, buckets), 1)
    total = jnp.zeros((width, LANES), f32)
    for g in range(-(-buckets // shard)):
        place = lax.broadcasted_iota(jnp.int32, (heads, LANES), 0) + 3 + g * heads == lane
        total += dot_nn(low(col == row + g * shard), low(dot_nn(low(bias_ref[...]), low(place))))
    place = lax.broadcasted_iota(jnp.int32, (3, LANES), 0) == lane
    all_ref[...] = total + dot_tn(low(jnp.concatenate(lines, 0)), low(place))


def finish_kernel(pieces, own_ref, *refs):
    rec_refs, out_refs = refs[:pieces], refs[pieces:]
    at = 0
    for out_ref, rec_ref in zip(out_refs, rec_refs if pieces > 1 else [rec_refs[0]] * len(out_refs)):
        cols = slice(at, at + out_ref.shape[1])
        at = cols.stop
        out_ref[...] = own_ref[:, cols].astype(f32) + rec_ref[:, cols].astype(f32)


def small_finish_kernel(own_ref, rec_ref, *out_refs):
    finish_kernel(1, own_ref, rec_ref, *out_refs[:-4])
    *gain_refs, bias_ref = out_refs[-4:]
    at = own_ref.shape[1] - LANES
    values = own_ref[:, at:].astype(f32) + rec_ref[:, at:].astype(f32)
    eye = (
        lax.broadcasted_iota(jnp.int32, (LANES, LANES), 0) == lax.broadcasted_iota(jnp.int32, (LANES, LANES), 1)
    ).astype(f32)
    turned = lax.dot_general(
        eye, values, (((1,), (1,)), ((), ())), precision=highest, preferred_element_type=f32
    )
    for i, gain_ref in enumerate(gain_refs):
        gain_ref[...] = turned[i, :]
    bias_ref[...] = turned[3 : 3 + bias_ref.shape[0], : bias_ref.shape[1]]


def gain_finish_kernel(own_ref, rec_ref, gain_own, gain_rec, *out_refs):
    finish_kernel(1, own_ref, rec_ref, *out_refs[:-1])
    out_refs[-1][...] = gain_own[...] + gain_rec[...]


def two_finish_kernel(own_ref, rec_ref, own_too, rec_too, out_ref, out_too):
    finish_kernel(1, own_ref, rec_ref, out_ref)
    finish_kernel(1, own_too, rec_too, out_too)


def split_kernel(shard, bit, low, sends, own_ref, *refs):
    rec_refs, keep_ref, send_refs = refs[: -1 - sends], refs[-1 - sends], refs[-sends:]
    own_bit = lax.axis_index("rows") // bit % 2
    each = send_refs[0].shape[1]
    at = 0
    for rec_ref in rec_refs:
        columns = rec_ref.shape[1]
        for j in range(keep_ref.shape[0] // shard):
            there = slice(j * shard, (j + 1) * shard)
            for which in (own_bit, 1 - own_bit):
                start = ((j // low * 2 + which) * low + j % low) * shard
                rows = pl.ds(pl.multiple_of(start, shard), shard)
                total = (
                    own_ref[rows, at : at + columns].astype(f32) + rec_ref[rows, :].astype(f32)
                ).astype(bf16)
                if which is own_bit:
                    keep_ref[there, at : at + columns] = total
                    continue
                for i, send_ref in enumerate(send_refs):
                    begin, end = max(at, i * each), min(at + columns, (i + 1) * each)
                    if begin < end:
                        send_ref[there, begin - i * each : end - i * each] = total[:, begin - at : end - at]
        at += columns


def fixed(shape, dtype):
    return pltpu.VMEM(shape, dtype)


def stored(shape, dtype):
    return pltpu.HBM(shape, dtype)


def whole(name, kernel, out_shapes, *args, scratch=(), in_hbm=0, in_vmem=0, mib=16):
    args = (
        [pltpu.with_memory_space_constraint(v, pltpu.HBM) for v in args[:in_hbm]]
        + [pltpu.with_memory_space_constraint(v, pltpu.VMEM) for v in args[in_hbm : in_hbm + in_vmem]]
        + list(args[in_hbm + in_vmem :])
    )
    vmem = pl.BlockSpec(memory_space=pltpu.VMEM)
    hbm = pl.BlockSpec(memory_space=pl.ANY)
    is_stored = lambda out: getattr(out, "memory_space", None) == pltpu.HBM
    with jax.named_scope(name):
        return pl.pallas_call(
            kernel,
            out_shape=out_shapes,
            in_specs=[hbm] * in_hbm + [vmem] * (len(args) - in_hbm),
            out_specs=jax.tree.map(lambda out: hbm if is_stored(out) else vmem, out_shapes),
            scratch_shapes=scratch,
            compiler_params=pltpu.CompilerParams(vmem_limit_bytes=mib * 1024 * 1024),
            cost_estimate=pl.CostEstimate(flops=1, bytes_accessed=1, transcendentals=0),
        )(*args)


def start_copies(sems, *pairs):
    copies = [pltpu.make_async_copy(src, dst, sems.at[i]) for i, (src, dst) in enumerate(pairs)]
    for copy in copies:
        copy.start()
    return copies


def swap(values, axis, bit=1):
    count = lax.axis_size(axis)
    return lax.ppermute(values, axis, [(i, i ^ bit) for i in range(count)])


def gather_all(values):
    bits = [1 << i for i in range(lax.axis_size("rows").bit_length() - 1)]
    steps = [bits[:1]] + [bits[i : i + 2] for i in range(1, len(bits), 2)]
    for step in steps:
        masks = step + ([step[0] | step[1]] if len(step) > 1 else [])
        values = jnp.concatenate([values] + [swap(values, "rows", mask) for mask in masks], 0)
    return jnp.concatenate([values, swap(values, "tower")], 0)


def row_halves(cur, bit, low, shard):
    columns = cur.shape[-1]
    view = cur.reshape(-1, 2, low * shard, columns)
    own_bit = (lax.axis_index("rows") & bit) // bit
    keep = lax.dynamic_index_in_dim(view, own_bit, 1, False).reshape(-1, columns)
    send = lax.dynamic_index_in_dim(view, 1 - own_bit, 1, False).reshape(-1, columns)
    return keep, send


class RowsScatter:
    def __init__(self, name, shard, own, received, swapped=False):
        self.name, self.shard = name, shard
        self.own, self.received = own, received
        self.bits = [1 << i for i in range(lax.axis_size("rows").bit_length() - 1)]
        self.order = list(self.bits)
        if swapped and len(self.order) > 1:
            self.order[0], self.order[1] = self.order[1], self.order[0]

    def split(self, sends=1):
        self.bit = self.order.pop(0)
        low = 1 << sorted(self.bits).index(self.bit)
        self.bits.remove(self.bit)
        rows, columns = self.own.shape[0] // 2, self.own.shape[1]
        if self.shard % 16 == 0:
            self.own, *self.send = whole(
                self.name,
                functools.partial(split_kernel, self.shard, self.bit, low, sends),
                (struct((rows, columns), bf16),) + (struct((rows, columns // sends), bf16),) * sends,
                self.own,
                *self.received,
            )
        else:
            self.own, send = row_halves(self.total().astype(bf16), self.bit, low, self.shard)
            self.send = jnp.split(send, sends, 1)

    def exchange(self):
        self.received = [swap(v, "rows", self.bit) for v in self.send]

    def step(self, sends=1):
        self.split(sends)
        self.exchange()

    def total(self):
        return self.own.astype(f32) + jnp.concatenate(self.received, 1).astype(f32)

    def finish(self, *columns):
        while self.order:
            self.step()
        outs = tuple(struct((self.own.shape[0], n), f32) for n in columns)
        kernel = functools.partial(finish_kernel, len(self.received))
        return whole(self.name + "_finish", kernel, outs, self.own, *self.received)

    def small_finish(self, bias_shape, *columns):
        while self.order:
            self.step()
        rows = self.own.shape[0]
        outs = tuple(struct((rows, n), f32) for n in columns)
        outs += (struct((rows,), f32),) * 3 + (struct(bias_shape, f32),)
        return whole(self.name + "_finish", small_finish_kernel, outs, self.own, *self.received)

    def gain_finish(self, gain, *columns):
        while self.order:
            self.step()
        outs = tuple(struct((self.own.shape[0], n), f32) for n in columns) + (struct(gain.shape, f32),)
        return whole(
            self.name + "_finish", gain_finish_kernel, outs, self.own, *self.received, gain, swap(gain, "mp")
        )


def finish_two(first, second):
    while first.order or second.order:
        for scatter in (first, second):
            if scatter.order:
                scatter.step()
    outs = tuple(struct(v.own.shape, f32) for v in (first, second))
    return whole("finish", two_finish_kernel, outs, first.own, *first.received, second.own, *second.received)


def tie(*values):
    return list(lax.optimization_barrier(values))


def struct(shape, dtype):
    return jax.ShapeDtypeStruct(shape, dtype)


def per_device(
    tokens,
    segment_ids,
    pair_ids,
    bucket_ids,
    attn_gain,
    query_weight,
    key_weight,
    value_weight,
    output_weight,
    bias_table,
    ff_gain,
    up_weight,
    down_weight,
    final_gain,
    proj_weight,
):
    length = tokens.shape[2]
    width = tokens.shape[3]
    inner = query_weight.shape[1]
    hidden = up_weight.shape[1]
    head_count = bias_table.shape[1]
    bucket_count = bias_table.shape[0]
    total_segs = pair_ids.shape[0]
    span = 2 * length
    size = length // CHUNKS
    chunks = range(CHUNKS)
    tower_index = lax.axis_index("tower")
    device_index = tower_index * lax.axis_size("rows") + lax.axis_index("rows")
    shard = width // (2 * lax.axis_size("rows"))

    token_row = tokens.reshape(length, width)
    segments = segment_ids.reshape(1, length)

    part_rows = inner // 2
    fetched = swap(
        lax.dynamic_slice_in_dim(output_weight, tower_index * part_rows, part_rows, 0), "mp"
    )

    normed_one, query, key, value, probs, mix_stored, tok, *mixes = whole(
        "attention",
        attend_kernel,
        (
            stored((length, width), bf16),
            stored((length, inner), bf16),
            stored((length, inner), bf16),
            stored((length, inner), bf16),
            stored((head_count, length, length), bf16),
            stored((length, inner), bf16),
            fixed((length, width), bf16),
        )
        + (fixed((size, inner), bf16),) * CHUNKS,
        token_row,
        query_weight,
        key_weight,
        value_weight,
        attn_gain,
        bias_table.T,
        bucket_ids,
        segments,
        scratch=[
            pltpu.VMEM((3, width, inner), bf16),
            pltpu.VMEM((width,), f32),
            pltpu.VMEM((head_count, bucket_count), f32),
            pltpu.VMEM((span - 1,), jnp.int32),
            pltpu.VMEM((1, length), jnp.int32),
            pltpu.VMEM((length, width), bf16),
            pltpu.VMEM((length, inner), bf16),
            pltpu.VMEM((length, inner), bf16),
            pltpu.VMEM((length, inner), bf16),
            pltpu.VMEM((head_count, length, length), bf16),
            pltpu.VMEM((length, inner), bf16),
            pltpu.VMEM((8, span), f32),
            pltpu.VMEM((length, length), f32),
            pltpu.VMEM((2, BLOCK, span), f32),
            pltpu.VMEM((2, BLOCK, length), f32),
            pltpu.SemaphoreType.DMA((8,)),
            pltpu.SemaphoreType.DMA((5 + inner // BLOCK,)),
        ],
        in_hbm=8,
        mib=24,
    )
    mix_received = [swap(mix, "mp") for mix in mixes]
    fetched, segments = tie(fetched, tie(segments, mixes[-1])[0])
    fetched_too = swap(fetched, "tower")
    output_whole, up_held, down_held, proj_held = whole(
        "load",
        load_kernel,
        (
            fixed((2 * inner, width), bf16),
            fixed((width, hidden), bf16),
            fixed((hidden, width), bf16),
            fixed((width, width), bf16),
        ),
        output_weight,
        up_weight,
        down_weight,
        proj_weight,
        fetched,
        fetched_too,
        scratch=[pltpu.SemaphoreType.DMA((6,))],
        in_hbm=4,
    )

    hidden_one, normed_two, active, slope, ff_part, ff_received = [], [], [], [], [], []
    for c in chunks:
        outs = whole(
            "feed_forward",
            functools.partial(ff_kernel, c),
            (
                fixed((size, width), f32),
                fixed((size, width), bf16),
                fixed((size, hidden), bf16),
                fixed((size, hidden), f32),
                fixed((size, width), bf16),
            ),
            tok,
            output_whole,
            up_held,
            down_held,
            mixes[c],
            mix_received[c],
            ff_gain,
            scratch=[pltpu.VMEM((size, 2 * inner), bf16)],
            in_vmem=5,
        )
        for kept, out in zip((hidden_one, normed_two, active, slope, ff_part), outs):
            kept.append(out)
        ff_received.append(swap(ff_part[c], "mp"))

    hidden_two, pooled = [], []
    for c in chunks:
        h2, total = whole(
            "pool",
            functools.partial(pool_kernel, c),
            (
                fixed((size, width), f32),
                struct((SEGS_ROW, width), bf16 if c == CHUNKS - 1 else f32),
            ),
            hidden_one[c],
            ff_part[c],
            ff_received[c],
            final_gain,
            segments,
            *pooled,
            in_vmem=2,
        )
        hidden_two.append(h2)
        pooled = [total]
    gathered = gather_all(pooled[0])
    loss, proj_grad, pooled_grad = whole(
        "contrast",
        functools.partial(contrast_kernel, total_segs),
        (
            struct((1, 1), f32),
            struct((shard, width), f32),
            struct((SEGS_ROW, width), f32),
        ),
        proj_held,
        gathered,
        pair_ids,
        in_vmem=1,
    )

    two_part, hidden_two_grad, ff_grad, up_out_grad, final_gain_part = whole(
        "feed_forward_back",
        ff_back_kernel,
        (
            fixed((length, width), bf16),
            fixed((length, width), f32),
            fixed((length, width), bf16),
            fixed((length, hidden), bf16),
            struct((1, width), f32),
        ),
        down_held,
        up_held,
        *hidden_two,
        *slope,
        pooled_grad,
        segments,
        final_gain,
        in_vmem=2 + 2 * CHUNKS,
    )
    two_received = swap(two_part, "mp")

    def half_shapes(sends):
        half = struct((width // 2, hidden), bf16)
        return (struct((width // 2, hidden // sends), bf16),) * sends + (half,)

    *halves, own = whole("down_weight", down_weight_kernel, half_shapes(DOWN_SENDS), ff_grad, *active, in_vmem=1 + CHUNKS)
    down_scatter = RowsScatter("down_split", shard, own, [swap(v, "tower") for v in halves])
    *halves, own = whole("up_weight", up_weight_kernel, half_shapes(UP_SENDS), up_out_grad, *normed_two, in_vmem=1 + CHUNKS)
    up_scatter = RowsScatter("up_split", shard, own, [swap(v, "tower") for v in halves])
    down_scatter.step()
    up_scatter.split()
    two_received, down_send, up_scatter.send = tie(
        two_received, down_scatter.send, up_scatter.send
    )
    up_scatter.exchange()
    hidden_one_grad, attn_grad, mix_grad, ff_gain_part, *heads_held = whole(
        "middle_back",
        middle_back_kernel,
        (
            fixed((length, width), f32),
            stored((length, width), bf16),
            fixed((length, inner), bf16),
            struct((1, width), f32),
        )
        + (fixed((length, inner), bf16),) * 3
        + (fixed((head_count, length, length), bf16),),
        query,
        key,
        value,
        probs,
        output_whole,
        two_part,
        hidden_two_grad,
        *hidden_one,
        two_received,
        ff_gain,
        scratch=[
            pltpu.VMEM((length, width), bf16),
            pltpu.SemaphoreType.DMA((4,)),
            pltpu.SemaphoreType.DMA((1,)),
        ],
        in_hbm=4,
        in_vmem=3 + CHUNKS,
    )

    down_scatter.received, mix_grad = tie(down_scatter.received, mix_grad)
    down_scatter.split()
    mix_grad = tie(mix_grad, down_scatter.send)[0]
    down_scatter.exchange()

    pair_shape = struct((width // 2, 2 * inner), bf16)
    more_shape = struct((width // 2, 2 * inner + LANES), bf16)
    one_part, first_other, first_own, second_other, second_own = whole(
        "attention_back",
        functools.partial(attend_back_kernel, shard),
        (
            fixed((length, width), bf16),
            more_shape,
            more_shape,
            pair_shape,
            pair_shape,
        ),
        query_weight,
        key_weight,
        value_weight,
        normed_one,
        mix_stored,
        attn_grad,
        *heads_held,
        mix_grad,
        tok,
        bucket_ids,
        ff_gain_part,
        final_gain_part,
        scratch=[
            pltpu.VMEM((length, 3 * inner), bf16),
            pltpu.VMEM((length, width), bf16),
            pltpu.VMEM((3, width, inner), bf16),
            pltpu.VMEM((length, inner), bf16),
            pltpu.VMEM((length, width), bf16),
            pltpu.VMEM((width, LANES), f32),
            pltpu.VMEM((bucket_count, head_count), f32),
            pltpu.VMEM((2, length, length), bf16),
            pltpu.VMEM((2, BLOCK, span), f32),
            pltpu.VMEM((8, span), f32),
            pltpu.VMEM((2, BLOCK, length), f32),
            pltpu.SemaphoreType.DMA((6,)),
        ],
        in_hbm=6,
        in_vmem=6,
        mib=24,
    )
    one_received = swap(one_part, "mp")
    first_other, second_other, down_scatter.received, up_scatter.received = tie(
        first_other, second_other, down_scatter.received, up_scatter.received
    )
    first_scatter = RowsScatter("query_key_split", shard, first_own, [swap(first_other, "tower")])
    second_scatter = RowsScatter("value_output_split", shard, second_own, [swap(second_other, "tower")])
    up_scatter.step()
    down_scatter.step()
    first_scatter.received = tie(first_scatter.received, up_scatter.send, down_scatter.send)[0]
    first_scatter.step()
    second_scatter.step()
    first_scatter.received, down_scatter.received = tie(
        first_scatter.received, down_scatter.received
    )
    first_scatter.step()
    first_scatter.send, up_scatter.received = tie(first_scatter.send, up_scatter.received)
    up_scatter.step()
    first_scatter.received, second_scatter.received, down_scatter.received = tie(
        first_scatter.received, second_scatter.received, down_scatter.received
    )
    second_scatter.step()
    first_scatter.step()
    down_sum, up_sum = finish_two(down_scatter, up_scatter)
    tokens_grad = whole(
        "last",
        last_kernel,
        stored((length, width), f32),
        tok,
        one_part,
        hidden_one_grad,
        attn_gain,
        one_received,
        scratch=[pltpu.VMEM((length, width), f32), pltpu.SemaphoreType.DMA((length // BLOCK,))],
        in_vmem=3,
    )
    second_scatter.received, tokens_grad, down_sum, up_sum = tie(
        second_scatter.received, tokens_grad, down_sum, up_sum
    )
    second_scatter.step()
    bias_pieces = -(-bucket_count // shard)
    query_sum, key_sum, attn_gain_sum, ff_gain_sum, final_gain_sum, turned = first_scatter.small_finish(
        (head_count * bias_pieces, min(shard, bucket_count)), inner, inner
    )
    value_sum, output_sum, attn_gain_sum = second_scatter.gain_finish(attn_gain_sum, inner, inner)
    bias_rows = [turned[g * head_count : (g + 1) * head_count, :] for g in range(bias_pieces)]
    bias_total = jnp.concatenate(bias_rows, 1)[:, :bucket_count].T
    return (
        loss[0, 0],
        tokens_grad.reshape(tokens.shape),
        attn_gain_sum,
        query_sum,
        key_sum,
        value_sum,
        output_sum.T,
        bias_total,
        ff_gain_sum,
        up_sum,
        down_sum.T,
        final_gain_sum,
        proj_grad,
    )


def solution(mesh):
    in_specs = (
        P("tower", "rows", None, None),
        P("tower", "rows", None),
        P(),
        P(),
        P(),
        P(None, "mp"),
        P(None, "mp"),
        P(None, "mp"),
        P("mp", None),
        P(None, "mp"),
        P(),
        P(None, "mp"),
        P("mp", None),
        P(),
        P(),
    )
    out_specs = (
        P(),
        P("tower", "rows", None, None),
        P(("tower", "rows")),
        P(("tower", "rows"), "mp"),
        P(("tower", "rows"), "mp"),
        P(("tower", "rows"), "mp"),
        P("mp", ("tower", "rows")),
        P(None, "mp"),
        P(("tower", "rows")),
        P(("tower", "rows"), "mp"),
        P("mp", ("tower", "rows")),
        P(("tower", "rows")),
        P(("tower", "rows"), None),
    )
    return jax.shard_map(
        per_device, mesh=mesh, in_specs=in_specs, out_specs=out_specs, check_vma=False
    )
```

```python
import functools

import jax
import jax.numpy as jnp
from jax import lax
from jax.experimental import pallas as pl
from jax.experimental.pallas import tpu as pltpu
from jax.sharding import PartitionSpec as P

SEGS_ROW = 8
BLOCK = 128
STRIP = 32
STEP = 384
LANES = 128
DOWN_SENDS, UP_SENDS = 4, 8
CHUNKS = 2

eps = 1e-06
logit_scale = 50.0
highest = lax.Precision.HIGHEST
f32 = jnp.float32
bf16 = jnp.bfloat16


def inv_rms(values):
    return lax.rsqrt(jnp.mean(values * values, -1, keepdims=True) + eps)


def dot_nn(a, b):
    return lax.dot_general(a, b, (((1,), (0,)), ((), ())), preferred_element_type=f32)


def dot_nt(a, b):
    return lax.dot_general(a, b, (((1,), (1,)), ((), ())), preferred_element_type=f32)


def dot_tn(a, b):
    return lax.dot_general(a, b, (((0,), (0,)), ((), ())), preferred_element_type=f32)


def gelu_parts(values):
    size = jnp.abs(values)
    bell = jnp.exp(-0.5 * values * values)
    t = 1.0 / (1.0 + (0.3275911 * 0.7071067811865476) * size)
    poly = t * (
        0.127414796
        + t * (-0.142248368 + t * (0.7107068705 + t * (-0.7265760135 + t * 0.5307027145)))
    )
    tail = poly * bell
    return bell, jnp.where(values >= 0, 1.0 - tail, tail)


def key_range(block, blocks):
    return max(0, block - 2), min(blocks, block + 3)


def split_low(values, parts):
    out = []
    for _ in range(parts):
        out.append(values.astype(bf16))
        values = values - out[-1].astype(f32)
    return out


def norm_back(values, inv, gain, grad):
    scaled = grad * gain
    inner_mean = jnp.mean(values * scaled, -1, keepdims=True)
    return inv * scaled - values * (inv * inv * inv * inner_mean)


def row_gain(gain_ref):
    return gain_ref[...].reshape(1, gain_ref.shape[0])


def attend_kernel(
    tok_hbm, wq_hbm, wk_hbm, wv_hbm, gain_hbm, table_hbm, ids_hbm, seg_hbm,
    n1_hbm, q_hbm, k_hbm, v_hbm, probs_hbm, mix_hbm, tok_ref, *rest,
):
    mix_refs = rest[:CHUNKS]
    (
        w_ref, gain_ref, table_ref, ids_ref, seg_ref, n1_ref, q_ref, k_ref, v_ref, probs_ref, mix_ref,
        rel_ref, mask_ref, skew_ref, score_ref, sems, out_sems,
    ) = rest[CHUNKS:]
    length, inner = q_ref.shape
    blocks = length // BLOCK
    heads, buckets = table_ref.shape
    pairs = inner // BLOCK
    span = rel_ref.shape[1]
    copies = start_copies(
        sems,
        (tok_hbm, tok_ref),
        (wq_hbm, w_ref.at[0]),
        (wk_hbm, w_ref.at[1]),
        (wv_hbm, w_ref.at[2]),
        (gain_hbm, gain_ref),
        (table_hbm, table_ref),
        (ids_hbm, ids_ref),
        (seg_hbm, seg_ref),
    )
    for copy in copies[4:]:
        copy.wait()
    hot = (
        lax.broadcasted_iota(jnp.int32, (buckets, span - 1), 0)
        == ids_ref[...].reshape(1, span - 1)
    ).astype(f32)
    rel_ref[...] = jnp.zeros_like(rel_ref)
    rel_ref[0:heads, 0 : span - 1] = lax.dot_general(
        table_ref[...], hot, (((1,), (0,)), ((), ())), precision=highest, preferred_element_type=f32
    )
    seg_row = seg_ref[...].astype(f32)
    for b in range(blocks):
        own = jnp.broadcast_to(seg_row[:, b * BLOCK : (b + 1) * BLOCK], (BLOCK, BLOCK)).T
        for c in range(blocks):
            other = jnp.broadcast_to(seg_row[:, c * BLOCK : (c + 1) * BLOCK], (BLOCK, BLOCK))
            mask_ref[b * BLOCK : (b + 1) * BLOCK, c * BLOCK : (c + 1) * BLOCK] = jnp.where(
                own == other, 0.0, -1e30
            )
    copies[0].wait()
    gain = row_gain(gain_ref)
    for at in range(0, length, STRIP):
        x = tok_ref[at : at + STRIP, :].astype(f32)
        n1_ref[at : at + STRIP, :] = (x * inv_rms(x) * gain).astype(bf16)
    n1 = n1_ref[...]
    for i, out_ref in enumerate((q_ref, k_ref, v_ref)):
        copies[1 + i].wait()
        out_ref[...] = dot_nn(n1, w_ref[i]).astype(bf16)
    outs = start_copies(out_sems, (n1_ref, n1_hbm), (q_ref, q_hbm), (k_ref, k_hbm), (v_ref, v_hbm))

    def probs_copy(pair):
        heads_of = pl.ds(2 * pair, 2)
        return pltpu.make_async_copy(probs_ref.at[heads_of], probs_hbm.at[heads_of], out_sems.at[4 + pair])

    low_lanes = lax.broadcasted_iota(jnp.int32, (BLOCK, BLOCK), 1) < BLOCK // 2
    zero = jnp.zeros((BLOCK, BLOCK), bf16)

    @pl.loop(0, pairs, unroll=True)
    def _(pair):
        lanes = pl.ds(pl.multiple_of(pair * BLOCK, BLOCK), BLOCK)
        for h in range(2):
            row = jnp.broadcast_to(rel_ref[pl.ds(pair * 2 + h, 1), :], (BLOCK, span))
            skew_ref[h] = pltpu.roll(row, span - (BLOCK - 1), 1, stride=1, stride_axis=0)
        for b in range(blocks):
            first, last = key_range(b, blocks)
            rows = slice(b * BLOCK, (b + 1) * BLOCK)
            keys = slice(first * BLOCK, last * BLOCK)
            shift = length - BLOCK - b * BLOCK
            q_pair = q_ref[rows, lanes]
            k_pair = k_ref[keys, lanes]
            v_pair = v_ref[keys, lanes]
            width = (last - first) * BLOCK
            for h in range(2):
                q_one = jnp.where(low_lanes if h == 0 else ~low_lanes, q_pair, zero)
                score_ref[h, :, :width] = dot_nt(q_one, k_pair)
            for at in range(0, BLOCK, STRIP):
                part = slice(b * BLOCK + at, b * BLOCK + at + STRIP)
                for h in range(2):
                    head = pair * 2 + h
                    scores = (
                        score_ref[h, at : at + STRIP, :width]
                        + skew_ref[h, at : at + STRIP, shift + first * BLOCK : shift + last * BLOCK]
                        + mask_ref[part, keys]
                    )
                    raised = jnp.exp(scores - jnp.max(scores, -1, keepdims=True))
                    scale = 1.0 / jnp.sum(raised, -1, keepdims=True)
                    probs_ref[head, part, keys] = (raised * scale).astype(bf16)
                    if first > 0:
                        probs_ref[head, part, 0 : first * BLOCK] = jnp.zeros((STRIP, first * BLOCK), bf16)
                    if last < blocks:
                        probs_ref[head, part, last * BLOCK :] = jnp.zeros(
                            (STRIP, length - last * BLOCK), bf16
                        )
            mix_ref[rows, lanes] = jnp.where(
                low_lanes,
                dot_nn(probs_ref[pair * 2, rows, keys], v_pair),
                dot_nn(probs_ref[pair * 2 + 1, rows, keys], v_pair),
            ).astype(bf16)
        probs_copy(pair).start()

    outs += start_copies(out_sems.at[4 + pairs :], (mix_ref, mix_hbm))
    for i, part in enumerate(mix_refs):
        part[...] = mix_ref[i * part.shape[0] : (i + 1) * part.shape[0], :]
    for copy in outs:
        copy.wait()
    for pair in range(pairs):
        probs_copy(pair).wait()


def load_kernel(
    wo_hbm, up_hbm, down_hbm, proj_hbm, fetched_hbm, fetched_too_hbm, wo_ref, up_ref, down_ref, proj_ref, sems
):
    me, tower_index = lax.axis_index("mp"), lax.axis_index("tower")
    inner = wo_hbm.shape[0]
    piece = inner // 2
    own_at = pl.multiple_of(me * inner, inner)
    other_at = (1 - me) * inner
    copies = start_copies(
        sems,
        (wo_hbm, wo_ref.at[pl.ds(own_at, inner), :]),
        (fetched_hbm, wo_ref.at[pl.ds(pl.multiple_of(other_at + tower_index * piece, piece), piece), :]),
        (fetched_too_hbm, wo_ref.at[pl.ds(pl.multiple_of(other_at + (1 - tower_index) * piece, piece), piece), :]),
        (up_hbm, up_ref),
        (down_hbm, down_ref),
        (proj_hbm, proj_ref),
    )
    for copy in copies:
        copy.wait()


def ff_kernel(
    chunk, tok_ref, wo_ref, up_ref, down_ref, mix_own, mix_other, gain_ref,
    h1_ref, n2_ref, a_ref, slope_ref, part_ref,
    mix_ref,
):
    size, width = h1_ref.shape
    inner = mix_own.shape[1]
    hidden = up_ref.shape[1]
    step = 512
    me = lax.axis_index("mp")
    mix_ref[:, pl.ds(pl.multiple_of(me * inner, inner), inner)] = mix_own[...]
    mix_ref[:, pl.ds(pl.multiple_of((1 - me) * inner, inner), inner)] = mix_other[...]
    h1_ref[...] = dot_nn(mix_ref[...], wo_ref[...])
    gain = row_gain(gain_ref)
    for at in range(0, size, STRIP):
        rows = slice(at, at + STRIP)
        h1 = tok_ref[chunk * size + at : chunk * size + at + STRIP, :].astype(f32) + h1_ref[rows, :]
        h1_ref[rows, :] = h1
        n2_ref[rows, :] = (h1 * inv_rms(h1) * gain).astype(bf16)
    n2 = n2_ref[...]
    for at in range(0, hidden, step):
        cols = slice(at, at + step)
        slope_ref[:, cols] = dot_nn(n2, up_ref[:, cols])
        for r in range(0, size, STRIP):
            rows = slice(r, r + STRIP)
            u = slope_ref[rows, cols]
            bell, below = gelu_parts(u)
            a_ref[rows, cols] = (u * below).astype(bf16)
            slope_ref[rows, cols] = below + u * bell * 0.3989422804014327
    part_ref[...] = dot_nn(a_ref[...], down_ref[...]).astype(bf16)


def pool_kernel(chunk, h1_ref, own_ref, rec_ref, gain_ref, seg_ref, *rest):
    total_ref = rest[0] if chunk > 0 else None
    h2_ref, out_ref = rest[-2:]
    size, width = h1_ref.shape
    gain = row_gain(gain_ref)
    number = lax.broadcasted_iota(jnp.int32, (SEGS_ROW, 1), 0)
    total = jnp.zeros((SEGS_ROW, width), f32)
    step = 128
    for at in range(0, size, step):
        rows = slice(at, at + step)
        h2 = h1_ref[rows, :] + (own_ref[rows, :].astype(f32) + rec_ref[rows, :].astype(f32))
        h2_ref[rows, :] = h2
        member = (seg_ref[:, chunk * size + at : chunk * size + at + step] == number).astype(f32).astype(bf16)
        for piece in split_low(h2 * inv_rms(h2) * gain, 2):
            total += dot_nn(member, piece)
    if chunk > 0:
        total += total_ref[...]
    if chunk == CHUNKS - 1:
        counts = jnp.sum((seg_ref[...] == number).astype(f32), -1, keepdims=True)
        total = total / counts
    out_ref[...] = total.astype(out_ref.dtype)


def contrast_kernel(
    total_segs, proj_ref, gathered_ref, pair_ref, loss_ref, dproj_ref, own_ref
):
    me = lax.axis_index("tower") * lax.axis_size("rows") + lax.axis_index("rows")
    count = gathered_ref.shape[0]
    row = lax.broadcasted_iota(jnp.int32, (count, count), 0)
    col = lax.broadcasted_iota(jnp.int32, (count, count), 1)
    order = (col == (row ^ (me * SEGS_ROW))).astype(f32).astype(bf16)
    pooled = dot_nn(order, gathered_ref[...]).astype(bf16)
    e = dot_nn(pooled, proj_ref[...])
    inv = lax.rsqrt(jnp.sum(e * e, -1, keepdims=True) + eps)
    unit = e * inv
    unit_low = unit.astype(bf16)
    zq, zd = unit_low[:total_segs], unit_low[total_segs:]
    logits = logit_scale * dot_nt(zd, zq)
    positive = (
        lax.broadcasted_iota(jnp.int32, (total_segs, total_segs), 0)
        == pair_ref[...].reshape(1, total_segs)
    ).astype(f32)
    norms, shares = [], []
    for axis in (0, 1):
        most = jnp.max(logits, axis, keepdims=True)
        raised = jnp.exp(logits - most)
        total = jnp.sum(raised, axis, keepdims=True)
        norms.append(jnp.log(total) + most)
        shares.append(raised / total)
    half_share = 0.5 / total_segs
    ends = jnp.sum(norms[0], 1, keepdims=True) + jnp.sum(norms[1], 0, keepdims=True)
    hits = jnp.sum(jnp.sum(logits * positive, 1, keepdims=True), 0, keepdims=True)
    loss_ref[...] = half_share * (ends - 2.0 * hits)
    grad = (half_share * (shares[0] + shares[1] - 2.0 * positive)).astype(bf16)
    dz = logit_scale * jnp.concatenate([dot_tn(grad, zd), dot_nn(grad, zq)], 0)
    de = ((dz - unit * jnp.sum(unit * dz, -1, keepdims=True)) * inv).astype(bf16)
    width, shard = proj_ref.shape[0], dproj_ref.shape[0]
    row = lax.broadcasted_iota(jnp.int32, (width, shard), 0)
    col = lax.broadcasted_iota(jnp.int32, (width, shard), 1)
    columns = (row == col + me * shard).astype(f32).astype(bf16)
    dproj_ref[...] = dot_tn(dot_nn(pooled, columns).astype(bf16), de)
    row = lax.broadcasted_iota(jnp.int32, (SEGS_ROW, count), 0)
    col = lax.broadcasted_iota(jnp.int32, (SEGS_ROW, count), 1)
    mine = (col == row + me * SEGS_ROW).astype(f32).astype(bf16)
    own_ref[...] = dot_nt(dot_nn(mine, de).astype(bf16), proj_ref[...])


def ff_back_kernel(down_ref, up_ref, *refs):
    h2_refs, slope_refs, refs = refs[:CHUNKS], refs[CHUNKS : 2 * CHUNKS], refs[2 * CHUNKS :]
    dpool_ref, seg_ref, gain_ref, part_ref, dh2_ref, df_ref, du_ref, dgain_ref = refs
    length, width = dh2_ref.shape
    size = length // CHUNKS
    hidden = down_ref.shape[0]
    step = 512
    gain = row_gain(gain_ref)
    number = lax.broadcasted_iota(jnp.int32, (SEGS_ROW, 1), 0)
    counts = jnp.sum((seg_ref[...] == number).astype(f32), -1, keepdims=True)
    pieces = jnp.concatenate([p.astype(f32) for p in split_low(dpool_ref[...] / counts, 4)], 0).astype(bf16)
    member = (seg_ref[...] == number).astype(f32)
    member = jnp.concatenate([member] * 4, 0).astype(bf16)
    dh2_ref[...] = dot_tn(member, pieces)
    dgain = jnp.zeros((1, width), f32)
    for at in range(0, length, STRIP):
        rows = slice(at, at + STRIP)
        h2 = h2_refs[at // size][at % size : at % size + STRIP, :]
        grad = dh2_ref[rows, :]
        inv = inv_rms(h2)
        dh2 = norm_back(h2, inv, gain, grad)
        dgain += jnp.sum(h2 * inv * grad, 0, keepdims=True)
        dh2_ref[rows, :] = dh2
        df_ref[rows, :] = dh2.astype(bf16)
    dgain_ref[...] = dgain
    df = df_ref[...]
    for at in range(0, hidden, step):
        cols = slice(at, at + step)
        da = dot_nt(df, down_ref[cols, :])
        for c in range(CHUNKS):
            rows = slice(c * size, (c + 1) * size)
            du_ref[rows, cols] = (da[rows, :] * slope_refs[c][:, cols]).astype(bf16)
    part_ref[...] = dot_nt(du_ref[...], up_ref[...]).astype(bf16)


def down_weight_kernel(df_ref, *refs):
    size = refs[0].shape[0]
    weight_products([df_ref.at[c * size : (c + 1) * size, :] for c in range(CHUNKS)], refs[:CHUNKS], refs[CHUNKS:-1], refs[-1])


def up_weight_kernel(du_ref, *refs):
    size = refs[0].shape[0]
    weight_products(refs[:CHUNKS], [du_ref.at[c * size : (c + 1) * size, :] for c in range(CHUNKS)], refs[CHUNKS:-1], refs[-1])


def middle_back_kernel(*refs):
    ahead, refs = refs[:4], refs[4:]
    wo_ref, own_ref, dh2_ref, *refs = refs
    h1_refs, refs = refs[:CHUNKS], refs[CHUNKS:]
    rec_ref, gain_ref, dh1_ref, da_hbm, dmix_ref, dgain_ref, *refs = refs
    held, (da_ref, sems, out_sems) = refs[:4], refs[4:]
    copies = start_copies(sems, *zip(ahead, held))
    length, width = dh1_ref.shape
    size = length // CHUNKS
    gain = row_gain(gain_ref)
    dgain = jnp.zeros((1, width), f32)
    for at in range(0, length, STRIP):
        rows = slice(at, at + STRIP)
        h1 = h1_refs[at // size][at % size : at % size + STRIP, :]
        grad = own_ref[rows, :].astype(f32) + rec_ref[rows, :].astype(f32)
        inv = inv_rms(h1)
        dh1 = dh2_ref[rows, :] + norm_back(h1, inv, gain, grad)
        dgain += jnp.sum(h1 * inv * grad, 0, keepdims=True)
        dh1_ref[rows, :] = dh1
        da_ref[rows, :] = dh1.astype(bf16)
    dgain_ref[...] = dgain
    copies += start_copies(out_sems, (da_ref, da_hbm))
    inner = dmix_ref.shape[1]
    own_at = pl.multiple_of(lax.axis_index("mp") * inner, inner)
    dmix_ref[...] = dot_nt(da_ref[...], wo_ref[pl.ds(own_at, inner), :]).astype(bf16)
    for copy in copies:
        copy.wait()


def attend_back_kernel(
    shard, wq_hbm, wk_hbm, wv_hbm, n1_hbm, mix_hbm, da_hbm, q_ref, k_ref, v_ref, probs_ref, mixg_ref, tok_ref,
    ids_ref, ff_gain, final_gain,
    part_ref, qk_other, qk_own, vo_other, vo_own,
    grads_ref, n1_ref, w_ref, mix_ref, da_ref, all_ref, biasg_ref, ds_ref, skew_ref, rel_ref, dp_ref, sems,
):
    length, inner = q_ref.shape
    blocks = length // BLOCK
    pairs = inner // BLOCK
    span = rel_ref.shape[1]
    later = start_copies(
        sems,
        (wq_hbm, w_ref.at[0]),
        (wk_hbm, w_ref.at[1]),
        (wv_hbm, w_ref.at[2]),
        (n1_hbm, n1_ref),
        (mix_hbm, mix_ref),
        (da_hbm, da_ref),
    )
    low_lanes = lax.broadcasted_iota(jnp.int32, (BLOCK, BLOCK), 1) < BLOCK // 2
    low_all = lax.broadcasted_iota(jnp.int32, (length, BLOCK), 1) < BLOCK // 2
    zero = jnp.zeros((BLOCK, BLOCK), bf16)
    rel_ref[...] = jnp.zeros_like(rel_ref)

    @pl.loop(0, pairs)
    def _(pair):
        lanes = pl.ds(pl.multiple_of(pair * BLOCK, BLOCK), BLOCK)
        skew_ref[...] = jnp.zeros_like(skew_ref)
        for b in range(blocks):
            first, last = key_range(b, blocks)
            rows = slice(b * BLOCK, (b + 1) * BLOCK)
            keys = slice(first * BLOCK, last * BLOCK)
            shift = length - BLOCK - b * BLOCK
            g_pair = mixg_ref[rows, lanes]
            k_pair = k_ref[keys, lanes]
            v_pair = v_ref[keys, lanes]
            width = (last - first) * BLOCK
            for h in range(2):
                g_one = jnp.where(low_lanes if h == 0 else ~low_lanes, g_pair, zero)
                dp_ref[h, :, :width] = dot_nt(g_one, v_pair)
            for at in range(0, BLOCK, STRIP):
                part = slice(b * BLOCK + at, b * BLOCK + at + STRIP)
                for h in range(2):
                    probs = probs_ref[pair * 2 + h, part, keys].astype(f32)
                    weighted = probs * dp_ref[h, at : at + STRIP, :width]
                    ds = weighted - probs * jnp.sum(weighted, -1, keepdims=True)
                    ds_ref[h, part, keys] = ds.astype(bf16)
                    if first > 0:
                        ds_ref[h, part, 0 : first * BLOCK] = jnp.zeros((STRIP, first * BLOCK), bf16)
                    if last < blocks:
                        ds_ref[h, part, last * BLOCK :] = jnp.zeros((STRIP, length - last * BLOCK), bf16)
                    skew_ref[h, at : at + STRIP, shift + first * BLOCK : shift + last * BLOCK] += ds
            grads_ref[rows, lanes] = jnp.where(
                low_lanes,
                dot_nn(ds_ref[0, rows, keys], k_pair),
                dot_nn(ds_ref[1, rows, keys], k_pair),
            ).astype(bf16)
        q_pair = q_ref[:, lanes]
        g_pair = mixg_ref[:, lanes]
        k_lanes = pl.ds(pl.multiple_of(inner + pair * BLOCK, BLOCK), BLOCK)
        v_lanes = pl.ds(pl.multiple_of(2 * inner + pair * BLOCK, BLOCK), BLOCK)
        grads_ref[:, k_lanes] = jnp.where(
            low_all, dot_tn(ds_ref[0], q_pair), dot_tn(ds_ref[1], q_pair)
        ).astype(bf16)
        grads_ref[:, v_lanes] = jnp.where(
            low_all,
            dot_tn(probs_ref[pair * 2], g_pair),
            dot_tn(probs_ref[pair * 2 + 1], g_pair),
        ).astype(bf16)
        for h in range(2):
            tiles = skew_ref[h, BLOCK - 8 :, :]
            for r in range(0, BLOCK - 8, 8):
                tiles += pltpu.roll(skew_ref[h, r : r + 8, :], BLOCK - 8 - r, 1)
            line = tiles[7:8, :]
            for r in range(7):
                line += pltpu.roll(tiles[r : r + 1, :], 7 - r, 1)
            rel_ref[pl.ds(pair * 2 + h, 1), :] = line

    hot = (
        lax.broadcasted_iota(jnp.int32, (biasg_ref.shape[0], span - 1), 0)
        == ids_ref[...].reshape(1, span - 1)
    ).astype(f32)
    total = lax.dot_general(
        hot, rel_ref[:, : span - 1], (((1,), (1,)), ((), ())), precision=highest, preferred_element_type=f32
    )
    biasg_ref[...] = total[:, : biasg_ref.shape[1]]
    for copy in later:
        copy.wait()
    part_ref[...] = (
        dot_nt(grads_ref[:, :inner], w_ref[0])
        + dot_nt(grads_ref[:, inner : 2 * inner], w_ref[1])
        + dot_nt(grads_ref[:, 2 * inner :], w_ref[2])
    ).astype(bf16)
    weight_products([n1_ref], [grads_ref.at[:, : 2 * inner]], [qk_other], qk_own)
    width = n1_ref.shape[1]
    dgain = jnp.zeros((1, width), f32)
    for at in range(0, length, STRIP):
        rows = slice(at, at + STRIP)
        x = tok_ref[rows, :].astype(f32)
        dgain += jnp.sum(x * inv_rms(x) * part_ref[rows, :].astype(f32), 0, keepdims=True)
    weight_products([n1_ref], [grads_ref.at[:, 2 * inner :]], [vo_other], vo_own)
    weight_products([da_ref], [mix_ref], [vo_other], vo_own, inner)
    small_columns(shard, biasg_ref, [dgain, ff_gain[...], final_gain[...]], all_ref)
    tower_index = lax.axis_index("tower")
    half = width // 2
    for which, out_ref in ((1 - tower_index, qk_other), (tower_index, qk_own)):
        rows = pl.ds(pl.multiple_of(which * half, half), half)
        out_ref[:, 2 * inner :] = all_ref[rows, :].astype(bf16)


def last_kernel(tok_ref, own_ref, dh1_ref, gain_ref, rec_ref, out_hbm, out_ref, sems):
    gain = row_gain(gain_ref)
    length = own_ref.shape[0]
    copies = []
    for at in range(0, length, STRIP):
        rows = slice(at, at + STRIP)
        x = tok_ref[rows, :].astype(f32)
        grad = own_ref[rows, :].astype(f32) + rec_ref[rows, :].astype(f32)
        out_ref[rows, :] = dh1_ref[rows, :] + norm_back(x, inv_rms(x), gain, grad)
        if (at + STRIP) % BLOCK == 0:
            done = pl.ds(at + STRIP - BLOCK, BLOCK)
            copies += start_copies(sems.at[len(copies) :], (out_ref.at[done, :], out_hbm.at[done, :]))
    for copy in copies:
        copy.wait()


def weight_products(lefts, rights, other_refs, own_ref, columns=0):
    tower_index = lax.axis_index("tower")
    half = lefts[0].shape[1] // 2
    each = other_refs[0].shape[1]
    for which in (1 - tower_index, tower_index):
        lanes = pl.ds(pl.multiple_of(which * half, half), half)
        turned = [left[:, lanes].T for left in lefts]
        for at in range(0, rights[0].shape[1], STEP):
            total = None
            for left, right in zip(turned, rights):
                term = dot_nn(left, right[:, at : at + STEP])
                total = term if total is None else total + term
            total = total.astype(bf16)
            there = columns + at
            if which is tower_index:
                own_ref[:, there : there + STEP] = total
                continue
            for i, other_ref in enumerate(other_refs):
                begin, end = max(there, i * each), min(there + STEP, (i + 1) * each)
                if begin < end:
                    other_ref[:, begin - i * each : end - i * each] = total[:, begin - there : end - there]


def small_columns(shard, bias_ref, lines, all_ref):
    width = all_ref.shape[0]
    buckets, heads = bias_ref.shape
    lane = lax.broadcasted_iota(jnp.int32, (1, LANES), 1)

    def low(values):
        return values.astype(f32).astype(bf16)

    row = lax.broadcasted_iota(jnp.int32, (width, buckets), 0) % shard
    col = lax.broadcasted_iota(jnp.int32, (width, buckets), 1)
    total = jnp.zeros((width, LANES), f32)
    for g in range(-(-buckets // shard)):
        place = lax.broadcasted_iota(jnp.int32, (heads, LANES), 0) + 3 + g * heads == lane
        total += dot_nn(low(col == row + g * shard), low(dot_nn(low(bias_ref[...]), low(place))))
    place = lax.broadcasted_iota(jnp.int32, (3, LANES), 0) == lane
    all_ref[...] = total + dot_tn(low(jnp.concatenate(lines, 0)), low(place))


def finish_kernel(pieces, own_ref, *refs):
    rec_refs, out_refs = refs[:pieces], refs[pieces:]
    at = 0
    for out_ref, rec_ref in zip(out_refs, rec_refs if pieces > 1 else [rec_refs[0]] * len(out_refs)):
        cols = slice(at, at + out_ref.shape[1])
        at = cols.stop
        out_ref[...] = own_ref[:, cols].astype(f32) + rec_ref[:, cols].astype(f32)


def small_finish_kernel(own_ref, rec_ref, *out_refs):
    finish_kernel(1, own_ref, rec_ref, *out_refs[:-4])
    *gain_refs, bias_ref = out_refs[-4:]
    at = own_ref.shape[1] - LANES
    values = own_ref[:, at:].astype(f32) + rec_ref[:, at:].astype(f32)
    eye = (
        lax.broadcasted_iota(jnp.int32, (LANES, LANES), 0) == lax.broadcasted_iota(jnp.int32, (LANES, LANES), 1)
    ).astype(f32)
    turned = lax.dot_general(
        eye, values, (((1,), (1,)), ((), ())), precision=highest, preferred_element_type=f32
    )
    for i, gain_ref in enumerate(gain_refs):
        gain_ref[...] = turned[i, :]
    bias_ref[...] = turned[3 : 3 + bias_ref.shape[0], : bias_ref.shape[1]]


def gain_finish_kernel(own_ref, rec_ref, gain_own, gain_rec, *out_refs):
    finish_kernel(1, own_ref, rec_ref, *out_refs[:-1])
    out_refs[-1][...] = gain_own[...] + gain_rec[...]


def two_finish_kernel(own_ref, rec_ref, own_too, rec_too, out_ref, out_too):
    finish_kernel(1, own_ref, rec_ref, out_ref)
    finish_kernel(1, own_too, rec_too, out_too)


def split_kernel(shard, bit, low, sends, own_ref, *refs):
    rec_refs, keep_ref, send_refs = refs[: -1 - sends], refs[-1 - sends], refs[-sends:]
    own_bit = lax.axis_index("rows") // bit % 2
    each = send_refs[0].shape[1]
    at = 0
    for rec_ref in rec_refs:
        columns = rec_ref.shape[1]
        for j in range(keep_ref.shape[0] // shard):
            there = slice(j * shard, (j + 1) * shard)
            for which in (own_bit, 1 - own_bit):
                start = ((j // low * 2 + which) * low + j % low) * shard
                rows = pl.ds(pl.multiple_of(start, shard), shard)
                total = (
                    own_ref[rows, at : at + columns].astype(f32) + rec_ref[rows, :].astype(f32)
                ).astype(bf16)
                if which is own_bit:
                    keep_ref[there, at : at + columns] = total
                    continue
                for i, send_ref in enumerate(send_refs):
                    begin, end = max(at, i * each), min(at + columns, (i + 1) * each)
                    if begin < end:
                        send_ref[there, begin - i * each : end - i * each] = total[:, begin - at : end - at]
        at += columns


def fixed(shape, dtype):
    return pltpu.VMEM(shape, dtype)


def stored(shape, dtype):
    return pltpu.HBM(shape, dtype)


def whole(name, kernel, out_shapes, *args, scratch=(), in_hbm=0, in_vmem=0, mib=16):
    args = (
        [pltpu.with_memory_space_constraint(v, pltpu.HBM) for v in args[:in_hbm]]
        + [pltpu.with_memory_space_constraint(v, pltpu.VMEM) for v in args[in_hbm : in_hbm + in_vmem]]
        + list(args[in_hbm + in_vmem :])
    )
    vmem = pl.BlockSpec(memory_space=pltpu.VMEM)
    hbm = pl.BlockSpec(memory_space=pl.ANY)
    is_stored = lambda out: getattr(out, "memory_space", None) == pltpu.HBM
    with jax.named_scope(name):
        return pl.pallas_call(
            kernel,
            out_shape=out_shapes,
            in_specs=[hbm] * in_hbm + [vmem] * (len(args) - in_hbm),
            out_specs=jax.tree.map(lambda out: hbm if is_stored(out) else vmem, out_shapes),
            scratch_shapes=scratch,
            compiler_params=pltpu.CompilerParams(vmem_limit_bytes=mib * 1024 * 1024),
            cost_estimate=pl.CostEstimate(flops=1, bytes_accessed=1, transcendentals=0),
        )(*args)


def start_copies(sems, *pairs):
    copies = [pltpu.make_async_copy(src, dst, sems.at[i]) for i, (src, dst) in enumerate(pairs)]
    for copy in copies:
        copy.start()
    return copies


def swap(values, axis, bit=1):
    count = lax.axis_size(axis)
    return lax.ppermute(values, axis, [(i, i ^ bit) for i in range(count)])


def gather_all(values):
    bits = [1 << i for i in range(lax.axis_size("rows").bit_length() - 1)]
    steps = [bits[:1]] + [bits[i : i + 2] for i in range(1, len(bits), 2)]
    for step in steps:
        masks = step + ([step[0] | step[1]] if len(step) > 1 else [])
        values = jnp.concatenate([values] + [swap(values, "rows", mask) for mask in masks], 0)
    return jnp.concatenate([values, swap(values, "tower")], 0)


def row_halves(cur, bit, low, shard):
    columns = cur.shape[-1]
    view = cur.reshape(-1, 2, low * shard, columns)
    own_bit = (lax.axis_index("rows") & bit) // bit
    keep = lax.dynamic_index_in_dim(view, own_bit, 1, False).reshape(-1, columns)
    send = lax.dynamic_index_in_dim(view, 1 - own_bit, 1, False).reshape(-1, columns)
    return keep, send


class RowsScatter:
    def __init__(self, name, shard, own, received, swapped=False):
        self.name, self.shard = name, shard
        self.own, self.received = own, received
        self.bits = [1 << i for i in range(lax.axis_size("rows").bit_length() - 1)]
        self.order = list(self.bits)
        if swapped and len(self.order) > 1:
            self.order[0], self.order[1] = self.order[1], self.order[0]

    def split(self, sends=1):
        self.bit = self.order.pop(0)
        low = 1 << sorted(self.bits).index(self.bit)
        self.bits.remove(self.bit)
        rows, columns = self.own.shape[0] // 2, self.own.shape[1]
        if self.shard % 16 == 0:
            self.own, *self.send = whole(
                self.name,
                functools.partial(split_kernel, self.shard, self.bit, low, sends),
                (struct((rows, columns), bf16),) + (struct((rows, columns // sends), bf16),) * sends,
                self.own,
                *self.received,
            )
        else:
            self.own, send = row_halves(self.total().astype(bf16), self.bit, low, self.shard)
            self.send = jnp.split(send, sends, 1)

    def exchange(self):
        self.received = [swap(v, "rows", self.bit) for v in self.send]

    def step(self, sends=1):
        self.split(sends)
        self.exchange()

    def total(self):
        return self.own.astype(f32) + jnp.concatenate(self.received, 1).astype(f32)

    def finish(self, *columns):
        while self.order:
            self.step()
        outs = tuple(struct((self.own.shape[0], n), f32) for n in columns)
        kernel = functools.partial(finish_kernel, len(self.received))
        return whole(self.name + "_finish", kernel, outs, self.own, *self.received)

    def small_finish(self, bias_shape, *columns):
        while self.order:
            self.step()
        rows = self.own.shape[0]
        outs = tuple(struct((rows, n), f32) for n in columns)
        outs += (struct((rows,), f32),) * 3 + (struct(bias_shape, f32),)
        return whole(self.name + "_finish", small_finish_kernel, outs, self.own, *self.received)

    def gain_finish(self, gain, *columns):
        while self.order:
            self.step()
        outs = tuple(struct((self.own.shape[0], n), f32) for n in columns) + (struct(gain.shape, f32),)
        return whole(
            self.name + "_finish", gain_finish_kernel, outs, self.own, *self.received, gain, swap(gain, "mp")
        )


def finish_two(first, second):
    while first.order or second.order:
        for scatter in (first, second):
            if scatter.order:
                scatter.step()
    outs = tuple(struct(v.own.shape, f32) for v in (first, second))
    return whole("finish", two_finish_kernel, outs, first.own, *first.received, second.own, *second.received)


def tie(*values):
    return list(lax.optimization_barrier(values))


def struct(shape, dtype):
    return jax.ShapeDtypeStruct(shape, dtype)


def per_device(
    tokens,
    segment_ids,
    pair_ids,
    bucket_ids,
    attn_gain,
    query_weight,
    key_weight,
    value_weight,
    output_weight,
    bias_table,
    ff_gain,
    up_weight,
    down_weight,
    final_gain,
    proj_weight,
):
    length = tokens.shape[2]
    width = tokens.shape[3]
    inner = query_weight.shape[1]
    hidden = up_weight.shape[1]
    head_count = bias_table.shape[1]
    bucket_count = bias_table.shape[0]
    total_segs = pair_ids.shape[0]
    span = 2 * length
    size = length // CHUNKS
    chunks = range(CHUNKS)
    tower_index = lax.axis_index("tower")
    device_index = tower_index * lax.axis_size("rows") + lax.axis_index("rows")
    shard = width // (2 * lax.axis_size("rows"))

    token_row = tokens.reshape(length, width)
    segments = segment_ids.reshape(1, length)

    part_rows = inner // 2
    fetched = swap(
        lax.dynamic_slice_in_dim(output_weight, tower_index * part_rows, part_rows, 0), "mp"
    )

    normed_one, query, key, value, probs, mix_stored, tok, *mixes = whole(
        "attention",
        attend_kernel,
        (
            stored((length, width), bf16),
            stored((length, inner), bf16),
            stored((length, inner), bf16),
            stored((length, inner), bf16),
            stored((head_count, length, length), bf16),
            stored((length, inner), bf16),
            fixed((length, width), bf16),
        )
        + (fixed((size, inner), bf16),) * CHUNKS,
        token_row,
        query_weight,
        key_weight,
        value_weight,
        attn_gain,
        bias_table.T,
        bucket_ids,
        segments,
        scratch=[
            pltpu.VMEM((3, width, inner), bf16),
            pltpu.VMEM((width,), f32),
            pltpu.VMEM((head_count, bucket_count), f32),
            pltpu.VMEM((span - 1,), jnp.int32),
            pltpu.VMEM((1, length), jnp.int32),
            pltpu.VMEM((length, width), bf16),
            pltpu.VMEM((length, inner), bf16),
            pltpu.VMEM((length, inner), bf16),
            pltpu.VMEM((length, inner), bf16),
            pltpu.VMEM((head_count, length, length), bf16),
            pltpu.VMEM((length, inner), bf16),
            pltpu.VMEM((8, span), f32),
            pltpu.VMEM((length, length), f32),
            pltpu.VMEM((2, BLOCK, span), f32),
            pltpu.VMEM((2, BLOCK, length), f32),
            pltpu.SemaphoreType.DMA((8,)),
            pltpu.SemaphoreType.DMA((5 + inner // BLOCK,)),
        ],
        in_hbm=8,
        mib=24,
    )
    mix_received = [swap(mix, "mp") for mix in mixes]
    fetched, segments = tie(fetched, tie(segments, mixes[-1])[0])
    fetched_too = swap(fetched, "tower")
    output_whole, up_held, down_held, proj_held = whole(
        "load",
        load_kernel,
        (
            fixed((2 * inner, width), bf16),
            fixed((width, hidden), bf16),
            fixed((hidden, width), bf16),
            fixed((width, width), bf16),
        ),
        output_weight,
        up_weight,
        down_weight,
        proj_weight,
        fetched,
        fetched_too,
        scratch=[pltpu.SemaphoreType.DMA((6,))],
        in_hbm=4,
    )

    hidden_one, normed_two, active, slope, ff_part, ff_received = [], [], [], [], [], []
    for c in chunks:
        outs = whole(
            "feed_forward",
            functools.partial(ff_kernel, c),
            (
                fixed((size, width), f32),
                fixed((size, width), bf16),
                fixed((size, hidden), bf16),
                fixed((size, hidden), f32),
                fixed((size, width), bf16),
            ),
            tok,
            output_whole,
            up_held,
            down_held,
            mixes[c],
            mix_received[c],
            ff_gain,
            scratch=[pltpu.VMEM((size, 2 * inner), bf16)],
            in_vmem=5,
        )
        for kept, out in zip((hidden_one, normed_two, active, slope, ff_part), outs):
            kept.append(out)
        ff_received.append(swap(ff_part[c], "mp"))

    hidden_two, pooled = [], []
    for c in chunks:
        h2, total = whole(
            "pool",
            functools.partial(pool_kernel, c),
            (
                fixed((size, width), f32),
                struct((SEGS_ROW, width), bf16 if c == CHUNKS - 1 else f32),
            ),
            hidden_one[c],
            ff_part[c],
            ff_received[c],
            final_gain,
            segments,
            *pooled,
            in_vmem=2,
        )
        hidden_two.append(h2)
        pooled = [total]
    gathered = gather_all(pooled[0])
    loss, proj_grad, pooled_grad = whole(
        "contrast",
        functools.partial(contrast_kernel, total_segs),
        (
            struct((1, 1), f32),
            struct((shard, width), f32),
            struct((SEGS_ROW, width), f32),
        ),
        proj_held,
        gathered,
        pair_ids,
        in_vmem=1,
    )

    two_part, hidden_two_grad, ff_grad, up_out_grad, final_gain_part = whole(
        "feed_forward_back",
        ff_back_kernel,
        (
            fixed((length, width), bf16),
            fixed((length, width), f32),
            fixed((length, width), bf16),
            fixed((length, hidden), bf16),
            struct((1, width), f32),
        ),
        down_held,
        up_held,
        *hidden_two,
        *slope,
        pooled_grad,
        segments,
        final_gain,
        in_vmem=2 + 2 * CHUNKS,
    )
    two_received = swap(two_part, "mp")

    def half_shapes(sends):
        half = struct((width // 2, hidden), bf16)
        return (struct((width // 2, hidden // sends), bf16),) * sends + (half,)

    *halves, own = whole("down_weight", down_weight_kernel, half_shapes(DOWN_SENDS), ff_grad, *active, in_vmem=1 + CHUNKS)
    down_scatter = RowsScatter("down_split", shard, own, [swap(v, "tower") for v in halves])
    *halves, own = whole("up_weight", up_weight_kernel, half_shapes(UP_SENDS), up_out_grad, *normed_two, in_vmem=1 + CHUNKS)
    up_scatter = RowsScatter("up_split", shard, own, [swap(v, "tower") for v in halves])
    down_scatter.step()
    up_scatter.split()
    two_received, down_send, up_scatter.send = tie(
        two_received, down_scatter.send, up_scatter.send
    )
    up_scatter.exchange()
    hidden_one_grad, attn_grad, mix_grad, ff_gain_part, *heads_held = whole(
        "middle_back",
        middle_back_kernel,
        (
            fixed((length, width), f32),
            stored((length, width), bf16),
            fixed((length, inner), bf16),
            struct((1, width), f32),
        )
        + (fixed((length, inner), bf16),) * 3
        + (fixed((head_count, length, length), bf16),),
        query,
        key,
        value,
        probs,
        output_whole,
        two_part,
        hidden_two_grad,
        *hidden_one,
        two_received,
        ff_gain,
        scratch=[
            pltpu.VMEM((length, width), bf16),
            pltpu.SemaphoreType.DMA((4,)),
            pltpu.SemaphoreType.DMA((1,)),
        ],
        in_hbm=4,
        in_vmem=3 + CHUNKS,
    )

    down_scatter.received, mix_grad = tie(down_scatter.received, mix_grad)
    down_scatter.split()
    mix_grad = tie(mix_grad, down_scatter.send)[0]
    down_scatter.exchange()

    pair_shape = struct((width // 2, 2 * inner), bf16)
    more_shape = struct((width // 2, 2 * inner + LANES), bf16)
    one_part, first_other, first_own, second_other, second_own = whole(
        "attention_back",
        functools.partial(attend_back_kernel, shard),
        (
            fixed((length, width), bf16),
            more_shape,
            more_shape,
            pair_shape,
            pair_shape,
        ),
        query_weight,
        key_weight,
        value_weight,
        normed_one,
        mix_stored,
        attn_grad,
        *heads_held,
        mix_grad,
        tok,
        bucket_ids,
        ff_gain_part,
        final_gain_part,
        scratch=[
            pltpu.VMEM((length, 3 * inner), bf16),
            pltpu.VMEM((length, width), bf16),
            pltpu.VMEM((3, width, inner), bf16),
            pltpu.VMEM((length, inner), bf16),
            pltpu.VMEM((length, width), bf16),
            pltpu.VMEM((width, LANES), f32),
            pltpu.VMEM((bucket_count, head_count), f32),
            pltpu.VMEM((2, length, length), bf16),
            pltpu.VMEM((2, BLOCK, span), f32),
            pltpu.VMEM((8, span), f32),
            pltpu.VMEM((2, BLOCK, length), f32),
            pltpu.SemaphoreType.DMA((6,)),
        ],
        in_hbm=6,
        in_vmem=6,
        mib=24,
    )
    one_received = swap(one_part, "mp")
    first_other, second_other, down_scatter.received, up_scatter.received = tie(
        first_other, second_other, down_scatter.received, up_scatter.received
    )
    first_scatter = RowsScatter("query_key_split", shard, first_own, [swap(first_other, "tower")])
    second_scatter = RowsScatter("value_output_split", shard, second_own, [swap(second_other, "tower")])
    up_scatter.step()
    down_scatter.step()
    first_scatter.received = tie(first_scatter.received, up_scatter.send, down_scatter.send)[0]
    first_scatter.step()
    second_scatter.step()
    first_scatter.received, down_scatter.received = tie(
        first_scatter.received, down_scatter.received
    )
    first_scatter.step()
    first_scatter.send, up_scatter.received = tie(first_scatter.send, up_scatter.received)
    up_scatter.step()
    first_scatter.received, second_scatter.received, down_scatter.received = tie(
        first_scatter.received, second_scatter.received, down_scatter.received
    )
    second_scatter.step()
    first_scatter.step()
    down_sum, up_sum = finish_two(down_scatter, up_scatter)
    tokens_grad = whole(
        "last",
        last_kernel,
        stored((length, width), f32),
        tok,
        one_part,
        hidden_one_grad,
        attn_gain,
        one_received,
        scratch=[pltpu.VMEM((length, width), f32), pltpu.SemaphoreType.DMA((length // BLOCK,))],
        in_vmem=3,
    )
    second_scatter.received, tokens_grad, down_sum, up_sum = tie(
        second_scatter.received, tokens_grad, down_sum, up_sum
    )
    second_scatter.step()
    bias_pieces = -(-bucket_count // shard)
    query_sum, key_sum, attn_gain_sum, ff_gain_sum, final_gain_sum, turned = first_scatter.small_finish(
        (head_count * bias_pieces, min(shard, bucket_count)), inner, inner
    )
    value_sum, output_sum, attn_gain_sum = second_scatter.gain_finish(attn_gain_sum, inner, inner)
    bias_rows = [turned[g * head_count : (g + 1) * head_count, :] for g in range(bias_pieces)]
    bias_total = jnp.concatenate(bias_rows, 1)[:, :bucket_count].T
    return (
        loss[0, 0],
        tokens_grad.reshape(tokens.shape),
        attn_gain_sum,
        query_sum,
        key_sum,
        value_sum,
        output_sum.T,
        bias_total,
        ff_gain_sum,
        up_sum,
        down_sum.T,
        final_gain_sum,
        proj_grad,
    )


def solution(mesh):
    in_specs = (
        P("tower", "rows", None, None),
        P("tower", "rows", None),
        P(),
        P(),
        P(),
        P(None, "mp"),
        P(None, "mp"),
        P(None, "mp"),
        P("mp", None),
        P(None, "mp"),
        P(),
        P(None, "mp"),
        P("mp", None),
        P(),
        P(),
    )
    out_specs = (
        P(),
        P("tower", "rows", None, None),
        P(("tower", "rows")),
        P(("tower", "rows"), "mp"),
        P(("tower", "rows"), "mp"),
        P(("tower", "rows"), "mp"),
        P("mp", ("tower", "rows")),
        P(None, "mp"),
        P(("tower", "rows")),
        P(("tower", "rows"), "mp"),
        P("mp", ("tower", "rows")),
        P(("tower", "rows")),
        P(("tower", "rows"), None),
    )
    return jax.shard_map(
        per_device, mesh=mesh, in_specs=in_specs, out_specs=out_specs, check_vma=False
    )
```
